32 devices in a mesh: row: 8 (over y, x, core), col: 4 (over z).
Axes of the slice: x: 2, y: 2, z: 4, core: 2. Of those that a mesh axis runs over, the one named last changes fastest.
Arguments:
- hidden_img: bfloat16 [4096, 2432], P('row', 'col'), may hold values from -75 to 75
- hidden_txt: bfloat16 [768, 2432], P('row', 'col'), may hold values from -75 to 75
- text_len: int32 [4], replicated, may hold values from 1 to 154, as said below
- step_index: int32 [4], replicated, may hold values from 0 to 27
- latent: float32 [4096, 64], P('row'), may hold values from -6 to 6
- cond: float32 [4, 2432], P(None, 'row'), may hold values from -6 to 6
- mod_weight: bfloat16 [2432, 7, 2432], P('row', None, 'col'), may hold values from -0.125 to 0.125
- qkv_weight: bfloat16 [2432, 3, 2048], P('row', None, 'col'), may hold values from -0.125 to 0.125
- kv_text_weight: bfloat16 [2432, 2, 2048], P('row', None, 'col'), may hold values from -0.125 to 0.125
- q_gain: float32 [64], replicated, may hold values from 0.5 to 6
- k_gain: float32 [2, 64], replicated, may hold values from 0.5 to 6
- out_weight: bfloat16 [2048, 2432], P('row', 'col'), may hold values from -6 to 6
- final_weight: bfloat16 [2432, 64], P('row'), may hold values from -0.125 to 0.125
Outputs:
- velocity: float32 [4096, 64], P('row')
- latent_next: float32 [4096, 64], P('row')
The draws below stay inside these ranges and needn't reach their ends.
Inputs may be any that keep to these rules, and one draw needn't show every extreme that they name: `text_len`: some request has exactly 154 text tokens in every draw.
All inputs are finite; a program needn't handle non-finite values.
Results may differ from the reference program's by a relative error of at most 0.015.
The reference program's roundings to bfloat16 on the way count: a program that leaves them out, or rounds other values in their place, can miss the bound.
Values may be sent and summed in bfloat16 or wider, within the bound.
No kernel may reach another device: no remote copies, remote signals or barrier semaphores. Data moves between devices by JAX's collectives and lax.ppermute only.
A program may use at most 64 MiB of HBM per device.

```python
import jax
import jax.numpy as jnp
from jax import lax

D = 2432
HEAD_DIM = 64
HEADS = 32
PATCH_OUT = 64
TXT_MAX = 154
STEPS = 28
REQ = 4
IMG = 1024
TXT = 192
QKW = 2048


def scaled_rows(key, row_total, col_total):
    key_noise, key_cols, key_rows = jax.random.split(key, 3)
    ramp = 3.0 ** (jnp.arange(col_total, dtype=jnp.float32) / (col_total - 1) - 0.5)
    col_scale = ramp * jnp.exp(jax.random.uniform(key_cols, (col_total,), jnp.float32, jnp.log(0.5), jnp.log(2.0)))
    row_scale = jnp.exp(jax.random.uniform(key_rows, (row_total, 1), jnp.float32, jnp.log(0.5), jnp.log(5.0)))
    noise = jax.random.truncated_normal(key_noise, -4.0, 4.0, (row_total, col_total), jnp.float32)
    return (noise * col_scale * row_scale).astype(jnp.bfloat16)


def draw_hidden_img(key, part):
    return scaled_rows(jax.random.fold_in(key, 11), REQ * IMG, D)


def draw_hidden_txt(key, part):
    return scaled_rows(jax.random.fold_in(key, 12), REQ * TXT, D)


def draw_text_len(key, part):
    key_lens, key_pick = jax.random.split(jax.random.fold_in(key, 13))
    lengths = jax.random.randint(key_lens, (REQ,), 1, TXT_MAX + 1, dtype=jnp.int32)
    picked = jax.random.randint(key_pick, (), 0, REQ, dtype=jnp.int32)
    return lengths.at[picked].set(TXT_MAX)


def gain_values(key, shape, low, high):
    return jnp.exp(jax.random.uniform(key, shape, jnp.float32, jnp.log(low), jnp.log(high)))


def draw_q_gain(key, part):
    return gain_values(jax.random.fold_in(key, 14), (HEAD_DIM,), 0.5, 2.0)


def draw_k_gain(key, part):
    image_gain = gain_values(jax.random.fold_in(key, 15), (1, HEAD_DIM), 0.5, 2.0)
    text_gain = gain_values(jax.random.fold_in(key, 16), (1, HEAD_DIM), 1.5, 3.0)
    return jnp.concatenate([image_gain, text_gain], axis=0)


def plant(result, rng, low, high):
    place = [jax.random.randint(jax.random.fold_in(rng, axis), (), 0, length) for axis, length in enumerate(result.shape)]
    widest = result.shape.index(max(result.shape))
    neighbour = place[:widest] + [(place[widest] + 1) % result.shape[widest]] + place[widest + 1:]
    return result.at[tuple(place)].set(low).at[tuple(neighbour)].set(high)


def level_of(stream_key, shape, cuts, least, top_value):
    def one(axis_at, shards_of):
        steps = jax.random.uniform(jax.random.fold_in(jax.random.fold_in(stream_key, 6), axis_at), (shards_of,), jnp.float32, least / len(cuts), top_value / len(cuts))
        return jnp.repeat(jnp.exp(steps), shape[axis_at] // shards_of).reshape((-1,) + (1,) * (len(shape) - axis_at - 1))

    gain = one(*cuts[0])
    for cut in cuts[1:]:
        gain = gain * one(*cut)
    return gain


def normal_values(stream_key, dims, width, reach, cuts=(), kind=jnp.bfloat16):
    level = level_of(stream_key, dims, cuts, -0.22, 0.18) if cuts else 1.0
    entries = jax.random.normal(stream_key, dims, jnp.float32) * width * level
    return jnp.minimum(jnp.maximum(entries, -reach), reach).astype(kind)


def setup_inputs(seed: int = 0) -> dict:
    key_list = jax.random.split(jax.random.key(seed), 14)
    hidden_img = draw_hidden_img(jax.random.fold_in(key_list[13], 71), 0)
    hidden_txt = draw_hidden_txt(jax.random.fold_in(key_list[13], 71), 0)
    text_len = draw_text_len(jax.random.fold_in(key_list[13], 71), 0)
    step_index = plant(jax.random.randint(key_list[3], (REQ,), 0, STEPS), jax.random.fold_in(key_list[3], 1), 0, STEPS - 1).astype(jnp.int32)
    latent = normal_values(key_list[4], (REQ * IMG, PATCH_OUT), 1.0, 6.0, ((0, 8),), jnp.float32)
    cond = normal_values(key_list[5], (REQ, D), 1.0, 6.0, ((1, 8),), jnp.float32)
    mod_weight = normal_values(key_list[6], (D, 7, D), D ** -0.5, 0.125, ((0, 8), (2, 4)))
    qkv_weight = normal_values(key_list[7], (D, 3, QKW), D ** -0.5, 0.125, ((0, 8), (2, 4)))
    kv_text_weight = normal_values(key_list[8], (D, 2, QKW), D ** -0.5, 0.125, ((0, 8), (2, 4)))
    q_gain = draw_q_gain(jax.random.fold_in(key_list[13], 71), 0)
    k_gain = draw_k_gain(jax.random.fold_in(key_list[13], 71), 0)
    out_weight = normal_values(key_list[11], (QKW, D), (max(HEAD_DIM // 64, 1)) ** -0.5, 6.0, ((0, 8), (1, 4)))
    final_weight = normal_values(key_list[12], (D, PATCH_OUT), D ** -0.5, 0.125, ((0, 8),))
    return {"hidden_img": hidden_img, "hidden_txt": hidden_txt, "text_len": text_len, "step_index": step_index, "latent": latent, "cond": cond, "mod_weight": mod_weight, "qkv_weight": qkv_weight, "kv_text_weight": kv_text_weight, "q_gain": q_gain, "k_gain": k_gain, "out_weight": out_weight, "final_weight": final_weight}


EPS_NORM = 1e-06

def modulate_full(values, offset, stretch):
    average = lax.optimization_barrier(jnp.mean(values, axis=1, keepdims=True))
    mean_square = lax.optimization_barrier(jnp.mean(values * values, axis=1, keepdims=True))
    normed = (values - average) * lax.rsqrt(mean_square - average * average + EPS_NORM)
    return (normed * (1.0 + stretch) + offset).astype(jnp.bfloat16)

def head_norm(values, gain_row):
    mean_square = lax.optimization_barrier(jnp.mean(values * values, axis=-1, keepdims=True))
    return (values * lax.rsqrt(mean_square + EPS_NORM) * gain_row).astype(jnp.bfloat16)

def sigma_of(step_now):
    remain = 1.0 - step_now.astype(jnp.float32) / STEPS
    return 3.0 * remain / (1.0 + 2.0 * remain)

def reference(hidden_img, hidden_txt, text_len, step_index, latent, cond, mod_weight, qkv_weight, kv_text_weight, q_gain, k_gain, out_weight, final_weight):
    activated = jax.nn.silu(cond).astype(jnp.bfloat16)
    modulation = jnp.dot(activated, mod_weight.reshape(D, 7 * D), preferred_element_type=jnp.float32).reshape(REQ, 7, D)
    qkv_flat = qkv_weight.reshape(D, 3 * QKW)
    kv_flat = kv_text_weight.reshape(D, 2 * QKW)
    scaling = HEAD_DIM ** (-0.5)

    def one_request(operands):
        img_part, txt_part, length, mod_row, latent_part, step_now = operands
        img_ready = modulate_full(img_part.astype(jnp.float32), mod_row[0], mod_row[1])
        txt_ready = modulate_full(txt_part.astype(jnp.float32), mod_row[3], mod_row[4])
        img_proj = jnp.dot(img_ready, qkv_flat, preferred_element_type=jnp.float32).reshape(IMG, 3, HEADS, HEAD_DIM)
        txt_proj = jnp.dot(txt_ready, kv_flat, preferred_element_type=jnp.float32).reshape(TXT, 2, HEADS, HEAD_DIM)
        queries = head_norm(img_proj[:, 0], q_gain)
        all_keys = jnp.concatenate([head_norm(img_proj[:, 1], k_gain[0]), head_norm(txt_proj[:, 0], k_gain[1])], axis=0)
        all_values = jnp.concatenate([img_proj[:, 2].astype(jnp.bfloat16), txt_proj[:, 1].astype(jnp.bfloat16)], axis=0)
        key_valid = jnp.concatenate([jnp.ones((IMG,), dtype=bool), jnp.arange(TXT) < length])

        def attend(head_ops):
            q_head, k_head, v_head = head_ops
            scores = jnp.dot(q_head, k_head.T, preferred_element_type=jnp.float32) * scaling
            scores = jnp.where(key_valid[None, :], scores, -jnp.inf)
            row_max = lax.optimization_barrier(jnp.max(scores, axis=1, keepdims=True))
            weights = jnp.exp(scores - row_max)
            probabilities = (weights / lax.optimization_barrier(jnp.sum(weights, axis=1, keepdims=True))).astype(jnp.bfloat16)
            return jnp.dot(probabilities, v_head, preferred_element_type=jnp.float32).astype(jnp.bfloat16)
        attended = lax.map(attend, (jnp.moveaxis(queries, 1, 0), jnp.moveaxis(all_keys, 1, 0), jnp.moveaxis(all_values, 1, 0)))
        attended = jnp.moveaxis(attended, 0, 1).reshape(IMG, QKW)
        projected = jnp.dot(attended, out_weight, preferred_element_type=jnp.float32)
        updated = (img_part.astype(jnp.float32) + mod_row[2] * projected).astype(jnp.bfloat16)
        head_in = modulate_full(updated.astype(jnp.float32), mod_row[5], mod_row[6])
        velocity = jnp.dot(head_in, final_weight, preferred_element_type=jnp.float32)
        sigma_step = sigma_of(step_now + 1) - sigma_of(step_now)
        return (velocity, latent_part + sigma_step * velocity)
    velocity, latent_next = lax.map(one_request, (hidden_img.reshape(REQ, IMG, D), hidden_txt.reshape(REQ, TXT, D), text_len, modulation, latent.reshape(REQ, IMG, PATCH_OUT), step_index))
    return (velocity.reshape(REQ * IMG, PATCH_OUT), latent_next.reshape(REQ * IMG, PATCH_OUT))
```

```python
import functools

import jax
import jax.numpy as jnp
from jax import lax
from jax.experimental import pallas as pl
from jax.experimental.pallas import tpu as pltpu
from jax.sharding import PartitionSpec as P

STEPS = 28
EPS_NORM = 1e-06
F32 = jnp.float32
BF16 = jnp.bfloat16
VMEM_LIMIT = 48 * 1024 * 1024
ANY = pl.BlockSpec(memory_space=pl.ANY)
VMEM = pl.BlockSpec(memory_space=pltpu.VMEM)
SMEM = pl.BlockSpec(memory_space=pltpu.SMEM)


def swap(block, axis, mask):
    count = lax.axis_size(axis)
    return lax.ppermute(block, axis, [(i, i ^ mask) for i in range(count)])


def shift(block, axis, step):
    count = lax.axis_size(axis)
    route = [(i, i + step) for i in range(count) if 0 <= i + step < count]
    return lax.ppermute(block, axis, route)


def line_gather(block, axis):
    held = {0: block}
    for step in range(1, lax.axis_size(axis)):
        held[-step] = shift(held[1 - step], axis, 1)
        held[step] = shift(held[step - 1], axis, -1)
    return held


def doubling_gather(block, axis, masks):
    held = {0: block}
    for mask in masks:
        for known in list(held):
            held[known | mask] = swap(held[known], axis, mask)
    return held


def in_line(held, axis):
    offsets, count = sorted(held), lax.axis_size(axis)
    rows = held[0].shape[0]
    if rows % 16 == 0:
        return [held[k] for k in offsets], offsets, count
    joined = jnp.concatenate([held[k] for k in offsets], axis=0)
    first = (count - 1 - lax.axis_index(axis)) * rows
    return [lax.dynamic_slice_in_dim(joined, first, count * rows, 0)], [None], 1


def in_order(held, axis):
    masks, count = sorted(held), lax.axis_size(axis)
    rows = held[0].shape[0]
    if rows % 16 == 0:
        return [held[k] for k in masks], masks
    joined = jnp.stack([held[k] for k in masks])
    order = jnp.bitwise_xor(jnp.arange(count), lax.axis_index(axis))
    return [joined[order].reshape((count * rows,) + joined.shape[2:])], [None]


def cost(flops, touched, exps=0):
    return pl.CostEstimate(flops=flops, bytes_accessed=touched, transcendentals=exps)


def call(kernel, outs, in_specs, scratch, estimate, out_specs=None):
    if out_specs is None:
        out_specs = jax.tree.map(lambda _: VMEM, outs)
    return pl.pallas_call(
        kernel,
        out_shape=outs,
        in_specs=in_specs,
        out_specs=out_specs,
        scratch_shapes=scratch,
        cost_estimate=estimate,
        compiler_params=pltpu.CompilerParams(vmem_limit_bytes=VMEM_LIMIT),
    )


def line_copies(refs, offsets, place, count, target, sems, act):
    for n, (ref, offset) in enumerate(zip(refs, offsets)):
        owner = 0 if offset is None else place + offset

        @pl.when((owner >= 0) & (owner < count))
        def _():
            copy = pltpu.make_async_copy(ref, target(owner), sems.at[n])
            getattr(copy, act)()


def mod_kernel(cond_ref, w_ref, out_ref):
    values = cond_ref[...]
    activated = (values * (1.0 / (1.0 + jnp.exp(-values)))).astype(BF16)
    for group in range(w_ref.shape[0]):
        out_ref[:, group, :] = jnp.dot(activated, w_ref[group], preferred_element_type=F32)


def norm_kernel(offsets, count, img, place_ref, mod_ref, *refs):
    blocks = refs[: len(offsets)]
    out_ref, x_ref, sems = refs[len(offsets) :]
    width, tokens = blocks[0].shape
    place = place_ref[1]
    target = lambda owner: x_ref.at[pl.ds(pl.multiple_of(owner * width, 16), width)]
    line_copies(blocks, offsets, place, count, target, sems, "start")
    line_copies(blocks, offsets, place, count, target, sems, "wait")
    rows = 16
    total = width * count

    def gather_stats(i, carry):
        part = x_ref[pl.ds(pl.multiple_of(i * rows, rows), rows)].astype(F32)
        sums, squares = carry
        for r in range(0, rows, 8):
            piece = part[r : r + 8]
            sums += piece
            squares += piece * piece
        return sums, squares

    zero = jnp.zeros((8, tokens), F32)
    sums, squares = lax.fori_loop(0, total // rows, gather_stats, (zero, zero), unroll=4)
    average = jnp.sum(sums, axis=0, keepdims=True) / total
    mean_square = jnp.sum(squares, axis=0, keepdims=True) / total
    inverse = lax.rsqrt(mean_square - average * average + EPS_NORM)
    shape = (rows, tokens)
    average = jnp.broadcast_to(average, shape)
    inverse = jnp.broadcast_to(inverse, shape)

    for owner in range(count):
        slot = 0 if count == 1 else jnp.bitwise_xor(owner, place)

        def normalise(i, _):
            at = pl.multiple_of(i * rows, rows)
            mod = mod_ref[slot, pl.ds(at, rows), :]
            here = pl.ds(pl.multiple_of(owner * width + i * rows, rows), rows)
            normed = (x_ref[here].astype(F32) - average) * inverse
            out_ref[here, :img] = (normed[:, :img] * mod[:, 1:2] + mod[:, 0:1]).astype(BF16)
            out_ref[here, img:] = (normed[:, img:] * mod[:, 4:5] + mod[:, 3:4]).astype(BF16)
            return 0

        lax.fori_loop(0, width // rows, normalise, 0, unroll=2)


def project_kernel(masks, img, head, place_ref, q_gain_ref, k_gain_ref, x_ref, *refs):
    blocks = refs[: len(masks)]
    q_ref, kv_ref, w_ref, sems = refs[len(masks) :]
    depth = blocks[0].shape[0]
    half = q_ref.shape[0]
    place = place_ref[0]
    copies = []
    for n, (ref, mask) in enumerate(zip(blocks, masks)):
        owner = 0 if mask is None else jnp.bitwise_xor(place, mask)
        copies.append(
            pltpu.make_async_copy(
                ref, w_ref.at[pl.ds(pl.multiple_of(owner * depth, 16), depth)], sems.at[n]
            )
        )
    for copy in copies:
        copy.start()
    for copy in copies:
        copy.wait()

    def product(part, low, high):
        return lax.dot_general(
            w_ref[:, part * half : (part + 1) * half],
            x_ref[:, low:high],
            (((0,), (0,)), ((), ())),
            preferred_element_type=F32,
        )

    def head_norm(values, gain):
        cols = values.shape[1]
        split = values.reshape(half // head, head, cols)
        mean_square = jnp.mean(split * split, axis=1, keepdims=True)
        normed = split * lax.rsqrt(mean_square + EPS_NORM) * gain[None]
        return normed.reshape(half, cols)

    tokens = x_ref.shape[1]
    scaling = head ** (-0.5)
    queries = head_norm(product(0, 0, img), q_gain_ref[...]).astype(BF16)
    q_ref[...] = (queries.astype(F32) * scaling).astype(BF16)
    kv_ref[:half, :img] = head_norm(product(1, 0, img), k_gain_ref[:, 0:1]).astype(BF16)
    kv_ref[half:, :img] = product(2, 0, img).astype(BF16)
    kv_ref[:half, img:] = head_norm(product(3, img, tokens), k_gain_ref[:, 1:2]).astype(BF16)
    kv_ref[half:, img:] = product(4, img, tokens).astype(BF16)


def attend_kernel(img, head, place_ref, q_ref, own_ref, peer_ref, out_ref, k_ref, v_ref):
    half, queries = q_ref.shape
    txt = own_ref.shape[1] - img
    room = (txt + 127) // 128 * 128
    side = lax.rem(place_ref[0], 2)
    length = place_ref[2]
    keys = 2 * img + 2 * room
    k_ref[:, 2 * img :] = jnp.zeros((half, 2 * room), BF16)
    v_ref[:, 2 * img :] = jnp.zeros((half, 2 * room), BF16)
    for n, ref in enumerate((own_ref, peer_ref)):
        at, tail = n * img, 2 * img + n * room
        k_ref[:, at : at + img] = ref[:half, :img]
        v_ref[:, at : at + img] = ref[half:, :img]
        k_ref[:, tail : tail + txt] = ref[:half, img:]
        v_ref[:, tail : tail + txt] = ref[half:, img:]
    slot = lax.broadcasted_iota(jnp.int32, (2 * room, 1), 0)
    second = (slot >= room).astype(jnp.int32)
    inside = slot - second * room
    owner = jnp.where(second == 1, 1 - side, side)
    allowed = (inside < txt) & (owner * txt + inside < length)
    step = 256 if queries % 256 == 0 else queries

    def one(i, _):
        at = pl.multiple_of(i * head, head)
        for low in range(0, queries, step):
            scores = lax.dot_general(
                k_ref[pl.ds(at, head)],
                q_ref[pl.ds(at, head), low : low + step],
                (((0,), (0,)), ((), ())),
                preferred_element_type=F32,
            )
            tail = jnp.where(allowed, scores[2 * img :], -1e30)
            scores = jnp.concatenate([scores[: 2 * img], tail], axis=0)
            weights = jnp.exp(scores - jnp.max(scores, axis=0, keepdims=True))
            inverse = 1.0 / jnp.sum(weights, axis=0, keepdims=True)
            mixed = jnp.dot(
                v_ref[pl.ds(at, head)], weights.astype(BF16), preferred_element_type=F32
            )
            out_ref[pl.ds(at, head), low : low + step] = (mixed * inverse).astype(BF16)
        return 0

    lax.fori_loop(0, half // head, one, 0)


def output_kernel(
    offsets, count, masks, place_ref, gate_ref, out_mod_ref, x_ref, *refs
):
    n_lines = len(offsets)
    firsts, refs = refs[:n_lines], refs[n_lines:]
    seconds, refs = refs[:n_lines], refs[n_lines:]
    weights, refs = refs[: len(masks)], refs[len(masks) :]
    out_ref, a_ref, w_ref, sems_a, sems_b, sems_w = refs
    width, tokens = x_ref.shape
    half = firsts[0].shape[0]
    place = place_ref[0]
    col = place_ref[1]
    copies = []
    for n, (ref, mask) in enumerate(zip(weights, masks)):
        owner = jnp.bitwise_xor(place, mask)
        copies.append(pltpu.make_async_copy(ref, w_ref.at[owner], sems_w.at[n]))
    for copy in copies:
        copy.start()
    lines = ((firsts, 0, sems_a), (seconds, 1, sems_b))
    for act in ("start", "wait"):
        for blocks, n, sems in lines:
            target = lambda owner, n=n: a_ref.at[
                pl.ds(pl.multiple_of((2 * owner + n) * half, half), half)
            ]
            line_copies(blocks, offsets, col, count, target, sems, act)
    for copy in copies:
        copy.wait()
    depth = w_ref.shape[2]
    blocks = w_ref.shape[0]

    projected = jnp.zeros((width, tokens), F32)
    for n in range(blocks):
        projected += jnp.dot(
            w_ref[n, :width], a_ref[n * depth : (n + 1) * depth], preferred_element_type=F32
        )
    updated = (x_ref[...].astype(F32) + gate_ref[...] * projected).astype(BF16)
    wide = updated.astype(F32)
    sums = jnp.sum(wide, axis=0, keepdims=True)
    squares = jnp.sum(wide * wide, axis=0, keepdims=True)

    per_col = blocks // count
    slab = width // per_col
    patch = out_ref.shape[0] - 8
    result = jnp.zeros((patch, tokens), F32)
    gains = jnp.zeros((patch, 1), F32)
    shifts = jnp.zeros((patch, 1), F32)
    for n in range(per_col):
        owner = col * per_col + n
        pieces = [
            w_ref[owner, width + k * patch : width + (k + 1) * patch]
            for k in range((w_ref.shape[1] - width) // patch)
        ]
        for k, piece in enumerate(pieces):
            low, high = k * depth, min((k + 1) * depth, slab)
            if low >= high:
                continue
            linear = piece[:, : high - low].astype(F32)
            gained = linear * (1.0 + out_mod_ref[n, 1:2, low:high])
            shifts += jnp.sum(linear * out_mod_ref[n, 0:1, low:high], axis=1, keepdims=True)
            gains += jnp.sum(gained, axis=1, keepdims=True)
            part = updated[n * slab + low : n * slab + high]
            for _ in range(3):
                term = gained.astype(BF16)
                result += jnp.dot(term, part, preferred_element_type=F32)
                gained = gained - term.astype(F32)
    out_ref[:patch, :tokens] = result
    row = lax.broadcasted_iota(jnp.int32, (8, tokens), 0)
    out_ref[patch:, :tokens] = jnp.where(row == 0, sums, jnp.where(row == 1, squares, 0.0))
    lane = lax.broadcasted_iota(jnp.int32, (patch, 128), 1)
    out_ref[:patch, tokens:] = jnp.where(lane == 0, gains, jnp.where(lane == 1, shifts, 0.0))
    out_ref[patch:, tokens:] = jnp.zeros((8, 128), F32)


def sigma_of(step_now):
    remain = 1.0 - step_now.astype(F32) / STEPS
    return 3.0 * remain / (1.0 + 2.0 * remain)


def per_device(
    hidden_img,
    hidden_txt,
    text_len,
    step_index,
    latent,
    cond,
    mod_weight,
    qkv_weight,
    kv_text_weight,
    q_gain,
    k_gain,
    out_weight,
    final_weight,
):
    row_count, col_count = lax.axis_size("row"), lax.axis_size("col")
    row_pos, col_pos = lax.axis_index("row"), lax.axis_index("col")
    request = row_pos // 2
    requests = cond.shape[0]
    img, width = hidden_img.shape
    txt = hidden_txt.shape[0]
    tokens = img + txt
    head = q_gain.shape[0]
    part_cols = qkv_weight.shape[2]
    half = part_cols // 2
    full_width = width * col_count
    length = lax.dynamic_index_in_dim(text_len, request, 0, keepdims=False)
    place = jnp.stack([row_pos, col_pos, length]).astype(jnp.int32)

    chip_masks = [1 << bit for bit in range(1, row_count.bit_length() - 1)]
    gathered = []
    packed = []
    for n in range(2):
        cols = slice(n * half, (n + 1) * half)
        packed.append(
            jnp.concatenate(
                [qkv_weight[:, k, cols] for k in range(3)]
                + [kv_text_weight[:, k, cols] for k in range(2)],
                axis=1,
            )
        )
    x_own = jnp.concatenate([hidden_img.T, hidden_txt.T], axis=1)
    x_blocks = line_gather(x_own, "col")
    for n in range(2):
        order = chip_masks[::-1] if n == 0 else chip_masks
        gathered.append(doubling_gather(packed[n], "row", order + [1]))

    mod_part = call(
        mod_kernel,
        jax.ShapeDtypeStruct((requests, 7, width), F32),
        [VMEM, VMEM],
        [],
        cost(2 * requests * cond.shape[1] * 7 * width, mod_weight.size * 2),
    )(cond, jnp.moveaxis(mod_weight, 1, 0))
    mask = row_count // 2
    while mask > 1:
        bit = (row_pos // mask) % 2
        pair = mod_part.reshape((2, mod_part.shape[0] // 2) + mod_part.shape[1:])
        keep = lax.dynamic_index_in_dim(pair, bit, 0, keepdims=False)
        give = lax.dynamic_index_in_dim(pair, 1 - bit, 0, keepdims=False)
        mod_part = keep + swap(give, "row", mask)
        mask //= 2
    mod_part = mod_part[0]
    mod_own = mod_part + swap(mod_part, "row", 1)
    norm_mod = mod_own[:5] + jnp.array([0.0, 1.0, 0.0, 0.0, 1.0], F32)[:, None]
    norm_mod = norm_mod[None]
    mask = 1
    while mask < col_count:
        norm_mod = jnp.concatenate([norm_mod, swap(norm_mod, "col", mask)], axis=0)
        mask *= 2
    norm_mod = jnp.swapaxes(norm_mod, 1, 2)

    x_blocks, offsets, count = in_line(x_blocks, "col")
    if count == 1:
        norm_mod = norm_mod[jnp.bitwise_xor(jnp.arange(col_count), col_pos)]
        norm_mod = norm_mod.reshape(1, full_width, 5)
    ready = call(
        functools.partial(norm_kernel, offsets, count, img),
        jax.ShapeDtypeStruct((full_width, tokens), BF16),
        [SMEM, VMEM] + [ANY] * len(offsets),
        [pltpu.VMEM((full_width, tokens), BF16), pltpu.SemaphoreType.DMA((len(offsets),))],
        cost(12 * full_width * tokens, 4 * full_width * tokens),
    )(place, norm_mod, *x_blocks)

    attended = []
    for n in range(2):
        blocks, masks = in_order(gathered[n], "row")
        queries, pair = call(
            functools.partial(project_kernel, masks, img, head),
            (
                jax.ShapeDtypeStruct((half, img), BF16),
                jax.ShapeDtypeStruct((2 * half, tokens), BF16),
            ),
            [SMEM, VMEM, VMEM, VMEM] + [ANY] * len(masks),
            [pltpu.VMEM((full_width, 5 * half), BF16), pltpu.SemaphoreType.DMA((len(masks),))],
            cost(2 * full_width * half * (3 * img + 2 * txt), 10 * full_width * half),
            (VMEM, VMEM),
        )(place, q_gain[:, None], k_gain.T, ready, *blocks)
        peer = swap(pair, "row", 1)
        keys = 2 * img + 2 * ((txt + 127) // 128 * 128)
        attended.append(
            call(
                functools.partial(attend_kernel, img, head),
                jax.ShapeDtypeStruct((half, img), BF16),
                [SMEM, VMEM, VMEM, VMEM],
                [pltpu.VMEM((half, keys), BF16)] * 2,
                cost(4 * half * keys * img, 8 * half * keys, keys * img * half // head),
            )(place, queries, pair, peer)
        )

    head_depth, patch = final_weight.shape
    depth = out_weight.shape[0]
    folds = -(-head_depth // depth)
    tail = jnp.pad(final_weight.T, ((0, 0), (0, folds * depth - head_depth)))
    tail = jnp.swapaxes(tail.reshape(patch, folds, depth), 0, 1).reshape(folds * patch, depth)
    out_packed = jnp.concatenate([out_weight.T, tail], axis=0)
    out_blocks = doubling_gather(out_packed, "row", [1] + chip_masks)
    masks = sorted(out_blocks)
    offsets = list(range(1 - col_count, col_count))
    lines = [line_gather(block, "col") for block in attended]
    per_col = row_count // col_count
    out_mod = mod_own[5:7].reshape(2, per_col, width // per_col).swapaxes(0, 1)
    partial_sum = call(
        functools.partial(output_kernel, offsets, col_count, masks),
        jax.ShapeDtypeStruct((patch + 8, img + 128), F32),
        [SMEM, VMEM, VMEM, VMEM] + [ANY] * (2 * len(offsets) + len(masks)),
        [
            pltpu.VMEM((part_cols * col_count, img), BF16),
            pltpu.VMEM((row_count,) + out_packed.shape, BF16),
            pltpu.SemaphoreType.DMA((len(offsets),)),
            pltpu.SemaphoreType.DMA((len(offsets),)),
            pltpu.SemaphoreType.DMA((len(masks),)),
        ],
        cost(2 * part_cols * col_count * width * img, 8 * part_cols * col_count * width),
    )(
        place,
        mod_own[2][:, None],
        out_mod,
        hidden_img.T,
        *[line[k] for line in lines for k in offsets],
        *[out_blocks[k] for k in masks],
    )
    mask = 1
    while mask < col_count:
        partial_sum = partial_sum + swap(partial_sum, "col", mask)
        mask *= 2
    average = partial_sum[patch : patch + 1, :img] / full_width
    mean_square = partial_sum[patch + 1 : patch + 2, :img] / full_width
    inverse = lax.rsqrt(mean_square - average * average + EPS_NORM)
    gains = partial_sum[:patch, img : img + 1]
    shifts = partial_sum[:patch, img + 1 : img + 2]
    velocity = inverse * (partial_sum[:patch, :img] - average * gains) + shifts
    step_now = lax.dynamic_index_in_dim(step_index, request, 0, keepdims=False)
    sigma_step = sigma_of(step_now + 1) - sigma_of(step_now)
    latent_next = latent.T + sigma_step * velocity
    return (velocity.T, latent_next.T)


def solution(mesh):
    in_specs = (
        P("row", "col"),
        P("row", "col"),
        P(),
        P(),
        P("row", None),
        P(None, "row"),
        P("row", None, "col"),
        P("row", None, "col"),
        P("row", None, "col"),
        P(),
        P(),
        P("row", "col"),
        P("row", None),
    )
    out_specs = (P("row", None), P("row", None))
    return jax.shard_map(
        per_device, mesh=mesh, in_specs=in_specs, out_specs=out_specs, check_vma=False
    )
```

```python
import functools

import jax
import jax.numpy as jnp
from jax import lax
from jax.experimental import pallas as pl
from jax.experimental.pallas import tpu as pltpu
from jax.sharding import PartitionSpec as P

STEPS = 28
EPS_NORM = 1e-06
F32 = jnp.float32
BF16 = jnp.bfloat16
VMEM_LIMIT = 24 * 1024 * 1024
ANY = pl.BlockSpec(memory_space=pl.ANY)
VMEM = pl.BlockSpec(memory_space=pltpu.VMEM)
SMEM = pl.BlockSpec(memory_space=pltpu.SMEM)


def swap(block, axis, mask):
    count = lax.axis_size(axis)
    return lax.ppermute(block, axis, [(i, i ^ mask) for i in range(count)])


def shift(block, axis, step):
    count = lax.axis_size(axis)
    route = [(i, i + step) for i in range(count) if 0 <= i + step < count]
    return lax.ppermute(block, axis, route)


def line_gather(block, axis):
    held = {0: block}
    for step in range(1, lax.axis_size(axis)):
        held[-step] = shift(held[1 - step], axis, 1)
        held[step] = shift(held[step - 1], axis, -1)
    return held


def doubling_gather(block, axis, masks):
    held = {0: block}
    for mask in masks:
        for known in list(held):
            held[known | mask] = swap(held[known], axis, mask)
    return held


def in_line(held, axis):
    offsets, count = sorted(held), lax.axis_size(axis)
    rows = held[0].shape[0]
    if rows % 16 == 0:
        return [held[k] for k in offsets], offsets, count
    joined = jnp.concatenate([held[k] for k in offsets], axis=0)
    first = (count - 1 - lax.axis_index(axis)) * rows
    return [lax.dynamic_slice_in_dim(joined, first, count * rows, 0)], [None], 1


def in_order(held, axis):
    masks, count = sorted(held), lax.axis_size(axis)
    rows = held[0].shape[0]
    if rows % 16 == 0:
        return [held[k] for k in masks], masks
    joined = jnp.stack([held[k] for k in masks])
    order = jnp.bitwise_xor(jnp.arange(count), lax.axis_index(axis))
    return [joined[order].reshape((count * rows,) + joined.shape[2:])], [None]


def cost(flops, touched, exps=0):
    return pl.CostEstimate(flops=flops, bytes_accessed=touched, transcendentals=exps)


def call(kernel, outs, in_specs, scratch, estimate, out_specs=None):
    if out_specs is None:
        out_specs = jax.tree.map(lambda _: VMEM, outs)
    return pl.pallas_call(
        kernel,
        out_shape=outs,
        in_specs=in_specs,
        out_specs=out_specs,
        scratch_shapes=scratch,
        cost_estimate=estimate,
        compiler_params=pltpu.CompilerParams(vmem_limit_bytes=VMEM_LIMIT),
    )


def line_copies(refs, offsets, place, count, target, sems, act):
    for n, (ref, offset) in enumerate(zip(refs, offsets)):
        owner = 0 if offset is None else place + offset

        @pl.when((owner >= 0) & (owner < count))
        def _():
            copy = pltpu.make_async_copy(ref, target(owner), sems.at[n])
            getattr(copy, act)()


def mod_kernel(place_ref, cond_ref, w_ref, out_ref):
    requests, groups, width = cond_ref.shape[0], w_ref.shape[0], w_ref.shape[2]
    request = place_ref[0] // 2
    values = jnp.concatenate(
        [cond_ref[pl.ds(jnp.bitwise_xor(request, k), 1), :] for k in range(requests)], axis=0
    )
    activated = (values * (1.0 / (1.0 + jnp.exp(-values)))).astype(BF16)
    out_ref[...] = jnp.zeros(out_ref.shape, F32)
    for group in range(groups):
        out_ref[:, group, :width] = jnp.dot(
            activated, w_ref[group], preferred_element_type=F32
        )


def pack_kernel(qkv_ref, kv_ref, first_ref, second_ref):
    half = first_ref.shape[1] // 5
    for n, out_ref in enumerate((first_ref, second_ref)):
        low, high = n * half, (n + 1) * half
        for k in range(3):
            out_ref[:, k * half : (k + 1) * half] = qkv_ref[k, :, low:high]
        for k in range(2):
            out_ref[:, (3 + k) * half : (4 + k) * half] = kv_ref[:, k, low:high]


def norm_kernel(offsets, count, img, place_ref, mod_ref, *refs):
    blocks = refs[: len(offsets)]
    out_ref, x_ref, average_ref, inverse_ref, sems = refs[len(offsets) :]
    width, tokens = blocks[0].shape
    place = place_ref[1]
    target = lambda owner: x_ref.at[pl.ds(pl.multiple_of(owner * width, 16), width)]
    line_copies(blocks, offsets, place, count, target, sems, "start")
    line_copies(blocks, offsets, place, count, target, sems, "wait")
    total = width * count
    chunk = 128

    def turn(i, carry):
        at = pl.multiple_of(i * chunk, chunk)
        part = x_ref[pl.ds(at, chunk)].T
        out_ref[:, pl.ds(at, chunk)] = part
        wide = part.astype(F32)
        sums, squares = carry
        return sums + wide, squares + wide * wide

    zero = jnp.zeros((tokens, chunk), F32)
    sums, squares = lax.fori_loop(0, total // chunk, turn, (zero, zero))
    average = jnp.sum(sums, axis=1, keepdims=True) / total
    mean_square = jnp.sum(squares, axis=1, keepdims=True) / total
    inverse = lax.rsqrt(mean_square - average * average + EPS_NORM)
    average_ref[...] = jnp.broadcast_to(average, (tokens, chunk))
    inverse_ref[...] = jnp.broadcast_to(inverse, (tokens, chunk))

    def normalise(i, _):
        at = pl.multiple_of(i * chunk, chunk)
        here = pl.ds(at, chunk)
        for low, high, group in ((0, img, 0), (img, tokens, 3)):
            normed = out_ref[low:high, here].astype(F32) - average_ref[low:high]
            normed = normed * inverse_ref[low:high]
            stretch = 1.0 + mod_ref[group + 1 : group + 2, here]
            out_ref[low:high, here] = (normed * stretch + mod_ref[group : group + 1, here]).astype(BF16)
        return 0

    lax.fori_loop(0, total // chunk, normalise, 0)


def project_kernel(masks, img, head, place_ref, gain_ref, x_ref, *refs):
    blocks = refs[: len(masks)]
    q_ref, kv_ref, w_ref, sems = refs[len(masks) :]
    depth = blocks[0].shape[0]
    half = q_ref.shape[1]
    place = place_ref[0]
    copies = []
    for n, (ref, mask) in enumerate(zip(blocks, masks)):
        owner = 0 if mask is None else jnp.bitwise_xor(place, mask)
        copies.append(
            pltpu.make_async_copy(
                ref, w_ref.at[pl.ds(pl.multiple_of(owner * depth, 16), depth)], sems.at[n]
            )
        )
    for copy in copies:
        copy.start()
    for copy in copies:
        copy.wait()
    row = lax.broadcasted_iota(jnp.int32, (half, half), 0) // head
    col = lax.broadcasted_iota(jnp.int32, (half, half), 1) // head
    mean_of = jnp.where(row == col, 1.0 / head, 0.0).astype(BF16)

    def product(part, low, high):
        return jnp.dot(
            x_ref[low:high],
            w_ref[:, part * half : (part + 1) * half],
            preferred_element_type=F32,
        )

    def head_norm(values, gain):
        square = values * values
        mean_square = jnp.zeros_like(square)
        for _ in range(3):
            term = square.astype(BF16)
            mean_square += jnp.dot(term, mean_of, preferred_element_type=F32)
            square = square - term.astype(F32)
        return (values * lax.rsqrt(mean_square + EPS_NORM) * gain).astype(BF16)

    tokens = x_ref.shape[0]
    scaling = head ** (-0.5)
    queries = head_norm(product(0, 0, img), gain_ref[0:1])
    q_ref[...] = (queries.astype(F32) * scaling).astype(BF16)
    kv_ref[:img, :half] = head_norm(product(1, 0, img), gain_ref[1:2])
    kv_ref[:img, half:] = product(2, 0, img).astype(BF16)
    kv_ref[img:, :half] = head_norm(product(3, img, tokens), gain_ref[2:3])
    kv_ref[img:, half:] = product(4, img, tokens).astype(BF16)


def attend_kernel(img, txt, head, place_ref, q_ref, own_ref, peer_ref, out_ref):
    queries, half = q_ref.shape
    room = own_ref.shape[0] - img
    side = lax.rem(place_ref[0], 2)
    length = place_ref[2]
    slot = lax.broadcasted_iota(jnp.int32, (room, 1), 0)
    parts = []
    for ref, owner in ((own_ref, side), (peer_ref, 1 - side)):
        allowed = (slot < txt) & (owner * txt + slot < length)
        parts.append((ref[:, :half], ref[:, half:].T, allowed))
    lane = lax.broadcasted_iota(jnp.int32, (1, half), 1) // head
    step = 256 if queries % 256 == 0 else queries
    for k in range(half // head):
        for low in range(0, queries, step):
            query = jnp.where(lane == k, q_ref[low : low + step], 0.0).astype(BF16)
            scores, tops = [], []
            for keys, _, allowed in parts:
                score = lax.dot_general(
                    keys, query, (((1,), (1,)), ((), ())), preferred_element_type=F32
                )
                tail = jnp.where(allowed, score[img:], -1e30)
                scores += [score[:img], tail]
            top = jnp.max(scores[0], axis=0, keepdims=True)
            for score in scores[1:]:
                top = jnp.maximum(top, jnp.max(score, axis=0, keepdims=True))
            total = jnp.zeros_like(top)
            mixed = jnp.zeros((head, step), F32)
            for n, (_, values, _) in enumerate(parts):
                weights = jnp.exp(jnp.concatenate(scores[2 * n : 2 * n + 2], axis=0) - top)
                total += jnp.sum(weights, axis=0, keepdims=True)
                mixed += jnp.dot(
                    values[k * head : (k + 1) * head],
                    weights.astype(BF16),
                    preferred_element_type=F32,
                )
            out_ref[k * head : (k + 1) * head, low : low + step] = (mixed / total).astype(BF16)


def output_kernel(
    offsets, count, masks, place_ref, gate_ref, out_mod_ref, x_ref, *refs
):
    n_lines = len(offsets)
    firsts, refs = refs[:n_lines], refs[n_lines:]
    seconds, refs = refs[:n_lines], refs[n_lines:]
    weights, refs = refs[: len(masks)], refs[len(masks) :]
    out_ref, a_ref, w_ref, sems_a, sems_b, sems_w = refs
    width, tokens = x_ref.shape
    half = firsts[0].shape[0]
    place = place_ref[0]
    col = place_ref[1]
    copies = []
    for n, (ref, mask) in enumerate(zip(weights, masks)):
        owner = jnp.bitwise_xor(place, mask)
        copies.append(pltpu.make_async_copy(ref, w_ref.at[owner], sems_w.at[n]))
    for copy in copies:
        copy.start()
    lines = ((firsts, 0, sems_a), (seconds, 1, sems_b))
    for act in ("start", "wait"):
        for blocks, n, sems in lines:
            target = lambda owner, n=n: a_ref.at[
                pl.ds(pl.multiple_of((2 * owner + n) * half, half), half)
            ]
            line_copies(blocks, offsets, col, count, target, sems, act)
    for copy in copies:
        copy.wait()
    depth = w_ref.shape[2]
    blocks = w_ref.shape[0]

    projected = jnp.zeros((width, tokens), F32)
    for n in range(blocks):
        projected += jnp.dot(
            w_ref[n, :width], a_ref[n * depth : (n + 1) * depth], preferred_element_type=F32
        )
    updated = (x_ref[...].astype(F32) + gate_ref[...] * projected).astype(BF16)
    wide = updated.astype(F32)
    sums = jnp.sum(wide, axis=0, keepdims=True)
    squares = jnp.sum(wide * wide, axis=0, keepdims=True)

    per_col = blocks // count
    slab = width // per_col
    patch = out_ref.shape[0] - 8
    result = jnp.zeros((patch, tokens), F32)
    gains = jnp.zeros((patch, 1), F32)
    shifts = jnp.zeros((patch, 1), F32)
    for n in range(per_col):
        owner = col * per_col + n
        pieces = [
            w_ref[owner, width + k * patch : width + (k + 1) * patch]
            for k in range((w_ref.shape[1] - width) // patch)
        ]
        for k, piece in enumerate(pieces):
            low, high = k * depth, min((k + 1) * depth, slab)
            if low >= high:
                continue
            linear = piece[:, : high - low].astype(F32)
            gained = linear * (1.0 + out_mod_ref[n, 1:2, low:high])
            shifts += jnp.sum(linear * out_mod_ref[n, 0:1, low:high], axis=1, keepdims=True)
            gains += jnp.sum(gained, axis=1, keepdims=True)
            part = updated[n * slab + low : n * slab + high]
            for _ in range(3):
                term = gained.astype(BF16)
                result += jnp.dot(term, part, preferred_element_type=F32)
                gained = gained - term.astype(F32)
    out_ref[:patch, :tokens] = result
    row = lax.broadcasted_iota(jnp.int32, (8, tokens), 0)
    out_ref[patch:, :tokens] = jnp.where(row == 0, sums, jnp.where(row == 1, squares, 0.0))
    lane = lax.broadcasted_iota(jnp.int32, (patch, 128), 1)
    out_ref[:patch, tokens:] = jnp.where(lane == 0, gains, jnp.where(lane == 1, shifts, 0.0))
    out_ref[patch:, tokens:] = jnp.zeros((8, 128), F32)


def sigma_of(step_now):
    remain = 1.0 - step_now.astype(F32) / STEPS
    return 3.0 * remain / (1.0 + 2.0 * remain)


def per_device(
    hidden_img,
    hidden_txt,
    text_len,
    step_index,
    latent,
    cond,
    mod_weight,
    qkv_weight,
    kv_text_weight,
    q_gain,
    k_gain,
    out_weight,
    final_weight,
):
    row_count, col_count = lax.axis_size("row"), lax.axis_size("col")
    row_pos, col_pos = lax.axis_index("row"), lax.axis_index("col")
    request = row_pos // 2
    requests = cond.shape[0]
    img, width = hidden_img.shape
    txt = hidden_txt.shape[0]
    head = q_gain.shape[0]
    part_cols = qkv_weight.shape[2]
    half = part_cols // 2
    full_width = width * col_count
    length = lax.dynamic_index_in_dim(text_len, request, 0, keepdims=False)
    place = jnp.stack([row_pos, col_pos, length]).astype(jnp.int32)

    room = -(-txt // 128) * 128
    tokens = img + room
    x_own = jnp.concatenate(
        [hidden_img.T, jnp.pad(hidden_txt.T, ((0, 0), (0, room - txt)))], axis=1
    )
    x_blocks = line_gather(x_own, "col")
    chip_masks = [1 << bit for bit in range(1, row_count.bit_length() - 1)]
    packed = call(
        pack_kernel,
        (jax.ShapeDtypeStruct((qkv_weight.shape[0], 5 * half), BF16),) * 2,
        [VMEM, VMEM],
        [],
        cost(0, 20 * qkv_weight.shape[0] * half),
        (VMEM, VMEM),
    )(jnp.moveaxis(qkv_weight, 1, 0), kv_text_weight)
    gathered = []
    for n in range(2):
        order = chip_masks[::-1] if n == 0 else chip_masks
        gathered.append(doubling_gather(packed[n], "row", order + [1]))

    wide = -(-width // 128) * 128
    mod_part = call(
        mod_kernel,
        jax.ShapeDtypeStruct((requests, 8, wide), F32),
        [SMEM, VMEM, VMEM],
        [],
        cost(2 * requests * cond.shape[1] * 7 * width, mod_weight.size * 2),
    )(place, cond, jnp.moveaxis(mod_weight, 1, 0))
    first = chip_masks[-1]
    mod_part, gathered[0][first] = lax.optimization_barrier((mod_part, gathered[0][first]))
    mod_own = mod_part[0]
    for k in range(1, requests):
        mod_own = mod_own + swap(mod_part[k], "row", 2 * k)
    mod_own = mod_own + swap(mod_own, "row", 1)
    norm_mod = lax.dynamic_update_slice_in_dim(
        jnp.zeros((8, full_width), F32), mod_own[:, :width], col_pos * width, 1
    )
    mask = 1
    while mask < col_count:
        norm_mod = norm_mod + swap(norm_mod, "col", mask)
        mask *= 2
    mod_own = mod_own[:, :width]

    x_blocks, offsets, count = in_line(x_blocks, "col")
    ready = call(
        functools.partial(norm_kernel, offsets, count, img),
        jax.ShapeDtypeStruct((tokens, full_width), BF16),
        [SMEM, VMEM] + [ANY] * len(offsets),
        [
            pltpu.VMEM((full_width, tokens), BF16),
            pltpu.VMEM((tokens, 128), F32),
            pltpu.VMEM((tokens, 128), F32),
            pltpu.SemaphoreType.DMA((len(offsets),)),
        ],
        cost(12 * full_width * tokens, 4 * full_width * tokens),
    )(place, norm_mod, *x_blocks)

    gains = jnp.tile(jnp.concatenate([q_gain[None], k_gain], axis=0), (1, half // head))
    attended = []
    for n in range(2):
        blocks, masks = in_order(gathered[n], "row")
        queries, pair = call(
            functools.partial(project_kernel, masks, img, head),
            (
                jax.ShapeDtypeStruct((img, half), BF16),
                jax.ShapeDtypeStruct((tokens, 2 * half), BF16),
            ),
            [SMEM, VMEM, VMEM] + [ANY] * len(masks),
            [pltpu.VMEM((full_width, 5 * half), BF16), pltpu.SemaphoreType.DMA((len(masks),))],
            cost(2 * full_width * half * (3 * img + 2 * txt), 10 * full_width * half),
            (VMEM, VMEM),
        )(place, gains, ready, *blocks)
        peer = swap(pair, "row", 1)
        attended.append(
            call(
                functools.partial(attend_kernel, img, txt, head),
                jax.ShapeDtypeStruct((half, img), BF16),
                [SMEM, VMEM, VMEM, VMEM],
                [],
                cost(8 * half * tokens * img, 8 * half * tokens, 2 * tokens * img * half // head),
            )(place, queries, pair, peer)
        )

    head_depth, patch = final_weight.shape
    depth = out_weight.shape[0]
    folds = -(-head_depth // depth)
    tail = jnp.pad(final_weight.T, ((0, 0), (0, folds * depth - head_depth)))
    tail = jnp.swapaxes(tail.reshape(patch, folds, depth), 0, 1).reshape(folds * patch, depth)
    out_packed = jnp.concatenate([out_weight.T, tail], axis=0)
    out_blocks = doubling_gather(out_packed, "row", [1] + chip_masks)
    masks = sorted(out_blocks)
    offsets = list(range(1 - col_count, col_count))
    lines = [line_gather(block, "col") for block in attended]
    per_col = row_count // col_count
    out_mod = mod_own[5:7].reshape(2, per_col, width // per_col).swapaxes(0, 1)
    partial_sum = call(
        functools.partial(output_kernel, offsets, col_count, masks),
        jax.ShapeDtypeStruct((patch + 8, img + 128), F32),
        [SMEM, VMEM, VMEM, VMEM] + [ANY] * (2 * len(offsets) + len(masks)),
        [
            pltpu.VMEM((part_cols * col_count, img), BF16),
            pltpu.VMEM((row_count,) + out_packed.shape, BF16),
            pltpu.SemaphoreType.DMA((len(offsets),)),
            pltpu.SemaphoreType.DMA((len(offsets),)),
            pltpu.SemaphoreType.DMA((len(masks),)),
        ],
        cost(2 * part_cols * col_count * width * img, 8 * part_cols * col_count * width),
    )(
        place,
        mod_own[2][:, None],
        out_mod,
        hidden_img.T,
        *[line[k] for line in lines for k in offsets],
        *[out_blocks[k] for k in masks],
    )
    mask = 1
    while mask < col_count:
        partial_sum = partial_sum + swap(partial_sum, "col", mask)
        mask *= 2
    average = partial_sum[patch : patch + 1, :img] / full_width
    mean_square = partial_sum[patch + 1 : patch + 2, :img] / full_width
    inverse = lax.rsqrt(mean_square - average * average + EPS_NORM)
    gains = partial_sum[:patch, img : img + 1]
    shifts = partial_sum[:patch, img + 1 : img + 2]
    velocity = inverse * (partial_sum[:patch, :img] - average * gains) + shifts
    step_now = lax.dynamic_index_in_dim(step_index, request, 0, keepdims=False)
    sigma_step = sigma_of(step_now + 1) - sigma_of(step_now)
    latent_next = latent.T + sigma_step * velocity
    return (velocity.T, latent_next.T)


def solution(mesh):
    in_specs = (
        P("row", "col"),
        P("row", "col"),
        P(),
        P(),
        P("row", None),
        P(None, "row"),
        P("row", None, "col"),
        P("row", None, "col"),
        P("row", None, "col"),
        P(),
        P(),
        P("row", "col"),
        P("row", None),
    )
    out_specs = (P("row", None), P("row", None))
    return jax.shard_map(
        per_device, mesh=mesh, in_specs=in_specs, out_specs=out_specs, check_vma=False
    )
```

```python
import functools

import jax
import jax.numpy as jnp
from jax import lax
from jax.experimental import pallas as pl
from jax.experimental.pallas import tpu as pltpu
from jax.sharding import PartitionSpec as P

STEPS = 28
EPS_NORM = 1e-06
F32 = jnp.float32
BF16 = jnp.bfloat16
ANY = pl.BlockSpec(memory_space=pl.ANY)
VMEM = pl.BlockSpec(memory_space=pltpu.VMEM)
SMEM = pl.BlockSpec(memory_space=pltpu.SMEM)


def swap(block, axis, mask):
    count = lax.axis_size(axis)
    return lax.ppermute(block, axis, [(i, i ^ mask) for i in range(count)])


def shift(block, axis, step):
    count = lax.axis_size(axis)
    route = [(i, i + step) for i in range(count) if 0 <= i + step < count]
    return lax.ppermute(block, axis, route)


def line_gather(block, axis):
    count = lax.axis_size(axis)
    if count == 4:
        send = lambda held, route: lax.ppermute(held, axis, route)
        middle, outward = [(1, 2), (2, 1)], [(1, 0), (2, 3)]
        pair = swap(block, axis, 1)
        near = send(block, middle)
        far = send(pair, middle)
        inner = lambda p: (p == 1) | (p == 2)
        outer = lambda p: (p == 0) | (p == 3)
        other = lambda p: jnp.where(p < 2, 2, 1)
        other_far = lambda p: jnp.where(p < 2, 3, 0)
        always = lambda p: p >= 0
        return [
            (block, lambda p: p, always),
            (pair, lambda p: jnp.bitwise_xor(p, 1), always),
            (near, other, inner),
            (send(near, outward), other, outer),
            (far, other_far, inner),
            (send(far, outward), other_far, outer),
        ]
    held = {0: block}
    for step in range(1, count):
        held[-step] = shift(held[1 - step], axis, 1)
        held[step] = shift(held[step - 1], axis, -1)
    result = []
    for offset in sorted(held):
        inside = lambda p, offset=offset: (p + offset >= 0) & (p + offset < count)
        result.append((held[offset], lambda p, offset=offset: p + offset, inside))
    return result


def doubling_gather(block, axis, masks):
    held = {0: block}
    for mask in masks:
        for known in list(held):
            held[known | mask] = swap(held[known], axis, mask)
    return held


def in_order(held, axis):
    masks, count = sorted(held), lax.axis_size(axis)
    rows = held[0].shape[0]
    if rows % 16 == 0:
        return [held[k] for k in masks], masks
    joined = jnp.stack([held[k] for k in masks])
    order = jnp.bitwise_xor(jnp.arange(count), lax.axis_index(axis))
    return [joined[order].reshape((count * rows,) + joined.shape[2:])], [None]


def cost(flops, touched, exps=0):
    return pl.CostEstimate(flops=flops, bytes_accessed=touched, transcendentals=exps)


def call(kernel, outs, in_specs, scratch, estimate, out_specs=None, vmem=24):
    if out_specs is None:
        out_specs = jax.tree.map(lambda _: VMEM, outs)
    return pl.pallas_call(
        kernel,
        out_shape=outs,
        in_specs=in_specs,
        out_specs=out_specs,
        scratch_shapes=scratch,
        cost_estimate=estimate,
        compiler_params=pltpu.CompilerParams(vmem_limit_bytes=vmem * 1024 * 1024),
    )


def line_copies(refs, routes, place, target, sems, act):
    for n, (ref, (owner, held)) in enumerate(zip(refs, routes)):

        @pl.when(held(place))
        def _():
            copy = pltpu.make_async_copy(ref, target(owner(place)), sems.at[n])
            getattr(copy, act)()


def mod_kernel(place_ref, cond_ref, w_ref, out_ref):
    requests, groups, width = cond_ref.shape[0], w_ref.shape[0], w_ref.shape[2]
    request = place_ref[0] // 2
    values = jnp.concatenate(
        [cond_ref[pl.ds(jnp.bitwise_xor(request, k), 1), :] for k in range(requests)], axis=0
    )
    activated = (values * (1.0 / (1.0 + jnp.exp(-values)))).astype(BF16)
    out_ref[...] = jnp.zeros(out_ref.shape, F32)
    for group in range(groups):
        out_ref[:, group, :width] = jnp.dot(
            activated, w_ref[group], preferred_element_type=F32
        )


def pack_kernel(qkv_ref, kv_ref, first_ref, second_ref):
    half = first_ref.shape[1] // 5
    for n, out_ref in enumerate((first_ref, second_ref)):
        low, high = n * half, (n + 1) * half
        for k in range(3):
            out_ref[:, k * half : (k + 1) * half] = qkv_ref[k, :, low:high]
        for k in range(2):
            out_ref[:, (3 + k) * half : (4 + k) * half] = kv_ref[:, k, low:high]


def stats_kernel(img_ref, txt_ref, out_ref):
    img = img_ref.shape[1]
    txt = txt_ref.shape[0]
    out_ref[...] = jnp.zeros(out_ref.shape, F32)
    for values, low, high in (
        (img_ref[...].astype(F32), 0, img),
        (txt_ref[...].astype(F32).T, img, img + txt),
    ):
        out_ref[0:1, low:high] = jnp.sum(values, axis=0, keepdims=True)
        out_ref[1:2, low:high] = jnp.sum(values * values, axis=0, keepdims=True)


def norm_kernel(total, img_ref, txt_ref, stats_ref, mod_ref, *out_refs):
    width, img = img_ref.shape
    txt = txt_ref.shape[0]
    stats = stats_ref[...] / total
    row = lax.broadcasted_iota(jnp.int32, stats.shape, 0)
    average = stats[0:1]
    inverse = lax.rsqrt(stats[1:2] - average * average + EPS_NORM)
    columns = jnp.where(row == 0, average, inverse).T
    split = out_refs[0].shape[0]
    chunk = 128
    for low in range(0, img + txt, chunk):
        for start in range(0, width, chunk):
            stop = min(start + chunk, width)
            if low < img:
                high = min(low + chunk, img)
                values, group = img_ref[start:stop, low:high].T, 0
            else:
                high = min(low + chunk, img + txt)
                values, group = txt_ref[low - img : high - img, start:stop], 3
            normed = (values.astype(F32) - columns[low:high, 0:1]) * columns[low:high, 1:2]
            stretch = 1.0 + mod_ref[group + 1 : group + 2, start:stop]
            normed = (normed * stretch + mod_ref[group : group + 1, start:stop]).astype(BF16)
            for n, out_ref in enumerate(out_refs):
                top, bottom = max(low, n * split), min(high, (n + 1) * split)
                if top < bottom:
                    out_ref[top - n * split : bottom - n * split, start:stop] = normed[
                        top - low : bottom - low
                    ]


def project_kernel(routes, masks, img, head, place_ref, gain_ref, *refs):
    lines = []
    for _ in range(2):
        lines.append(refs[: len(routes)])
        refs = refs[len(routes) :]
    blocks, refs = refs[: len(masks)], refs[len(masks) :]
    q_ref, kv_ref, x_ref, w_ref, img_ref, txt_ref, sems_x, sems_w = refs
    split = lines[0][0].shape[0]
    txt = 2 * split - img
    count, width = x_ref.shape[0], x_ref.shape[2]
    half = q_ref.shape[1]
    place = place_ref[0]
    for n, line in enumerate(lines):
        target = lambda owner, n=n: x_ref.at[owner, pl.ds(n * split, split)]
        line_copies(line, routes, place_ref[1], target, sems_x.at[n], "start")
    chips = {}
    if masks == [None]:
        chips[0] = [pltpu.make_async_copy(blocks[0], w_ref, sems_w.at[0])]
    else:
        depth = blocks[0].shape[0]
        for n, (ref, mask) in enumerate(zip(blocks, masks)):
            owner = jnp.bitwise_xor(place, mask)
            here = pl.ds(pl.multiple_of(owner % 2 * depth, 16), depth)
            copy = pltpu.make_async_copy(ref, w_ref.at[owner // 2, here], sems_w.at[n])
            chips.setdefault(mask // 2, []).append(copy)
    for copies in chips.values():
        for copy in copies:
            copy.start()
    for n, line in enumerate(lines):
        target = lambda owner, n=n: x_ref.at[owner, pl.ds(n * split, split)]
        line_copies(line, routes, place_ref[1], target, sems_x.at[n], "wait")
    for k in range(count):
        for copy in chips.get(k, ()):
            copy.wait()
        chip = jnp.bitwise_xor(place // 2, k)
        for ref, low, rows, first, parts in ((img_ref, 0, img, 0, 3), (txt_ref, img, txt, 3, 2)):
            for part in range(parts):
                term = jnp.dot(
                    x_ref[chip, low : low + rows],
                    w_ref[chip, :, (first + part) * half : (first + part + 1) * half],
                    preferred_element_type=F32,
                )
                ref[part] = term if k == 0 else ref[part] + term

    row = lax.broadcasted_iota(jnp.int32, (half, half), 0) // head
    col = lax.broadcasted_iota(jnp.int32, (half, half), 1) // head
    mean_of = jnp.where(row == col, 1.0 / head, 0.0).astype(BF16)

    def head_norm(values, gain):
        square = values * values
        mean_square = jnp.zeros_like(square)
        for _ in range(3):
            term = square.astype(BF16)
            mean_square += jnp.dot(term, mean_of, preferred_element_type=F32)
            square = square - term.astype(F32)
        return (values * lax.rsqrt(mean_square + EPS_NORM) * gain).astype(BF16)

    scaling = head ** (-0.5)
    queries = head_norm(img_ref[0], gain_ref[0:1])
    q_ref[...] = (queries.astype(F32) * scaling).astype(BF16)
    kv_ref[:img, :half] = head_norm(img_ref[1], gain_ref[1:2])
    kv_ref[:img, half:] = img_ref[2].astype(BF16)
    kv_ref[img : img + txt, :half] = head_norm(txt_ref[0], gain_ref[2:3])
    kv_ref[img : img + txt, half:] = txt_ref[1].astype(BF16)
    kv_ref[img + txt :] = jnp.zeros((kv_ref.shape[0] - img - txt, 2 * half), BF16)


def attend_kernel(img, txt, head, place_ref, q_ref, own_ref, peer_ref, out_ref):
    queries, half = q_ref.shape
    room = own_ref.shape[0] - img
    side = lax.rem(place_ref[0], 2)
    length = place_ref[2]
    slot = lax.broadcasted_iota(jnp.int32, (room, 1), 0)
    parts = []
    for ref, owner in ((own_ref, side), (peer_ref, 1 - side)):
        allowed = (slot < txt) & (owner * txt + slot < length)
        parts.append((ref[:, :half], ref[:, half:].T, allowed))
    lane = lax.broadcasted_iota(jnp.int32, (1, half), 1) // head
    step = 256 if queries % 256 == 0 else queries
    for k in range(half // head):
        for low in range(0, queries, step):
            query = jnp.where(lane == k, q_ref[low : low + step], 0.0).astype(BF16)
            scores, tops = [], []
            for keys, _, allowed in parts:
                score = lax.dot_general(
                    keys, query, (((1,), (1,)), ((), ())), preferred_element_type=F32
                )
                tail = jnp.where(allowed, score[img:], -1e30)
                scores += [score[:img], tail]
            top = jnp.max(scores[0], axis=0, keepdims=True)
            for score in scores[1:]:
                top = jnp.maximum(top, jnp.max(score, axis=0, keepdims=True))
            total = jnp.zeros_like(top)
            mixed = jnp.zeros((head, step), F32)
            for n, (_, values, _) in enumerate(parts):
                weights = jnp.exp(jnp.concatenate(scores[2 * n : 2 * n + 2], axis=0) - top)
                total += jnp.sum(weights, axis=0, keepdims=True)
                mixed += jnp.dot(
                    values[k * head : (k + 1) * head],
                    weights.astype(BF16),
                    preferred_element_type=F32,
                )
            out_ref[k * head : (k + 1) * head, low : low + step] = (mixed / total).astype(BF16)


def output_kernel(
    routes, count, masks, place_ref, gate_ref, out_mod_ref, x_ref, *refs
):
    n_lines = len(routes)
    firsts, refs = refs[:n_lines], refs[n_lines:]
    seconds, refs = refs[:n_lines], refs[n_lines:]
    weights, refs = refs[: len(masks)], refs[len(masks) :]
    out_ref, a_ref, w_ref, sems_a, sems_b, sems_w = refs
    width, tokens = x_ref.shape
    half = firsts[0].shape[0]
    place = place_ref[0]
    col = place_ref[1]
    copies = []
    for n, (ref, mask) in enumerate(zip(weights, masks)):
        owner = jnp.bitwise_xor(place, mask)
        copies.append(pltpu.make_async_copy(ref, w_ref.at[owner], sems_w.at[n]))
    for copy in copies:
        copy.start()
    lines = ((firsts, 0, sems_a), (seconds, 1, sems_b))
    for act in ("start", "wait"):
        for blocks, n, sems in lines:
            target = lambda owner, n=n: a_ref.at[
                pl.ds(pl.multiple_of((2 * owner + n) * half, half), half)
            ]
            line_copies(blocks, routes, col, target, sems, act)
    for copy in copies:
        copy.wait()
    depth = w_ref.shape[2]
    blocks = w_ref.shape[0]

    projected = jnp.zeros((width, tokens), F32)
    for n in range(blocks):
        projected += jnp.dot(
            w_ref[n, :width], a_ref[n * depth : (n + 1) * depth], preferred_element_type=F32
        )
    updated = (x_ref[...].astype(F32) + gate_ref[...] * projected).astype(BF16)
    wide = updated.astype(F32)
    sums = jnp.sum(wide, axis=0, keepdims=True)
    squares = jnp.sum(wide * wide, axis=0, keepdims=True)

    per_col = blocks // count
    slab = width // per_col
    patch = out_ref.shape[0] - 8
    result = jnp.zeros((patch, tokens), F32)
    gains = jnp.zeros((patch, 1), F32)
    shifts = jnp.zeros((patch, 1), F32)
    for n in range(per_col):
        owner = col * per_col + n
        pieces = [
            w_ref[owner, width + k * patch : width + (k + 1) * patch]
            for k in range((w_ref.shape[1] - width) // patch)
        ]
        for k, piece in enumerate(pieces):
            low, high = k * depth, min((k + 1) * depth, slab)
            if low >= high:
                continue
            linear = piece[:, : high - low].astype(F32)
            gained = linear * (1.0 + out_mod_ref[n, 1:2, low:high])
            shifts += jnp.sum(linear * out_mod_ref[n, 0:1, low:high], axis=1, keepdims=True)
            gains += jnp.sum(gained, axis=1, keepdims=True)
            part = updated[n * slab + low : n * slab + high]
            for _ in range(3):
                term = gained.astype(BF16)
                result += jnp.dot(term, part, preferred_element_type=F32)
                gained = gained - term.astype(F32)
    out_ref[:patch, :tokens] = result
    row = lax.broadcasted_iota(jnp.int32, (8, tokens), 0)
    out_ref[patch:, :tokens] = jnp.where(row == 0, sums, jnp.where(row == 1, squares, 0.0))
    lane = lax.broadcasted_iota(jnp.int32, (patch, 128), 1)
    out_ref[:patch, tokens:] = jnp.where(lane == 0, gains, jnp.where(lane == 1, shifts, 0.0))
    out_ref[patch:, tokens:] = jnp.zeros((8, 128), F32)


def sigma_of(step_now):
    remain = 1.0 - step_now.astype(F32) / STEPS
    return 3.0 * remain / (1.0 + 2.0 * remain)


def per_device(
    hidden_img,
    hidden_txt,
    text_len,
    step_index,
    latent,
    cond,
    mod_weight,
    qkv_weight,
    kv_text_weight,
    q_gain,
    k_gain,
    out_weight,
    final_weight,
):
    row_count, col_count = lax.axis_size("row"), lax.axis_size("col")
    row_pos, col_pos = lax.axis_index("row"), lax.axis_index("col")
    request = row_pos // 2
    requests = cond.shape[0]
    img, width = hidden_img.shape
    txt = hidden_txt.shape[0]
    head = q_gain.shape[0]
    part_cols = qkv_weight.shape[2]
    half = part_cols // 2
    full_width = width * col_count
    length = lax.dynamic_index_in_dim(text_len, request, 0, keepdims=False)
    place = jnp.stack([row_pos, col_pos, length]).astype(jnp.int32)

    wide = -(-width // 128) * 128
    room = -(-txt // 128) * 128
    tokens = img + room
    mod_part = call(
        mod_kernel,
        jax.ShapeDtypeStruct((requests, 8, wide), F32),
        [SMEM, VMEM, VMEM],
        [],
        cost(2 * requests * cond.shape[1] * 7 * width, mod_weight.size * 2),
    )(place, cond, jnp.moveaxis(mod_weight, 1, 0))
    mod_own = mod_part[0]
    for k in range(1, requests):
        mod_own = mod_own + swap(mod_part[k], "row", 2 * k)
    mod_own = mod_own + swap(mod_own, "row", 1)
    stats = call(
        stats_kernel,
        jax.ShapeDtypeStruct((8, tokens), F32),
        [VMEM, VMEM],
        [],
        cost(4 * width * tokens, 2 * width * tokens),
    )(hidden_img.T, hidden_txt)
    mask = 1
    while mask < col_count:
        stats = stats + swap(stats, "col", mask)
        mask *= 2

    chip_masks = [1 << bit for bit in range(1, row_count.bit_length() - 1)]
    packed = call(
        pack_kernel,
        (jax.ShapeDtypeStruct((qkv_weight.shape[0], 5 * half), BF16),) * 2,
        [VMEM, VMEM],
        [],
        cost(0, 20 * qkv_weight.shape[0] * half),
        (VMEM, VMEM),
    )(jnp.moveaxis(qkv_weight, 1, 0), kv_text_weight)
    packed, mod_own = lax.optimization_barrier((packed, mod_own))
    gathered = []
    for n in range(2):
        order = chip_masks[::-1] if n == 0 else chip_masks
        gathered.append(doubling_gather(packed[n], "row", order + [1]))

    split = (img + txt) // 2
    ready = call(
        functools.partial(norm_kernel, full_width),
        (jax.ShapeDtypeStruct((split, width), BF16),) * 2,
        [VMEM] * 4,
        [],
        cost(12 * width * tokens, 4 * width * tokens),
        (VMEM, VMEM),
    )(hidden_img.T, hidden_txt, stats, mod_own)
    lines = [line_gather(part, "col") for part in ready]
    routes = [entry[1:] for entry in lines[0]]

    gains = jnp.tile(jnp.concatenate([q_gain[None], k_gain], axis=0), (1, half // head))
    attended = []
    for n in range(2):
        blocks, masks = in_order(gathered[n], "row")
        if masks == [None]:
            blocks = [blocks[0].reshape(col_count, width, 5 * half)]
        queries, pair = call(
            functools.partial(project_kernel, routes, masks, img, head),
            (
                jax.ShapeDtypeStruct((img, half), BF16),
                jax.ShapeDtypeStruct((tokens, 2 * half), BF16),
            ),
            [SMEM, VMEM] + [ANY] * (2 * len(routes) + len(masks)),
            [
                pltpu.VMEM((col_count, img + txt, width), BF16),
                pltpu.VMEM((col_count, width, 5 * half), BF16),
                pltpu.VMEM((3, img, half), F32),
                pltpu.VMEM((2, txt, half), F32),
                pltpu.SemaphoreType.DMA((2, len(routes))),
                pltpu.SemaphoreType.DMA((len(masks),)),
            ],
            cost(2 * full_width * half * (3 * img + 2 * txt), 10 * full_width * half),
            (VMEM, VMEM),
        )(place, gains, *[entry[0] for line in lines for entry in line], *blocks)
        peer = swap(pair, "row", 1)
        attended.append(
            call(
                functools.partial(attend_kernel, img, txt, head),
                jax.ShapeDtypeStruct((half, img), BF16),
                [SMEM, VMEM, VMEM, VMEM],
                [],
                cost(8 * half * tokens * img, 8 * half * tokens, 2 * tokens * img * half // head),
            )(place, queries, pair, peer)
        )

    head_depth, patch = final_weight.shape
    depth = out_weight.shape[0]
    folds = -(-head_depth // depth)
    tail = jnp.pad(final_weight.T, ((0, 0), (0, folds * depth - head_depth)))
    tail = jnp.swapaxes(tail.reshape(patch, folds, depth), 0, 1).reshape(folds * patch, depth)
    out_packed = jnp.concatenate([out_weight.T, tail], axis=0)
    out_blocks = doubling_gather(out_packed, "row", [1] + chip_masks)
    masks = sorted(out_blocks)
    lines = [line_gather(block, "col") for block in attended]
    per_col = row_count // col_count
    out_mod = mod_own[5:7, :width].reshape(2, per_col, width // per_col).swapaxes(0, 1)
    partial_sum = call(
        functools.partial(output_kernel, routes, col_count, masks),
        jax.ShapeDtypeStruct((patch + 8, img + 128), F32),
        [SMEM, VMEM, VMEM, VMEM] + [ANY] * (2 * len(routes) + len(masks)),
        [
            pltpu.VMEM((part_cols * col_count, img), BF16),
            pltpu.VMEM((row_count,) + out_packed.shape, BF16),
            pltpu.SemaphoreType.DMA((len(routes),)),
            pltpu.SemaphoreType.DMA((len(routes),)),
            pltpu.SemaphoreType.DMA((len(masks),)),
        ],
        cost(2 * part_cols * col_count * width * img, 8 * part_cols * col_count * width),
        vmem=48,
    )(
        place,
        mod_own[2, :width][:, None],
        out_mod,
        hidden_img.T,
        *[entry[0] for line in lines for entry in line],
        *[out_blocks[k] for k in masks],
    )
    mask = 1
    while mask < col_count:
        partial_sum = partial_sum + swap(partial_sum, "col", mask)
        mask *= 2
    average = partial_sum[patch : patch + 1, :img] / full_width
    mean_square = partial_sum[patch + 1 : patch + 2, :img] / full_width
    inverse = lax.rsqrt(mean_square - average * average + EPS_NORM)
    gains = partial_sum[:patch, img : img + 1]
    shifts = partial_sum[:patch, img + 1 : img + 2]
    velocity = inverse * (partial_sum[:patch, :img] - average * gains) + shifts
    step_now = lax.dynamic_index_in_dim(step_index, request, 0, keepdims=False)
    sigma_step = sigma_of(step_now + 1) - sigma_of(step_now)
    latent_next = latent.T + sigma_step * velocity
    return (velocity.T, latent_next.T)


def solution(mesh):
    in_specs = (
        P("row", "col"),
        P("row", "col"),
        P(),
        P(),
        P("row", None),
        P(None, "row"),
        P("row", None, "col"),
        P("row", None, "col"),
        P("row", None, "col"),
        P(),
        P(),
        P("row", "col"),
        P("row", None),
    )
    out_specs = (P("row", None), P("row", None))
    return jax.shard_map(
        per_device, mesh=mesh, in_specs=in_specs, out_specs=out_specs, check_vma=False
    )
```

```python
import functools

import jax
import jax.numpy as jnp
from jax import lax
from jax.experimental import pallas as pl
from jax.experimental.pallas import tpu as pltpu
from jax.sharding import PartitionSpec as P

STEPS = 28
EPS_NORM = 1e-06
F32 = jnp.float32
BF16 = jnp.bfloat16
HBM = pl.BlockSpec(memory_space=pltpu.HBM)
VMEM = pl.BlockSpec(memory_space=pltpu.VMEM)
SMEM = pl.BlockSpec(memory_space=pltpu.SMEM)


def swap(block, axis, mask):
    count = lax.axis_size(axis)
    return lax.ppermute(block, axis, [(i, i ^ mask) for i in range(count)])


def shift(block, axis, step):
    count = lax.axis_size(axis)
    route = [(i, i + step) for i in range(count) if 0 <= i + step < count]
    return lax.ppermute(block, axis, route)


def tie(*arrays):
    return lax.optimization_barrier(arrays)


def line_gather(block, axis):
    held = {0: block}
    for step in range(1, lax.axis_size(axis)):
        held[-step] = shift(held[1 - step], axis, 1)
        held[step] = shift(held[step - 1], axis, -1)
    return [held[k] for k in sorted(held)]


def line_routes(count):
    if count == 4:
        near = lambda p: jnp.where(p < 2, 2, 1)
        far = lambda p: jnp.where(p < 2, 3, 0)
        inner = lambda p: (p == 1) | (p == 2)
        outer = lambda p: (p == 0) | (p == 3)
        always = lambda p: p >= 0
        return [
            (lambda p: p, always),
            (lambda p: jnp.bitwise_xor(p, 1), always),
            (near, inner),
            (near, outer),
            (far, inner),
            (far, outer),
        ]
    result = []
    for offset in range(1 - count, count):
        inside = lambda p, offset=offset: (p + offset >= 0) & (p + offset < count)
        result.append((lambda p, offset=offset: p + offset, inside))
    return result


MIDDLE = [(1, 2), (2, 1)]
OUTWARD = [(1, 0), (2, 3)]


def line_four(block, axis):
    pair = swap(block, axis, 1)
    near = lax.ppermute(block, axis, MIDDLE)
    far = lax.ppermute(pair, axis, MIDDLE)
    near_end = lax.ppermute(near, axis, OUTWARD)
    return [block, pair, near, near_end, far, lax.ppermute(far, axis, OUTWARD)]


def gather_both(tokens, weights):
    lines = [[block] for block in tokens]
    out = lambda held: lax.ppermute(held, "col", OUTWARD)
    for line in lines:
        line += [swap(line[0], "col", 1), lax.ppermute(line[0], "col", MIDDLE)]
    held = [{0: weights[0]}, {0: weights[1]}]
    held[1][2] = swap(weights[1], "row", 2)
    held[0][4] = swap(weights[0], "row", 4)
    for n, line in enumerate(lines):
        if n == 1:
            line[1], line[2], held[1][2], held[0][4] = tie(
                line[1], line[2], held[1][2], held[0][4]
            )
        line += [out(line[2]), lax.ppermute(line[1], "col", MIDDLE)]
    held[0][2] = swap(weights[0], "row", 2)
    held[1][4] = swap(weights[1], "row", 4)
    held[0][6] = swap(held[0][4], "row", 2)
    held[1][6] = swap(held[1][2], "row", 4)
    for n, line in enumerate(lines):
        if n == 1:
            line[4], held[0][2], held[1][4] = tie(line[4], held[0][2], held[1][4])
        line.append(out(line[4]))
    for half in held:
        for mask in list(half):
            half[mask + 1] = swap(half[mask], "row", 1)
    return lines, held


def doubling_gather(block, axis, masks):
    held = {0: block}
    for mask in masks:
        for known in list(held):
            held[known | mask] = swap(held[known], axis, mask)
    return held


def in_order(held, axis):
    masks, count = sorted(held), lax.axis_size(axis)
    rows = held[0].shape[0]
    if rows % 16 == 0:
        return [held[k] for k in masks], masks
    joined = jnp.stack([held[k] for k in masks])
    order = jnp.bitwise_xor(jnp.arange(count), lax.axis_index(axis))
    return [joined[order].reshape((count * rows,) + joined.shape[2:])], [None]


def cost(us):
    return pl.CostEstimate(flops=int(us * 1.15e9), bytes_accessed=0, transcendentals=0)


def call(kernel, outs, in_specs, scratch, estimate, out_specs=None, vmem=16):
    if out_specs is None:
        out_specs = jax.tree.map(lambda _: VMEM, outs)
    return pl.pallas_call(
        kernel,
        out_shape=outs,
        in_specs=in_specs,
        out_specs=out_specs,
        scratch_shapes=scratch,
        cost_estimate=estimate,
        compiler_params=pltpu.CompilerParams(vmem_limit_bytes=vmem * 1024 * 1024),
    )


def line_copies(refs, routes, place, target, sems, act):
    for n, (ref, (owner, held)) in enumerate(zip(refs, routes)):

        @pl.when(held(place))
        def _():
            copy = pltpu.make_async_copy(ref, target(owner(place)), sems.at[n])
            getattr(copy, act)()


def mod_kernel(cond_ref, w_ref, out_ref):
    requests, groups, width = cond_ref.shape[0], w_ref.shape[0], w_ref.shape[2]
    request = lax.axis_index("row") // 2
    values = jnp.concatenate(
        [cond_ref[pl.ds(jnp.bitwise_xor(request, k), 1), :] for k in range(requests)], axis=0
    )
    activated = (values * (1.0 / (1.0 + jnp.exp(-values)))).astype(BF16)
    out_ref[...] = jnp.zeros(out_ref.shape, F32)
    for group in range(groups):
        out_ref[:, group, :width] = jnp.dot(
            activated, w_ref[group], preferred_element_type=F32
        )


def pack_kernel(qkv_ref, kv_ref, first_ref, second_ref):
    half = first_ref.shape[1] // 5
    for n, out_ref in enumerate((first_ref, second_ref)):
        low, high = n * half, (n + 1) * half
        for k in range(3):
            out_ref[:, k * half : (k + 1) * half] = qkv_ref[k, :, low:high]
        for k in range(2):
            out_ref[:, (3 + k) * half : (4 + k) * half] = kv_ref[:, k, low:high]


def stats_kernel(img_ref, txt_ref, out_ref):
    img = img_ref.shape[1]
    txt = txt_ref.shape[0]
    out_ref[...] = jnp.zeros(out_ref.shape, F32)
    for values, low, high in (
        (img_ref[...].astype(F32), 0, img),
        (txt_ref[...].astype(F32).T, img, img + txt),
    ):
        out_ref[0:1, low:high] = jnp.sum(values, axis=0, keepdims=True)
        out_ref[1:2, low:high] = jnp.sum(values * values, axis=0, keepdims=True)


def norm_kernel(total, img_ref, txt_ref, stats_ref, mod_ref, *out_refs):
    width, img = img_ref.shape
    txt = txt_ref.shape[0]
    stats = stats_ref[...] / total
    row = lax.broadcasted_iota(jnp.int32, stats.shape, 0)
    average = stats[0:1]
    inverse = lax.rsqrt(stats[1:2] - average * average + EPS_NORM)
    columns = jnp.where(row == 0, average, inverse).T
    split = out_refs[0].shape[0]
    chunk = 128
    for low in range(0, img + txt, chunk):
        for start in range(0, width, chunk):
            stop = min(start + chunk, width)
            if low < img:
                high = min(low + chunk, img)
                values, group = img_ref[start:stop, low:high].T, 0
            else:
                high = min(low + chunk, img + txt)
                values, group = txt_ref[low - img : high - img, start:stop], 3
            normed = (values.astype(F32) - columns[low:high, 0:1]) * columns[low:high, 1:2]
            stretch = 1.0 + mod_ref[group + 1 : group + 2, start:stop]
            normed = (normed * stretch + mod_ref[group : group + 1, start:stop]).astype(BF16)
            for n, out_ref in enumerate(out_refs):
                top, bottom = max(low, n * split), min(high, (n + 1) * split)
                if top < bottom:
                    out_ref[top - n * split : bottom - n * split, start:stop] = normed[
                        top - low : bottom - low
                    ]


def project_kernel(routes, masks, img, head, gain_ref, *refs):
    lines = []
    for _ in range(2):
        lines.append(refs[: len(routes)])
        refs = refs[len(routes) :]
    blocks, refs = refs[: len(masks)], refs[len(masks) :]
    q_ref, kv_ref, x_ref, w_ref, img_ref, txt_ref, sems_x, sems_w = refs
    split = lines[0][0].shape[0]
    txt = 2 * split - img
    count, width = x_ref.shape[0], x_ref.shape[2]
    half = q_ref.shape[1]
    place, col = lax.axis_index("row"), lax.axis_index("col")
    for n, line in enumerate(lines):
        target = lambda owner, n=n: x_ref.at[owner, pl.ds(n * split, split)]
        line_copies(line, routes, col, target, sems_x.at[n], "start")
    chips = {}
    if masks == [None]:
        chips[0] = [pltpu.make_async_copy(blocks[0], w_ref, sems_w.at[0])]
    else:
        depth = blocks[0].shape[0]
        for n, (ref, mask) in enumerate(zip(blocks, masks)):
            owner = jnp.bitwise_xor(place, mask)
            here = pl.ds(pl.multiple_of(owner % 2 * depth, 16), depth)
            copy = pltpu.make_async_copy(ref, w_ref.at[owner // 2, here], sems_w.at[n])
            chips.setdefault(mask // 2, []).append(copy)
    for copies in chips.values():
        for copy in copies:
            copy.start()
    for n, line in enumerate(lines):
        target = lambda owner, n=n: x_ref.at[owner, pl.ds(n * split, split)]
        line_copies(line, routes, col, target, sems_x.at[n], "wait")
    for k in range(count):
        for copy in chips.get(k, ()):
            copy.wait()
        chip = jnp.bitwise_xor(place // 2, k)
        for ref, low, rows, first, parts in ((img_ref, 0, img, 0, 3), (txt_ref, img, txt, 3, 2)):
            for part in range(parts):
                term = jnp.dot(
                    x_ref[chip, low : low + rows],
                    w_ref[chip, :, (first + part) * half : (first + part + 1) * half],
                    preferred_element_type=F32,
                )
                ref[part] = term if k == 0 else ref[part] + term

    row = lax.broadcasted_iota(jnp.int32, (half, half), 0) // head
    col = lax.broadcasted_iota(jnp.int32, (half, half), 1) // head
    mean_of = jnp.where(row == col, 1.0 / head, 0.0).astype(BF16)

    def head_norm(values, gain):
        square = values * values
        mean_square = jnp.zeros_like(square)
        for _ in range(3):
            term = square.astype(BF16)
            mean_square += jnp.dot(term, mean_of, preferred_element_type=F32)
            square = square - term.astype(F32)
        return (values * lax.rsqrt(mean_square + EPS_NORM) * gain).astype(BF16)

    scaling = head ** (-0.5)
    queries = head_norm(img_ref[0], gain_ref[0:1])
    q_ref[...] = (queries.astype(F32) * scaling).astype(BF16)
    kv_ref[:img, :half] = head_norm(img_ref[1], gain_ref[1:2])
    kv_ref[:img, half:] = img_ref[2].astype(BF16)
    kv_ref[img : img + txt, :half] = head_norm(txt_ref[0], gain_ref[2:3])
    kv_ref[img : img + txt, half:] = txt_ref[1].astype(BF16)
    kv_ref[img + txt :] = jnp.zeros((kv_ref.shape[0] - img - txt, 2 * half), BF16)


def attend_kernel(img, txt, head, length_ref, q_ref, own_ref, peer_ref, out_ref):
    queries, half = q_ref.shape
    room = own_ref.shape[0] - img
    place = lax.axis_index("row")
    side = lax.rem(place, 2)
    length = length_ref[place // 2]
    slot = lax.broadcasted_iota(jnp.int32, (room, 1), 0)
    parts = []
    for ref, owner in ((own_ref, side), (peer_ref, 1 - side)):
        allowed = (slot < txt) & (owner * txt + slot < length)
        parts.append((ref[:, :half], ref[:, half:].T, allowed))
    lane = lax.broadcasted_iota(jnp.int32, (1, half), 1) // head
    step = 256 if queries % 256 == 0 else queries
    for k in range(half // head):
        for low in range(0, queries, step):
            query = jnp.where(lane == k, q_ref[low : low + step], 0.0).astype(BF16)
            scores, tops = [], []
            for keys, _, allowed in parts:
                score = lax.dot_general(
                    keys, query, (((1,), (1,)), ((), ())), preferred_element_type=F32
                )
                tail = jnp.where(allowed, score[img:], -1e30)
                scores += [score[:img], tail]
            top = jnp.max(scores[0], axis=0, keepdims=True)
            for score in scores[1:]:
                top = jnp.maximum(top, jnp.max(score, axis=0, keepdims=True))
            total = jnp.zeros_like(top)
            mixed = jnp.zeros((head, step), F32)
            for n, (_, values, _) in enumerate(parts):
                weights = jnp.exp(jnp.concatenate(scores[2 * n : 2 * n + 2], axis=0) - top)
                total += jnp.sum(weights, axis=0, keepdims=True)
                mixed += jnp.dot(
                    values[k * head : (k + 1) * head],
                    weights.astype(BF16),
                    preferred_element_type=F32,
                )
            out_ref[k * head : (k + 1) * head, low : low + step] = (mixed / total).astype(BF16)


def output_kernel(
    routes, count, masks, gate_ref, out_mod_ref, x_ref, *refs
):
    n_lines = len(routes)
    firsts, refs = refs[:n_lines], refs[n_lines:]
    seconds, refs = refs[:n_lines], refs[n_lines:]
    weights, refs = refs[: len(masks)], refs[len(masks) :]
    out_ref, a_ref, w_ref, sems_a, sems_b, sems_w = refs
    width, tokens = x_ref.shape
    half = firsts[0].shape[0]
    place, col = lax.axis_index("row"), lax.axis_index("col")
    copies = []
    for n, (ref, mask) in enumerate(zip(weights, masks)):
        owner = jnp.bitwise_xor(place, mask)
        copies.append(pltpu.make_async_copy(ref, w_ref.at[owner], sems_w.at[n]))
    for copy in copies:
        copy.start()
    lines = ((firsts, 0, sems_a), (seconds, 1, sems_b))
    for act in ("start", "wait"):
        for blocks, n, sems in lines:
            target = lambda owner, n=n: a_ref.at[
                pl.ds(pl.multiple_of((2 * owner + n) * half, half), half)
            ]
            line_copies(blocks, routes, col, target, sems, act)
    for copy in copies:
        copy.wait()
    depth = w_ref.shape[2]
    blocks = w_ref.shape[0]

    projected = jnp.zeros((width, tokens), F32)
    for n in range(blocks):
        projected += jnp.dot(
            w_ref[n, :width], a_ref[n * depth : (n + 1) * depth], preferred_element_type=F32
        )
    updated = (x_ref[...].astype(F32) + gate_ref[...] * projected).astype(BF16)
    wide = updated.astype(F32)
    sums = jnp.sum(wide, axis=0, keepdims=True)
    squares = jnp.sum(wide * wide, axis=0, keepdims=True)

    per_col = blocks // count
    slab = width // per_col
    patch = out_ref.shape[0] - 8
    result = jnp.zeros((patch, tokens), F32)
    gains = jnp.zeros((patch, 1), F32)
    shifts = jnp.zeros((patch, 1), F32)
    for n in range(per_col):
        owner = col * per_col + n
        pieces = [
            w_ref[owner, width + k * patch : width + (k + 1) * patch]
            for k in range((w_ref.shape[1] - width) // patch)
        ]
        for k, piece in enumerate(pieces):
            low, high = k * depth, min((k + 1) * depth, slab)
            if low >= high:
                continue
            linear = piece[:, : high - low].astype(F32)
            gained = linear * (1.0 + out_mod_ref[n, 1:2, low:high])
            shifts += jnp.sum(linear * out_mod_ref[n, 0:1, low:high], axis=1, keepdims=True)
            gains += jnp.sum(gained, axis=1, keepdims=True)
            part = updated[n * slab + low : n * slab + high]
            for _ in range(3):
                term = gained.astype(BF16)
                result += jnp.dot(term, part, preferred_element_type=F32)
                gained = gained - term.astype(F32)
    out_ref[:patch, :tokens] = result
    row = lax.broadcasted_iota(jnp.int32, (8, tokens), 0)
    out_ref[patch:, :tokens] = jnp.where(row == 0, sums, jnp.where(row == 1, squares, 0.0))
    lane = lax.broadcasted_iota(jnp.int32, (patch, 128), 1)
    out_ref[:patch, tokens:] = jnp.where(lane == 0, gains, jnp.where(lane == 1, shifts, 0.0))
    out_ref[patch:, tokens:] = jnp.zeros((8, 128), F32)


def sigma_of(step_now):
    remain = 1.0 - step_now.astype(F32) / STEPS
    return 3.0 * remain / (1.0 + 2.0 * remain)


def per_device(
    hidden_img,
    hidden_txt,
    text_len,
    step_index,
    latent,
    cond,
    mod_weight,
    qkv_weight,
    kv_text_weight,
    q_gain,
    k_gain,
    out_weight,
    final_weight,
):
    row_count, col_count = lax.axis_size("row"), lax.axis_size("col")
    request = lax.axis_index("row") // 2
    requests = cond.shape[0]
    img, width = hidden_img.shape
    txt = hidden_txt.shape[0]
    head = q_gain.shape[0]
    part_cols = qkv_weight.shape[2]
    half = part_cols // 2
    full_width = width * col_count

    wide = -(-width // 128) * 128
    room = -(-txt // 128) * 128
    tokens = img + room
    mod_part = call(
        mod_kernel,
        jax.ShapeDtypeStruct((requests, 8, wide), F32),
        [VMEM, VMEM],
        [],
        cost(2),
    )(cond, jnp.moveaxis(mod_weight, 1, 0))
    mod_own = mod_part[0]
    for k in range(1, requests):
        mod_own = mod_own + swap(mod_part[k], "row", 2 * k)
    mod_own = mod_own + swap(mod_own, "row", 1)
    stats = call(
        stats_kernel,
        jax.ShapeDtypeStruct((8, tokens), F32),
        [VMEM, VMEM],
        [],
        cost(1),
    )(hidden_img.T, hidden_txt)
    mask = 1
    while mask < col_count:
        stats = stats + swap(stats, "col", mask)
        mask *= 2

    chip_masks = [1 << bit for bit in range(1, row_count.bit_length() - 1)]
    packed = call(
        pack_kernel,
        (jax.ShapeDtypeStruct((qkv_weight.shape[0], 5 * half), BF16),) * 2,
        [VMEM, VMEM],
        [],
        cost(2),
        (VMEM, VMEM),
    )(jnp.moveaxis(qkv_weight, 1, 0), kv_text_weight)
    packed, mod_own = lax.optimization_barrier((packed, mod_own))
    split = (img + txt) // 2
    ready = call(
        functools.partial(norm_kernel, full_width),
        (jax.ShapeDtypeStruct((split, width), BF16),) * 2,
        [VMEM] * 4,
        [],
        cost(1),
        (VMEM, VMEM),
    )(hidden_img.T, hidden_txt, stats, mod_own)
    routes = line_routes(col_count)
    small = col_count == 4 and row_count == 8
    if small:
        lines, gathered = gather_both(ready, packed)
    else:
        lines = [line_gather(part, "col") for part in ready]
        gathered = [doubling_gather(part, "row", chip_masks + [1]) for part in packed]

    gains = jnp.tile(jnp.concatenate([q_gain[None], k_gain], axis=0), (1, half // head))
    attended = []
    for n in range(2):
        blocks, masks = in_order(gathered[n], "row")
        if masks == [None]:
            blocks = [blocks[0].reshape(col_count, width, 5 * half)]
        queries, pair = call(
            functools.partial(project_kernel, routes, masks, img, head),
            (
                jax.ShapeDtypeStruct((img, half), BF16),
                jax.ShapeDtypeStruct((tokens, 2 * half), BF16),
            ),
            [VMEM] + [HBM] * (2 * len(routes) + len(masks)),
            [
                pltpu.VMEM((col_count, img + txt, width), BF16),
                pltpu.VMEM((col_count, width, 5 * half), BF16),
                pltpu.VMEM((3, img, half), F32),
                pltpu.VMEM((2, txt, half), F32),
                pltpu.SemaphoreType.DMA((2, len(routes))),
                pltpu.SemaphoreType.DMA((len(masks),)),
            ],
            cost(8),
            (VMEM, VMEM),
            vmem=56,
        )(gains, *[part for line in lines for part in line], *blocks)
        peer = swap(pair, "row", 1)
        attended.append(
            call(
                functools.partial(attend_kernel, img, txt, head),
                jax.ShapeDtypeStruct((half, img), BF16),
                [SMEM, VMEM, VMEM, VMEM],
                [],
                cost(6),
                vmem=24,
            )(text_len, queries, pair, peer)
        )

    head_depth, patch = final_weight.shape
    depth = out_weight.shape[0]
    folds = -(-head_depth // depth)
    tail = jnp.pad(final_weight.T, ((0, 0), (0, folds * depth - head_depth)))
    tail = jnp.swapaxes(tail.reshape(patch, folds, depth), 0, 1).reshape(folds * patch, depth)
    out_packed = jnp.concatenate([out_weight.T, tail], axis=0)
    out_blocks = doubling_gather(out_packed, "row", [1] + chip_masks)
    masks = sorted(out_blocks)
    lines = [(line_four if small else line_gather)(block, "col") for block in attended]
    per_col = row_count // col_count
    out_mod = mod_own[5:7, :width].reshape(2, per_col, width // per_col).swapaxes(0, 1)
    partial_sum = call(
        functools.partial(output_kernel, routes, col_count, masks),
        jax.ShapeDtypeStruct((patch + 8, img + 128), F32),
        [VMEM, VMEM, VMEM] + [HBM] * (2 * len(routes) + len(masks)),
        [
            pltpu.VMEM((part_cols * col_count, img), BF16),
            pltpu.VMEM((row_count,) + out_packed.shape, BF16),
            pltpu.SemaphoreType.DMA((len(routes),)),
            pltpu.SemaphoreType.DMA((len(routes),)),
            pltpu.SemaphoreType.DMA((len(masks),)),
        ],
        cost(5),
        vmem=56,
    )(
        mod_own[2, :width][:, None],
        out_mod,
        hidden_img.T,
        *[part for line in lines for part in line],
        *[out_blocks[k] for k in masks],
    )
    mask = 1
    while mask < col_count:
        partial_sum = partial_sum + swap(partial_sum, "col", mask)
        mask *= 2
    average = partial_sum[patch : patch + 1, :img] / full_width
    mean_square = partial_sum[patch + 1 : patch + 2, :img] / full_width
    inverse = lax.rsqrt(mean_square - average * average + EPS_NORM)
    gains = partial_sum[:patch, img : img + 1]
    shifts = partial_sum[:patch, img + 1 : img + 2]
    velocity = inverse * (partial_sum[:patch, :img] - average * gains) + shifts
    step_now = lax.dynamic_index_in_dim(step_index, request, 0, keepdims=False)
    sigma_step = sigma_of(step_now + 1) - sigma_of(step_now)
    latent_next = latent.T + sigma_step * velocity
    return (velocity.T, latent_next.T)


def solution(mesh):
    in_specs = (
        P("row", "col"),
        P("row", "col"),
        P(),
        P(),
        P("row", None),
        P(None, "row"),
        P("row", None, "col"),
        P("row", None, "col"),
        P("row", None, "col"),
        P(),
        P(),
        P("row", "col"),
        P("row", None),
    )
    out_specs = (P("row", None), P("row", None))
    return jax.shard_map(
        per_device, mesh=mesh, in_specs=in_specs, out_specs=out_specs, check_vma=False
    )
```

```python
import functools

import jax
import jax.numpy as jnp
from jax import lax
from jax.experimental import pallas as pl
from jax.experimental.pallas import tpu as pltpu
from jax.sharding import PartitionSpec as P

STEPS = 28
EPS_NORM = 1e-06
ATTEND = 6
PROJECT = 20
AHEAD = 2
EARLY = 48
F32 = jnp.float32
BF16 = jnp.bfloat16
HBM = pl.BlockSpec(memory_space=pltpu.HBM)
VMEM = pl.BlockSpec(memory_space=pltpu.VMEM)
SMEM = pl.BlockSpec(memory_space=pltpu.SMEM)


def swap(block, axis, mask):
    count = lax.axis_size(axis)
    return lax.ppermute(block, axis, [(i, i ^ mask) for i in range(count)])


def shift(block, axis, step):
    count = lax.axis_size(axis)
    route = [(i, i + step) for i in range(count) if 0 <= i + step < count]
    return lax.ppermute(block, axis, route)


def tie(*arrays):
    return lax.optimization_barrier(arrays)


def line_gather(block, axis):
    held = {0: block}
    for step in range(1, lax.axis_size(axis)):
        held[-step] = shift(held[1 - step], axis, 1)
        held[step] = shift(held[step - 1], axis, -1)
    return [held[k] for k in sorted(held)]


def line_routes(count):
    if count == 4:
        near = lambda p: jnp.where(p < 2, 2, 1)
        far = lambda p: jnp.where(p < 2, 3, 0)
        inner = lambda p: (p == 1) | (p == 2)
        outer = lambda p: (p == 0) | (p == 3)
        always = lambda p: p >= 0
        return [
            (lambda p: p, always),
            (lambda p: jnp.bitwise_xor(p, 1), always),
            (near, inner),
            (near, outer),
            (far, inner),
            (far, outer),
        ]
    result = []
    for offset in range(1 - count, count):
        inside = lambda p, offset=offset: (p + offset >= 0) & (p + offset < count)
        result.append((lambda p, offset=offset: p + offset, inside))
    return result


def far_routes(count):
    routes = list(enumerate(line_routes(count)))
    if count == 4:
        return routes[:4], routes[4:], routes[4][1][0]
    far = lambda p: count - 1 - p
    early, late = [], []
    for n, (owner, held) in routes:
        is_far = lambda p, owner=owner: owner(p) == far(p)
        early.append((n, (owner, lambda p, held=held, is_far=is_far: held(p) & ~is_far(p))))
        late.append((n, (owner, lambda p, held=held, is_far=is_far: held(p) & is_far(p))))
    return early, late, far


MIDDLE = [(1, 2), (2, 1)]
OUTWARD = [(1, 0), (2, 3)]


def line_four(block, axis):
    pair = swap(block, axis, 1)
    near = lax.ppermute(block, axis, MIDDLE)
    far = lax.ppermute(pair, axis, MIDDLE)
    near_end = lax.ppermute(near, axis, OUTWARD)
    return [block, pair, near, near_end, far, lax.ppermute(far, axis, OUTWARD)]


def gather_both(tokens, weights):
    send = lambda held, route: lax.ppermute(held, "col", route)
    first, second = weights
    pair, near = swap(tokens, "col", 1), send(tokens, MIDDLE)
    first_y, second_x = swap(first, "row", 4), swap(second, "row", 2)
    pair, near, first_y, second_x, first, second = tie(
        pair, near, first_y, second_x, first, second
    )
    near_end, far = send(near, OUTWARD), send(pair, MIDDLE)
    first_x, second_y = swap(first, "row", 2), swap(second, "row", 4)
    near_end, far, first_x, second_y, first_y, second_x, tokens, pair, near = tie(
        near_end, far, first_x, second_y, first_y, second_x, tokens, pair, near
    )
    far_end = send(far, OUTWARD)
    other = lambda held: swap(held, "row", 1)
    peer = other(tokens)
    peer, pair, near, near_end, far = tie(peer, pair, near, near_end, far)
    peers = [peer, other(pair), other(near), other(near_end), other(far), other(far_end)]
    held = [
        {0: first, 4: first_y, 2: first_x, 6: swap(first_y, "row", 2)},
        {0: second, 2: second_x, 4: second_y, 6: swap(second_x, "row", 4)},
    ]
    return [tokens, pair, near, near_end, far, far_end], peers, held


def direct_gather(block, axis, masks):
    return {mask: swap(block, axis, mask) if mask else block for mask in masks}


def doubling_gather(block, axis, masks):
    held = {0: block}
    for mask in masks:
        for known in list(held):
            held[known | mask] = swap(held[known], axis, mask)
    return held


def in_order(pieces, axis):
    masks, place = sorted(pieces[0]), lax.axis_index(axis)
    core = place % 2
    joined = jnp.stack([jnp.stack([piece[k] for k in masks]) for piece in pieces], axis=1)
    joined = joined[jnp.bitwise_xor(jnp.arange(len(masks)), place // 2)]
    joined = jnp.where(core == 0, joined, joined[:, ::-1])
    return joined.reshape(joined.shape[0], -1, joined.shape[-1])


def cost(us):
    return pl.CostEstimate(flops=int(us * 1.15e9), bytes_accessed=0, transcendentals=0)


def call(kernel, outs, in_specs, scratch, estimate, out_specs=None, vmem=16):
    if out_specs is None:
        out_specs = jax.tree.map(lambda _: VMEM, outs)
    return pl.pallas_call(
        kernel,
        out_shape=outs,
        in_specs=in_specs,
        out_specs=out_specs,
        scratch_shapes=scratch,
        cost_estimate=estimate,
        compiler_params=pltpu.CompilerParams(vmem_limit_bytes=vmem * 1024 * 1024),
    )


def line_copies(refs, routes, place, target, sems, act):
    for n, (ref, (owner, held)) in enumerate(zip(refs, routes)):

        @pl.when(held(place))
        def _():
            copy = pltpu.make_async_copy(ref, target(owner(place)), sems.at[n])
            getattr(copy, act)()


def mod_kernel(cond_ref, w_ref, out_ref):
    requests, groups, width = cond_ref.shape[0], w_ref.shape[0], w_ref.shape[2]
    request = lax.axis_index("row") // 2
    values = jnp.concatenate(
        [cond_ref[pl.ds(jnp.bitwise_xor(request, k), 1), :] for k in range(requests)], axis=0
    )
    activated = (values * (1.0 / (1.0 + jnp.exp(-values)))).astype(BF16)
    out_ref[...] = jnp.zeros(out_ref.shape, F32)
    for group in range(groups):
        out_ref[:, group, :width] = jnp.dot(
            activated, w_ref[group], preferred_element_type=F32
        )


def pack_kernel(qkv_ref, kv_ref, keep_ref, give_ref):
    half = keep_ref.shape[1] // 5
    first = lax.axis_index("row") % 2 == 0
    for k in range(5):
        rows = qkv_ref[k] if k < 3 else kv_ref[:, k - 3]
        low, high = rows[:, :half], rows[:, half:]
        here = slice(k * half, (k + 1) * half)
        keep_ref[:, here] = jnp.where(first, low, high)
        give_ref[:, here] = jnp.where(first, high, low)


def stats_kernel(img_ref, txt_ref, out_ref):
    img = img_ref.shape[1]
    txt = txt_ref.shape[0]
    out_ref[...] = jnp.zeros(out_ref.shape, F32)
    for values, low, high in (
        (img_ref[...].astype(F32), 0, img),
        (txt_ref[...].astype(F32).T, img, img + txt),
    ):
        out_ref[0:1, low:high] = jnp.sum(values, axis=0, keepdims=True)
        out_ref[1:2, low:high] = jnp.sum(values * values, axis=0, keepdims=True)


def norm_kernel(total, img_ref, txt_ref, stats_ref, mod_ref, out_ref):
    width, img = img_ref.shape
    txt = txt_ref.shape[0]
    stats = stats_ref[...] / total
    row = lax.broadcasted_iota(jnp.int32, stats.shape, 0)
    average = stats[0:1]
    inverse = lax.rsqrt(stats[1:2] - average * average + EPS_NORM)
    columns = jnp.where(row == 0, average, inverse).T
    chunk = 128
    for low in range(0, img + txt, chunk):
        for start in range(0, width, chunk):
            stop = min(start + chunk, width)
            if low < img:
                high = min(low + chunk, img)
                values, group = img_ref[start:stop, low:high].T, 0
            else:
                high = min(low + chunk, img + txt)
                values, group = txt_ref[low - img : high - img, start:stop], 3
            normed = (values.astype(F32) - columns[low:high, 0:1]) * columns[low:high, 1:2]
            stretch = 1.0 + mod_ref[group + 1 : group + 2, start:stop]
            normed = normed * stretch + mod_ref[group : group + 1, start:stop]
            out_ref[low:high, start:stop] = normed.astype(BF16)


def attend(img, txt, head, length_ref, queries, keys, values, out_ref):
    width = queries.shape[1]
    place = lax.axis_index("row")
    side = lax.rem(place, 2)
    slot = lax.broadcasted_iota(jnp.int32, (2 * txt, 1), 0)
    other = (slot >= txt).astype(jnp.int32)
    owner = jnp.where(other == 1, 1 - side, side)
    allowed = owner * txt + slot - other * txt < length_ref[place // 2]
    turned = values.T
    ones = jnp.ones((16, keys.shape[0]), BF16)
    rows = [
        jnp.concatenate([turned[k * head : (k + 1) * head], ones], axis=0)
        for k in range(width // head)
    ]
    lane = lax.broadcasted_iota(jnp.int32, (1, width), 1) // head
    step = 256 if img % 256 == 0 else img

    def scores_of(k, low):
        query = jnp.where(lane == k, queries[low : low + step], 0.0).astype(BF16)
        score = lax.dot_general(
            keys, query, (((1,), (1,)), ((), ())), preferred_element_type=F32
        )
        tail = jnp.where(allowed, score[2 * img :], -1e30)
        return jnp.concatenate([score[: 2 * img], tail], axis=0)

    work = [(k, low) for k in range(width // head) for low in range(0, img, step)]
    ahead = scores_of(*work[0])
    for n, (k, low) in enumerate(work):
        scores = ahead
        if n + 1 < len(work):
            ahead = scores_of(*work[n + 1])
        weights = jnp.exp(scores - jnp.max(scores, axis=0, keepdims=True)).astype(BF16)
        mixed = jnp.dot(rows[k], weights, preferred_element_type=F32)
        out_ref[k * head : (k + 1) * head, low : low + step] = (
            mixed[:head] / mixed[head : head + 1]
        ).astype(BF16)


def attend_kernel(img, txt, head, length_ref, q_ref, k_ref, v_ref, out_ref, *scratch):
    parts, sems = scratch[:-1], scratch[-1]
    copies = [
        pltpu.make_async_copy(ref, part, sems.at[n])
        for n, (ref, part) in enumerate(zip((q_ref, k_ref, v_ref), parts))
    ]
    for copy in copies:
        copy.start()
    for copy in copies:
        copy.wait()
    attend(img, txt, head, length_ref, *[part[...] for part in parts], out_ref)


def project_kernel(routes, masks, img, head, length_ref, gain_ref, *refs):
    lines = refs[: len(routes)], refs[len(routes) : 2 * len(routes)]
    refs = refs[2 * len(routes) :]
    n_blocks = 2 * len(masks) if masks else 1
    blocks, refs = refs[:n_blocks], refs[n_blocks:]
    outs, (x_ref, w_ref, img_ref, txt_ref, sems_x, sems_w) = refs[:-6], refs[-6:]
    tokens = lines[0][0].shape[0]
    txt = tokens - img
    count, _, width = x_ref.shape
    half = img_ref.shape[1] // 3
    place, col = lax.axis_index("row"), lax.axis_index("col")
    chip, core = place // 2, lax.rem(place, 2)

    def copy_lines(act):
        for n, line in enumerate(lines):
            for k, (low, high, to) in enumerate(
                ((0, img, n * img), (img, tokens, 2 * img + n * txt))
            ):
                parts = [ref.at[pl.ds(low, high - low)] for ref in line]
                target = lambda owner: x_ref.at[owner, pl.ds(to, high - low)]
                line_copies(parts, routes, col, target, sems_x.at[n, k], act)

    copy_lines("start")
    stages = []
    for k in range(count):
        copies = []
        if not masks:
            if k == 0:
                copies.append(pltpu.make_async_copy(blocks[0], w_ref, sems_w.at[0, 0]))
        else:
            depth = blocks[0].shape[0]
            for piece in range(2):
                row = jnp.where(core == piece, 0, depth)
                target = w_ref.at[
                    jnp.bitwise_xor(chip, k), pl.ds(pl.multiple_of(row, 16), depth)
                ]
                ref = blocks[piece * len(masks) + k]
                copies.append(pltpu.make_async_copy(ref, target, sems_w.at[piece, k]))
        stages.append(copies)

    def start(n):
        for copy in stages[n] if n < count else ():
            copy.start()

    for n in range(AHEAD):
        start(n)
    row = lax.broadcasted_iota(jnp.int32, (half, half), 0) // head
    column = lax.broadcasted_iota(jnp.int32, (half, half), 1) // head
    mean_of = jnp.where(row == column, 1.0 / head, 0.0).astype(BF16)

    def head_norm(values, gain):
        square = values * values
        mean_square = jnp.zeros_like(square)
        for _ in range(3):
            term = square.astype(BF16)
            mean_square += jnp.dot(term, mean_of, preferred_element_type=F32)
            square = square - term.astype(F32)
        return (values * lax.rsqrt(mean_square + EPS_NORM) * gain).astype(BF16)

    copy_lines("wait")
    for k in range(count):
        for copy in stages[k]:
            copy.wait()
        start(k + AHEAD)
        here = jnp.bitwise_xor(chip, k)
        for ref, low, high, first, parts in (
            (img_ref, 0, 2 * img, 0, 3),
            (txt_ref, 2 * img, 2 * tokens, 3, 2),
        ):
            term = jnp.dot(
                x_ref[here, low:high],
                w_ref[here, :, first * half : (first + parts) * half],
                preferred_element_type=F32,
            )
            ref[...] = term if k == 0 else ref[...] + term
    scaling = head ** (-0.5)
    queries = head_norm(img_ref[:, :half], gain_ref[0:1])
    queries = (queries.astype(F32) * scaling).astype(BF16)
    keys = jnp.concatenate(
        [
            head_norm(img_ref[:, half : 2 * half], gain_ref[1:2]),
            head_norm(txt_ref[:, :half], gain_ref[2:3]),
        ],
        axis=0,
    )
    values = jnp.concatenate(
        [img_ref[:, 2 * half :].astype(BF16), txt_ref[:, half:].astype(BF16)], axis=0
    )
    for ref, part in zip(outs[1:], (queries[img:], keys, values)):
        ref[...] = part
    attend(img, txt, head, length_ref, queries[:img], keys, values, outs[0])


def place_heads(lines, routes, col, target, sems):
    core = lax.rem(lax.axis_index("row"), 2)
    size = lines[0][0].shape[0]
    for act in ("start", "wait"):
        for n, line in enumerate(lines):
            rows = pl.ds(pl.multiple_of(jnp.where(core == n, 0, size), 16), size)
            line_copies(line, routes, col, lambda owner: target(owner, rows), sems.at[n], act)


def early_kernel(routes, far, masks, mod_ref, *refs):
    n_lines = len(routes)
    lines = [refs[n * n_lines : (n + 1) * n_lines] for n in range(2)]
    refs = refs[2 * n_lines :]
    weights, refs = refs[:2], refs[2:]
    sum_ref, far_ref, gain_ref, const_ref, a_ref, w_ref, sems_a, sems_w = refs
    width = sum_ref.shape[0]
    count = a_ref.shape[0]
    depth = w_ref.shape[2]
    place, col = lax.axis_index("row"), lax.axis_index("col")
    copies = []
    for k, ref in enumerate(weights):
        for n, mask in enumerate(masks):
            target = w_ref.at[jnp.bitwise_xor(place, mask + k)]
            source = ref.at[pl.ds(n * w_ref.shape[1], w_ref.shape[1])]
            copies.append(pltpu.make_async_copy(source, target, sems_w.at[k, n]))
    for copy in copies:
        copy.start()
    place_heads(lines, routes, col, lambda owner, rows: a_ref.at[owner, rows], sems_a)
    for copy in copies:
        copy.wait()
    per_col = w_ref.shape[0] // count
    farthest = far(col)
    total = None
    for k in range(1, count):
        owner = lax.rem(farthest + k, count)
        for n in range(per_col):
            term = jnp.dot(
                w_ref[owner * per_col + n, :width],
                a_ref[owner, n * depth : (n + 1) * depth],
                preferred_element_type=F32,
            )
            total = term if total is None else total + term
    sum_ref[...] = total
    for n in range(per_col):
        far_ref[:, n * depth : (n + 1) * depth] = w_ref[farthest * per_col + n, :width]

    patch = gain_ref.shape[0] // 3
    slab = width // per_col
    gains = jnp.zeros((patch, 1), F32)
    shifts = jnp.zeros((patch, 1), F32)
    for n in range(per_col):
        for k in range((w_ref.shape[1] - width) // patch):
            low, high = k * depth, min((k + 1) * depth, slab)
            if low >= high:
                continue
            piece = w_ref[col * per_col + n, width + k * patch : width + (k + 1) * patch]
            here = slice(n * slab + low, n * slab + high)
            linear = piece[:, : high - low].astype(F32)
            gained = linear * (1.0 + mod_ref[6:7, here])
            shifts += jnp.sum(linear * mod_ref[5:6, here], axis=1, keepdims=True)
            gains += jnp.sum(gained, axis=1, keepdims=True)
            for t in range(3):
                term = gained.astype(BF16)
                gain_ref[t * patch : (t + 1) * patch, here] = term
                gained = gained - term.astype(F32)
    lane = lax.broadcasted_iota(jnp.int32, const_ref.shape, 1)
    const_ref[...] = jnp.where(lane == 0, gains, jnp.where(lane == 1, shifts, 0.0))


def late_kernel(routes, mod_ref, x_ref, sum_ref, far_ref, gain_ref, const_ref, *refs):
    n_lines = len(routes)
    lines = [refs[n * n_lines : (n + 1) * n_lines] for n in range(2)]
    out_ref, a_ref, sems_a = refs[2 * n_lines :]
    width, tokens = x_ref.shape
    col = lax.axis_index("col")
    place_heads(lines, routes, col, lambda owner, rows: a_ref.at[rows], sems_a)
    gate = mod_ref[...].T[:width, 2:3]
    projected = sum_ref[...] + jnp.dot(far_ref[...], a_ref[...], preferred_element_type=F32)
    updated = (x_ref[...].astype(F32) + gate * projected).astype(BF16)
    wide = updated.astype(F32)
    sums = jnp.sum(wide, axis=0, keepdims=True)
    squares = jnp.sum(wide * wide, axis=0, keepdims=True)
    patch = const_ref.shape[0]
    terms = jnp.dot(gain_ref[...], updated, preferred_element_type=F32)
    out_ref[:patch, :tokens] = terms[:patch] + terms[patch : 2 * patch] + terms[2 * patch :]
    row = lax.broadcasted_iota(jnp.int32, (8, tokens), 0)
    out_ref[patch:, :tokens] = jnp.where(row == 0, sums, jnp.where(row == 1, squares, 0.0))
    out_ref[:patch, tokens:] = const_ref[...]
    out_ref[patch:, tokens:] = jnp.zeros((8, 128), F32)


def sigma_of(step_now):
    remain = 1.0 - step_now.astype(F32) / STEPS
    return 3.0 * remain / (1.0 + 2.0 * remain)


def per_device(
    hidden_img,
    hidden_txt,
    text_len,
    step_index,
    latent,
    cond,
    mod_weight,
    qkv_weight,
    kv_text_weight,
    q_gain,
    k_gain,
    out_weight,
    final_weight,
):
    row_count, col_count = lax.axis_size("row"), lax.axis_size("col")
    request = lax.axis_index("row") // 2
    requests = cond.shape[0]
    img, width = hidden_img.shape
    txt = hidden_txt.shape[0]
    head = q_gain.shape[0]
    part_cols = qkv_weight.shape[2]
    half = part_cols // 2
    full_width = width * col_count

    wide = -(-width // 128) * 128
    room = -(-txt // 128) * 128
    tokens = img + room
    mod_part = call(
        mod_kernel,
        jax.ShapeDtypeStruct((requests, 8, wide), F32),
        [VMEM, VMEM],
        [],
        cost(2),
    )(cond, jnp.moveaxis(mod_weight, 1, 0))
    mod_own = mod_part[0]
    for k in range(1, requests):
        mod_own = mod_own + swap(mod_part[k], "row", 2 * k)
    stats = call(
        stats_kernel,
        jax.ShapeDtypeStruct((8, tokens), F32),
        [VMEM, VMEM],
        [],
        cost(1),
    )(hidden_img.T, hidden_txt)
    stats = sum((swap(stats, "col", mask) for mask in range(1, col_count)), stats)

    chip_masks = [1 << bit for bit in range(1, row_count.bit_length() - 1)]
    packed = call(
        pack_kernel,
        (jax.ShapeDtypeStruct((qkv_weight.shape[0], 5 * half), BF16),) * 2,
        [VMEM, VMEM],
        [],
        cost(2),
        (VMEM, VMEM),
    )(jnp.moveaxis(qkv_weight, 1, 0), kv_text_weight)
    packed = packed[0], swap(packed[1], "row", 1)
    *packed, mod_own = tie(*packed, mod_own)
    mod_own = mod_own + swap(mod_own, "row", 1)
    ready = call(
        functools.partial(norm_kernel, full_width),
        jax.ShapeDtypeStruct((img + txt, width), BF16),
        [VMEM] * 4,
        [],
        cost(1),
    )(hidden_img.T, hidden_txt, stats, mod_own)
    routes = line_routes(col_count)
    small = col_count == 4 and row_count == 8
    if small:
        ready, *packed = tie(ready, *packed)
        line, peer_line, gathered = gather_both(ready, packed)
    else:
        line = line_gather(ready, "col")
        peer_line = [swap(part, "row", 1) for part in line]
        gathered = [doubling_gather(part, "row", chip_masks) for part in packed]

    if gathered[0][0].shape[0] % 16 == 0:
        masks = sorted(gathered[0])
        blocks = [piece[k] for piece in gathered for k in masks]
    else:
        masks, blocks = [], [in_order(gathered, "row")]
    gains = jnp.tile(jnp.concatenate([q_gain[None], k_gain], axis=0), (1, half // head))
    heads_out = jax.ShapeDtypeStruct((half, img), BF16)
    rest = [jax.ShapeDtypeStruct((rows, half), BF16) for rows in (img, *[2 * (img + txt)] * 2)]
    projected = call(
        functools.partial(project_kernel, routes, masks, img, head),
        (heads_out, *rest),
        [SMEM, VMEM] + [HBM] * (2 * len(routes) + len(blocks)),
        [
            pltpu.VMEM((col_count, 2 * (img + txt), width), BF16),
            pltpu.VMEM((col_count, width, 5 * half), BF16),
            pltpu.VMEM((2 * img, 3 * half), F32),
            pltpu.VMEM((2 * txt, 2 * half), F32),
            pltpu.SemaphoreType.DMA((2, 2, len(routes))),
            pltpu.SemaphoreType.DMA((2, max(len(masks), 1))),
        ],
        cost(PROJECT),
        (VMEM,) * 4,
        vmem=56,
    )(text_len, gains, *line, *peer_line, *blocks)
    head_depth, patch = final_weight.shape
    depth = out_weight.shape[0]
    folds = -(-head_depth // depth)
    tail = jnp.pad(final_weight.T, ((0, 0), (0, folds * depth - head_depth)))
    tail = jnp.swapaxes(tail.reshape(patch, folds, depth), 0, 1).reshape(folds * patch, depth)
    out_packed = jnp.concatenate([out_weight.T, tail], axis=0)
    masks = list(range(0, row_count, 2))
    out_blocks = direct_gather(out_packed, "row", masks)

    own_heads, *rest = projected
    others = [out_blocks[k] for k in masks[1:]]
    *rest, = tie(*rest, *others)
    rest, others = rest[:3], rest[3:]
    give = call(
        functools.partial(attend_kernel, img, txt, head),
        heads_out,
        [SMEM, HBM, HBM, HBM],
        [pltpu.VMEM(part.shape, BF16) for part in rest] + [pltpu.SemaphoreType.DMA((3,))],
        cost(ATTEND),
        vmem=24,
    )(text_len, *rest)
    attended = [own_heads, swap(give, "row", 1)]
    lines = [(line_four if small else line_gather)(block, "col") for block in attended]
    own_rows = jnp.concatenate([out_packed, *others], axis=0)
    other_rows = swap(own_rows, "row", 1)
    early, late, far = far_routes(col_count)
    sems = pltpu.SemaphoreType.DMA((2, len(routes)))
    bundle = call(
        functools.partial(early_kernel, [route for _, route in early], far, masks),
        (
            jax.ShapeDtypeStruct((width, img), F32),
            jax.ShapeDtypeStruct((width, part_cols), BF16),
            jax.ShapeDtypeStruct((3 * patch, width), BF16),
            jax.ShapeDtypeStruct((patch, 128), F32),
        ),
        [VMEM] + [HBM] * (2 * len(early) + 2),
        [
            pltpu.VMEM((col_count, part_cols, img), BF16),
            pltpu.VMEM((row_count,) + out_packed.shape, BF16),
            sems,
            pltpu.SemaphoreType.DMA((2, len(masks))),
        ],
        cost(5),
        (VMEM,) * 4,
        vmem=EARLY,
    )(
        mod_own,
        *[line[k] for line in lines for k, _ in early],
        own_rows,
        other_rows,
    )
    partial_sum = call(
        functools.partial(late_kernel, [route for _, route in late]),
        jax.ShapeDtypeStruct((patch + 8, img + 128), F32),
        [VMEM] * 6 + [HBM] * (2 * len(late)),
        [pltpu.VMEM((part_cols, img), BF16), sems],
        cost(3),
        vmem=24,
    )(mod_own, hidden_img.T, *bundle, *[line[k] for line in lines for k, _ in late])
    mask = 1
    while mask < col_count:
        partial_sum = partial_sum + swap(partial_sum, "col", mask)
        mask *= 2
    average = partial_sum[patch : patch + 1, :img] / full_width
    mean_square = partial_sum[patch + 1 : patch + 2, :img] / full_width
    inverse = lax.rsqrt(mean_square - average * average + EPS_NORM)
    gains = partial_sum[:patch, img : img + 1]
    shifts = partial_sum[:patch, img + 1 : img + 2]
    velocity = inverse * (partial_sum[:patch, :img] - average * gains) + shifts
    step_now = lax.dynamic_index_in_dim(step_index, request, 0, keepdims=False)
    sigma_step = sigma_of(step_now + 1) - sigma_of(step_now)
    latent_next = latent.T + sigma_step * velocity
    return (velocity.T, latent_next.T)


def solution(mesh):
    in_specs = (
        P("row", "col"),
        P("row", "col"),
        P(),
        P(),
        P("row", None),
        P(None, "row"),
        P("row", None, "col"),
        P("row", None, "col"),
        P("row", None, "col"),
        P(),
        P(),
        P("row", "col"),
        P("row", None),
    )
    out_specs = (P("row", None), P("row", None))
    return jax.shard_map(
        per_device, mesh=mesh, in_specs=in_specs, out_specs=out_specs, check_vma=False
    )
```

```python
import functools

import jax
import jax.numpy as jnp
from jax import lax
from jax.experimental import pallas as pl
from jax.experimental.pallas import tpu as pltpu
from jax.sharding import PartitionSpec as P

STEPS = 28
EPS_NORM = 1e-06
ATTEND = 6
ATTEND_MIB = 56
PROJECT = 20
EARLY = 48
F32 = jnp.float32
BF16 = jnp.bfloat16
HBM = pl.BlockSpec(memory_space=pltpu.HBM)
VMEM = pl.BlockSpec(memory_space=pltpu.VMEM)
SMEM = pl.BlockSpec(memory_space=pltpu.SMEM)


def swap(block, axis, mask):
    count = lax.axis_size(axis)
    return lax.ppermute(block, axis, [(i, i ^ mask) for i in range(count)])


def shift(block, axis, step):
    count = lax.axis_size(axis)
    route = [(i, i + step) for i in range(count) if 0 <= i + step < count]
    return lax.ppermute(block, axis, route)


def tie(*arrays):
    return lax.optimization_barrier(arrays)


def line_gather(block, axis):
    held = {0: block}
    for step in range(1, lax.axis_size(axis)):
        held[-step] = shift(held[1 - step], axis, 1)
        held[step] = shift(held[step - 1], axis, -1)
    return [held[k] for k in sorted(held)]


def line_routes(count):
    if count == 4:
        near = lambda p: jnp.where(p < 2, 2, 1)
        far = lambda p: jnp.where(p < 2, 3, 0)
        inner = lambda p: (p == 1) | (p == 2)
        outer = lambda p: (p == 0) | (p == 3)
        always = lambda p: p >= 0
        return [
            (lambda p: p, always),
            (lambda p: jnp.bitwise_xor(p, 1), always),
            (near, inner),
            (near, outer),
            (far, inner),
            (far, outer),
        ]
    result = []
    for offset in range(1 - count, count):
        inside = lambda p, offset=offset: (p + offset >= 0) & (p + offset < count)
        result.append((lambda p, offset=offset: p + offset, inside))
    return result


def far_routes(count):
    routes = list(enumerate(line_routes(count)))
    if count == 4:
        return routes[:4], routes[4:], routes[4][1][0]
    far = lambda p: count - 1 - p
    early, late = [], []
    for n, (owner, held) in routes:
        is_far = lambda p, owner=owner: owner(p) == far(p)
        early.append((n, (owner, lambda p, held=held, is_far=is_far: held(p) & ~is_far(p))))
        late.append((n, (owner, lambda p, held=held, is_far=is_far: held(p) & is_far(p))))
    return early, late, far


MIDDLE = [(1, 2), (2, 1)]
OUTWARD = [(1, 0), (2, 3)]


def gather_heads(keep, give, others):
    send = lambda held, route: lax.ppermute(held, "col", route)
    pair, near = swap(keep, "col", 1), send(keep, MIDDLE)
    pair, near, give = tie(pair, near, give)
    near_end, far = send(near, OUTWARD), send(pair, MIDDLE)
    take = swap(give, "row", 1)
    take_pair, take_near = swap(take, "col", 1), send(take, MIDDLE)
    near_end, far, take_pair, take_near = tie(near_end, far, take_pair, take_near)
    far_end = send(far, OUTWARD)
    take_end, take_far = send(take_near, OUTWARD), send(take_pair, MIDDLE)
    far_end, take_end, take_far, *others = tie(far_end, take_end, take_far, *others)
    first = [keep, pair, near, near_end, far, far_end]
    second = [take, take_pair, take_near, take_end, take_far, send(take_far, OUTWARD)]
    return [first, second], others


def gather_both(tokens, weights):
    send = lambda held, route: lax.ppermute(held, "col", route)
    first, second = weights
    pair, near = swap(tokens, "col", 1), send(tokens, MIDDLE)
    first_y, second_x = swap(first, "row", 4), swap(second, "row", 2)
    other = lambda held: swap(held, "row", 1)
    peer = other(tokens)
    pair, near, first_y, second_x, first, second = tie(
        pair, near, first_y, second_x, first, second
    )
    near_end, far = send(near, OUTWARD), send(pair, MIDDLE)
    first_x, second_y = swap(first, "row", 2), swap(second, "row", 4)
    near_end, far, first_x, second_y, first_y, second_x, pair, near, peer = tie(
        near_end, far, first_x, second_y, first_y, second_x, pair, near, peer
    )
    far_end = send(far, OUTWARD)
    first_d, second_d = swap(first_y, "row", 2), swap(second_x, "row", 4)
    far_end, first_d, second_d = tie(far_end, first_d, second_d)
    peers = [peer, other(pair), other(near), other(near_end), other(far), other(far_end)]
    held = [
        {0: first, 4: first_y, 2: first_x, 6: first_d},
        {0: second, 2: second_x, 4: second_y, 6: second_d},
    ]
    return [tokens, pair, near, near_end, far, far_end], peers, held


def direct_gather(block, axis, masks):
    return {mask: swap(block, axis, mask) if mask else block for mask in masks}


def doubling_gather(block, axis, masks):
    held = {0: block}
    for mask in masks:
        for known in list(held):
            held[known | mask] = swap(held[known], axis, mask)
    return held


def in_order(pieces, axis):
    masks, place = sorted(pieces[0]), lax.axis_index(axis)
    core = place % 2
    joined = jnp.stack([jnp.stack([piece[k] for k in masks]) for piece in pieces], axis=1)
    joined = joined[jnp.bitwise_xor(jnp.arange(len(masks)), place // 2)]
    joined = jnp.where(core == 0, joined, joined[:, ::-1])
    return joined.reshape(joined.shape[0], -1, joined.shape[-1])


def cost(us):
    return pl.CostEstimate(flops=int(us * 1.15e9), bytes_accessed=0, transcendentals=0)


def call(kernel, outs, in_specs, scratch, estimate, out_specs=None, vmem=16):
    if out_specs is None:
        out_specs = jax.tree.map(lambda _: VMEM, outs)
    return pl.pallas_call(
        kernel,
        out_shape=outs,
        in_specs=in_specs,
        out_specs=out_specs,
        scratch_shapes=scratch,
        cost_estimate=estimate,
        compiler_params=pltpu.CompilerParams(vmem_limit_bytes=vmem * 1024 * 1024),
    )


def line_copies(refs, routes, place, target, sems, act):
    for n, (ref, (owner, held)) in enumerate(zip(refs, routes)):

        @pl.when(held(place))
        def _():
            copy = pltpu.make_async_copy(ref, target(owner(place)), sems.at[n])
            getattr(copy, act)()


def mod_kernel(cond_ref, w_ref, out_ref):
    requests, groups, width = cond_ref.shape[0], w_ref.shape[0], w_ref.shape[2]
    request = lax.axis_index("row") // 2
    values = jnp.concatenate(
        [cond_ref[pl.ds(jnp.bitwise_xor(request, k), 1), :] for k in range(requests)], axis=0
    )
    activated = (values * (1.0 / (1.0 + jnp.exp(-values)))).astype(BF16)
    out_ref[...] = jnp.zeros(out_ref.shape, F32)
    for group in range(groups):
        out_ref[:, group, :width] = jnp.dot(
            activated, w_ref[group], preferred_element_type=F32
        )


def pack_kernel(qkv_ref, kv_ref, keep_ref, give_ref):
    half = keep_ref.shape[1] // 5
    first = lax.axis_index("row") % 2 == 0
    for k in range(5):
        rows = qkv_ref[k] if k < 3 else kv_ref[:, k - 3]
        low, high = rows[:, :half], rows[:, half:]
        here = slice(k * half, (k + 1) * half)
        keep_ref[:, here] = jnp.where(first, low, high)
        give_ref[:, here] = jnp.where(first, high, low)


def stats_kernel(img_ref, txt_ref, out_ref):
    img = img_ref.shape[1]
    txt = txt_ref.shape[0]
    out_ref[...] = jnp.zeros(out_ref.shape, F32)
    for values, low, high in (
        (img_ref[...].astype(F32), 0, img),
        (txt_ref[...].astype(F32).T, img, img + txt),
    ):
        out_ref[0:1, low:high] = jnp.sum(values, axis=0, keepdims=True)
        out_ref[1:2, low:high] = jnp.sum(values * values, axis=0, keepdims=True)


def norm_kernel(total, img_ref, txt_ref, stats_ref, mod_ref, out_ref):
    width, img = img_ref.shape
    txt = txt_ref.shape[0]
    stats = stats_ref[...] / total
    row = lax.broadcasted_iota(jnp.int32, stats.shape, 0)
    average = stats[0:1]
    inverse = lax.rsqrt(stats[1:2] - average * average + EPS_NORM)
    columns = jnp.where(row == 0, average, inverse).T
    chunk = 128
    if out_ref.shape[1] > width:
        out_ref[:, width:] = jnp.zeros((img + txt, out_ref.shape[1] - width), BF16)
    for low in range(0, img + txt, chunk):
        for start in range(0, width, chunk):
            stop = min(start + chunk, width)
            if low < img:
                high = min(low + chunk, img)
                values, group = img_ref[start:stop, low:high].T, 0
            else:
                high = min(low + chunk, img + txt)
                values, group = txt_ref[low - img : high - img, start:stop], 3
            normed = (values.astype(F32) - columns[low:high, 0:1]) * columns[low:high, 1:2]
            stretch = 1.0 + mod_ref[group + 1 : group + 2, start:stop]
            normed = normed * stretch + mod_ref[group : group + 1, start:stop]
            out_ref[low:high, start:stop] = normed.astype(BF16)


def attend(img, txt, head, length_ref, queries, keys, values, out_ref):
    width = queries.shape[1]
    place = lax.axis_index("row")
    side = lax.rem(place, 2)
    slot = lax.broadcasted_iota(jnp.int32, (2 * txt, 1), 0)
    other = (slot >= txt).astype(jnp.int32)
    owner = jnp.where(other == 1, 1 - side, side)
    allowed = owner * txt + slot - other * txt < length_ref[place // 2]
    turned = values.T
    ones = jnp.ones((16, keys.shape[0]), BF16)
    rows = [
        jnp.concatenate([turned[k * head : (k + 1) * head], ones], axis=0)
        for k in range(width // head)
    ]
    lane = lax.broadcasted_iota(jnp.int32, (1, width), 1) // head
    step = 256 if img % 256 == 0 else img

    def scores_of(k, low):
        query = jnp.where(lane == k, queries[low : low + step], 0.0).astype(BF16)
        score = lax.dot_general(
            keys, query, (((1,), (1,)), ((), ())), preferred_element_type=F32
        )
        tail = jnp.where(allowed, score[2 * img :], -1e30)
        return jnp.concatenate([score[: 2 * img], tail], axis=0)

    work = [(k, low) for k in range(width // head) for low in range(0, img, step)]
    ahead = scores_of(*work[0])
    for n, (k, low) in enumerate(work):
        scores = ahead
        if n + 1 < len(work):
            ahead = scores_of(*work[n + 1])
        weights = jnp.exp(scores - jnp.max(scores, axis=0, keepdims=True)).astype(BF16)
        mixed = jnp.dot(rows[k], weights, preferred_element_type=F32)
        out_ref[k * head : (k + 1) * head, low : low + step] = (
            mixed[:head] / mixed[head : head + 1]
        ).astype(BF16)


def attend_kernel(img, txt, head, length_ref, q_ref, k_ref, v_ref, out_ref, *scratch):
    parts, sems = scratch[:-1], scratch[-1]
    copies = [
        pltpu.make_async_copy(ref, part, sems.at[n])
        for n, (ref, part) in enumerate(zip((q_ref, k_ref, v_ref), parts))
    ]
    for copy in copies:
        copy.start()
    for copy in copies:
        copy.wait()
    attend(img, txt, head, length_ref, *[part[...] for part in parts], out_ref)


def project_kernel(routes, masks, img, head, length_ref, q_gain_ref, k_gain_ref, *refs):
    lines = refs[: len(routes)], refs[len(routes) : 2 * len(routes)]
    refs = refs[2 * len(routes) :]
    n_blocks = 2 * len(masks) if masks else 1
    blocks, refs = refs[:n_blocks], refs[n_blocks:]
    outs, refs = refs[:4], refs[4:]
    x_ref, w_ref, img_ref, txt_ref, q_ref, k_ref, v_ref, sems_x, sems_w, sems_o = refs
    tokens, wide = lines[0][0].shape
    txt = tokens - img
    count = x_ref.shape[1] // wide
    half = img_ref.shape[1] // 3
    place, col = lax.axis_index("row"), lax.axis_index("col")
    chip, core = place // 2, lax.rem(place, 2)

    def copy_line(n, act):
        for k, (low, high, to) in enumerate(
            ((0, img, n * img), (img, tokens, 2 * img + n * txt))
        ):
            parts = [ref.at[pl.ds(low, high - low)] for ref in lines[n]]
            target = lambda owner: x_ref.at[
                pl.ds(to, high - low), pl.ds(pl.multiple_of(owner * wide, 128), wide)
            ]
            line_copies(parts, routes, col, target, sems_x.at[n, k], act)

    copy_line(0, "start")
    stages = [[], []]
    if not masks:
        width = blocks[0].shape[1]
        for k in range(count):
            target = w_ref.at[pl.ds(k * wide, width)]
            stages[0].append(pltpu.make_async_copy(blocks[0].at[k], target, sems_w.at[0, k]))
    else:
        depth = blocks[0].shape[0]
        width = 2 * depth
        for k in range(count):
            for piece in range(2):
                row = jnp.bitwise_xor(chip, k) * wide + jnp.where(core == piece, 0, depth)
                target = w_ref.at[pl.ds(pl.multiple_of(row, 16), depth)]
                ref = blocks[piece * len(masks) + k]
                copy = pltpu.make_async_copy(ref, target, sems_w.at[piece, k])
                stages[2 * k // count].append(copy)
    for copy in stages[0]:
        copy.start()
    for k in range(count):
        if wide > width:
            w_ref[k * wide + width : (k + 1) * wide] = jnp.zeros((wide - width, 5 * half), BF16)
    row = lax.broadcasted_iota(jnp.int32, (half, half), 0) // head
    column = lax.broadcasted_iota(jnp.int32, (half, half), 1) // head
    mean_of = jnp.where(row == column, 1.0 / head, 0.0).astype(BF16)

    def head_norm(values, gain):
        square = values * values
        mean_square = jnp.zeros_like(square)
        for _ in range(2):
            term = square.astype(BF16)
            mean_square += jnp.dot(term, mean_of, preferred_element_type=F32)
            square = square - term.astype(F32)
        return (values * lax.rsqrt(mean_square + EPS_NORM) * gain).astype(BF16)

    copy_line(0, "wait")
    depth = count // 2 * wide
    for k in range(2):
        for copy in stages[k]:
            copy.wait()
        if k == 0:
            for copy in stages[1]:
                copy.start()
        else:
            copy_line(1, "start")
        if not masks:
            here = pl.ds(k * depth, depth)
        else:
            here = pl.ds(pl.multiple_of(jnp.bitwise_xor(2 * chip // count, k) * depth, 128), depth)
        term = jnp.dot(x_ref[:img, here], w_ref[here, : 3 * half], preferred_element_type=F32)
        img_ref[:img] = term if k == 0 else img_ref[:img] + term
    copy_line(1, "wait")
    img_ref[img:] = jnp.dot(
        x_ref[img : 2 * img], w_ref[:, : 3 * half], preferred_element_type=F32
    )
    txt_ref[...] = jnp.dot(x_ref[2 * img :], w_ref[:, 3 * half :], preferred_element_type=F32)
    scaling = head ** (-0.5)
    wide_gain = lambda gain: jnp.concatenate([gain] * (half // head), axis=1)
    queries = head_norm(img_ref[:, :half], wide_gain(q_gain_ref[...]))
    q_ref[...] = (queries.astype(F32) * scaling).astype(BF16)
    k_ref[: 2 * img] = head_norm(img_ref[:, half : 2 * half], wide_gain(k_gain_ref[0:1]))
    k_ref[2 * img :] = head_norm(txt_ref[:, :half], wide_gain(k_gain_ref[1:2]))
    v_ref[: 2 * img] = img_ref[:, 2 * half :].astype(BF16)
    v_ref[2 * img :] = txt_ref[:, half:].astype(BF16)
    copies = [
        pltpu.make_async_copy(part, ref, sems_o.at[n])
        for n, (part, ref) in enumerate(zip((q_ref.at[pl.ds(img, img)], k_ref, v_ref), outs[1:]))
    ]
    for copy in copies:
        copy.start()
    attend(img, txt, head, length_ref, q_ref[:img], k_ref[...], v_ref[...], outs[0])
    for copy in copies:
        copy.wait()


def place_heads(lines, routes, col, target, sems):
    core = lax.rem(lax.axis_index("row"), 2)
    size = lines[0][0].shape[0]
    for act in ("start", "wait"):
        for n, line in enumerate(lines):
            rows = pl.ds(pl.multiple_of(jnp.where(core == n, 0, size), 16), size)
            line_copies(line, routes, col, lambda owner: target(owner, rows), sems.at[n], act)


def early_kernel(routes, far, masks, mod_ref, *refs):
    n_lines = len(routes)
    lines = [refs[n * n_lines : (n + 1) * n_lines] for n in range(2)]
    refs = refs[2 * n_lines :]
    weights, refs = refs[:2], refs[2:]
    sum_ref, far_ref, gain_ref, const_ref, a_ref, w_ref, sems_a, sems_w = refs
    width = sum_ref.shape[0]
    count = a_ref.shape[0]
    depth = w_ref.shape[2]
    place, col = lax.axis_index("row"), lax.axis_index("col")
    copies = []
    for k, ref in enumerate(weights):
        for n, mask in enumerate(masks):
            target = w_ref.at[jnp.bitwise_xor(place, mask + k)]
            source = ref.at[pl.ds(n * w_ref.shape[1], w_ref.shape[1])]
            copies.append(pltpu.make_async_copy(source, target, sems_w.at[k, n]))
    for copy in copies:
        copy.start()
    place_heads(lines, routes, col, lambda owner, rows: a_ref.at[owner, rows], sems_a)
    for copy in copies:
        copy.wait()
    per_col = w_ref.shape[0] // count
    farthest = far(col)
    total = None
    for k in range(1, count):
        owner = lax.rem(farthest + k, count)
        for n in range(per_col):
            term = jnp.dot(
                w_ref[owner * per_col + n, :width],
                a_ref[owner, n * depth : (n + 1) * depth],
                preferred_element_type=F32,
            )
            total = term if total is None else total + term
    sum_ref[...] = total
    for n in range(per_col):
        far_ref[:, n * depth : (n + 1) * depth] = w_ref[farthest * per_col + n, :width]

    patch = gain_ref.shape[0] // 3
    slab = width // per_col
    consts = jnp.zeros((8, patch), F32)
    row = lax.broadcasted_iota(jnp.int32, (8, patch), 0)
    for n in range(per_col):
        for k in range((w_ref.shape[1] - width) // patch):
            low, high = k * depth, min((k + 1) * depth, slab)
            if low >= high:
                continue
            piece = w_ref[col * per_col + n, width + k * patch : width + (k + 1) * patch]
            here = slice(n * slab + low, n * slab + high)
            linear = piece[:, : high - low].astype(F32)
            gained = linear * (1.0 + mod_ref[6:7, here])
            both = (jnp.sum(gained, axis=1, keepdims=True), linear * mod_ref[5:6, here])
            both = jnp.concatenate(
                [jnp.broadcast_to(both[0], (patch, 128)), jnp.broadcast_to(
                    jnp.sum(both[1], axis=1, keepdims=True), (patch, 128))], axis=0
            ).T
            consts += jnp.where(
                row == 2, both[:8, :patch], jnp.where(row == 3, both[:8, patch:], 0.0)
            )
            for t in range(3):
                term = gained.astype(BF16)
                gain_ref[t * patch : (t + 1) * patch, here] = term
                gained = gained - term.astype(F32)
    const_ref[...] = jnp.zeros(const_ref.shape, F32)
    const_ref[:, :patch] = consts


def late_kernel(routes, mod_ref, x_ref, sum_ref, far_ref, gain_ref, const_ref, *refs):
    n_lines = len(routes)
    lines = [refs[n * n_lines : (n + 1) * n_lines] for n in range(2)]
    out_ref, a_ref, sems_a = refs[2 * n_lines :]
    width, tokens = x_ref.shape
    col = lax.axis_index("col")
    place_heads(lines, routes, col, lambda owner, rows: a_ref.at[rows], sems_a)
    gate = mod_ref[...].T[:width, 2:3]
    projected = sum_ref[...] + jnp.dot(far_ref[...], a_ref[...], preferred_element_type=F32)
    updated = (x_ref[...].astype(F32) + gate * projected).astype(BF16)
    wide = updated.astype(F32)
    sums = jnp.sum(wide, axis=0, keepdims=True)
    squares = jnp.sum(wide * wide, axis=0, keepdims=True)
    patch = gain_ref.shape[0] // 3
    terms = jnp.dot(gain_ref[...], updated, preferred_element_type=F32)
    out_ref[:patch] = terms[:patch] + terms[patch : 2 * patch] + terms[2 * patch :]
    row = lax.broadcasted_iota(jnp.int32, (8, tokens), 0)
    out_ref[patch:] = jnp.where(row == 0, sums, jnp.where(row == 1, squares, const_ref[...]))


def sigma_of(step_now):
    remain = 1.0 - step_now.astype(F32) / STEPS
    return 3.0 * remain / (1.0 + 2.0 * remain)


def per_device(
    hidden_img,
    hidden_txt,
    text_len,
    step_index,
    latent,
    cond,
    mod_weight,
    qkv_weight,
    kv_text_weight,
    q_gain,
    k_gain,
    out_weight,
    final_weight,
):
    row_count, col_count = lax.axis_size("row"), lax.axis_size("col")
    request = lax.axis_index("row") // 2
    requests = cond.shape[0]
    img, width = hidden_img.shape
    txt = hidden_txt.shape[0]
    head = q_gain.shape[0]
    part_cols = qkv_weight.shape[2]
    half = part_cols // 2
    full_width = width * col_count

    wide = -(-width // 128) * 128
    room = -(-txt // 128) * 128
    tokens = img + room
    mod_part = call(
        mod_kernel,
        jax.ShapeDtypeStruct((requests, 8, wide), F32),
        [VMEM, VMEM],
        [],
        cost(2),
    )(cond, jnp.moveaxis(mod_weight, 1, 0))
    mod_own = mod_part[0]
    for k in range(1, requests):
        mod_own = mod_own + swap(mod_part[k], "row", 2 * k)
    stats = call(
        stats_kernel,
        jax.ShapeDtypeStruct((8, tokens), F32),
        [VMEM, VMEM],
        [],
        cost(1),
    )(hidden_img.T, hidden_txt)
    stats = sum((swap(stats, "col", mask) for mask in range(1, col_count)), stats)

    chip_masks = [1 << bit for bit in range(1, row_count.bit_length() - 1)]
    packed = call(
        pack_kernel,
        (jax.ShapeDtypeStruct((qkv_weight.shape[0], 5 * half), BF16),) * 2,
        [VMEM, VMEM],
        [],
        cost(2),
        (VMEM, VMEM),
    )(jnp.moveaxis(qkv_weight, 1, 0), kv_text_weight)
    packed = packed[0], swap(packed[1], "row", 1)
    *packed, mod_own = tie(*packed, mod_own)
    mod_own = mod_own + swap(mod_own, "row", 1)
    ready = call(
        functools.partial(norm_kernel, full_width),
        jax.ShapeDtypeStruct((img + txt, wide), BF16),
        [VMEM] * 4,
        [],
        cost(1),
    )(hidden_img.T, hidden_txt, stats, mod_own)
    routes = line_routes(col_count)
    small = col_count == 4 and row_count == 8
    if small:
        ready, *packed = tie(ready, *packed)
        line, peer_line, gathered = gather_both(ready, packed)
    else:
        line = line_gather(ready, "col")
        peer_line = [swap(part, "row", 1) for part in line]
        gathered = [doubling_gather(part, "row", chip_masks) for part in packed]

    if gathered[0][0].shape[0] % 16 == 0:
        masks = sorted(gathered[0])
        blocks = [piece[k] for piece in gathered for k in masks]
    else:
        masks, blocks = [], [in_order(gathered, "row")]
    heads_out = jax.ShapeDtypeStruct((half, img), BF16)
    full_wide = col_count * wide
    rest = [jax.ShapeDtypeStruct((rows, half), BF16) for rows in (img, *[2 * (img + txt)] * 2)]
    projected = call(
        functools.partial(project_kernel, routes, masks, img, head),
        (heads_out, *rest),
        [SMEM, VMEM, VMEM] + [HBM] * (2 * len(routes) + len(blocks)),
        [
            pltpu.VMEM((2 * (img + txt), full_wide), BF16),
            pltpu.VMEM((full_wide, 5 * half), BF16),
            pltpu.VMEM((2 * img, 3 * half), F32),
            pltpu.VMEM((2 * txt, 2 * half), F32),
            pltpu.VMEM((2 * img, half), BF16),
            *[pltpu.VMEM((2 * (img + txt), half), BF16)] * 2,
            pltpu.SemaphoreType.DMA((2, 2, len(routes))),
            pltpu.SemaphoreType.DMA((2, col_count)),
            pltpu.SemaphoreType.DMA((3,)),
        ],
        cost(PROJECT),
        (VMEM, HBM, HBM, HBM),
        vmem=56,
    )(text_len, q_gain[None], k_gain, *line, *peer_line, *blocks)
    head_depth, patch = final_weight.shape
    depth = out_weight.shape[0]
    folds = -(-head_depth // depth)
    tail = jnp.pad(final_weight.T, ((0, 0), (0, folds * depth - head_depth)))
    tail = jnp.swapaxes(tail.reshape(patch, folds, depth), 0, 1).reshape(folds * patch, depth)
    out_packed = jnp.concatenate([out_weight.T, tail], axis=0)
    masks = list(range(0, row_count, 2))
    out_blocks = direct_gather(out_packed, "row", masks)

    own_heads, *rest = projected
    give = call(
        functools.partial(attend_kernel, img, txt, head),
        heads_out,
        [SMEM, HBM, HBM, HBM],
        [pltpu.VMEM(part.shape, BF16) for part in rest] + [pltpu.SemaphoreType.DMA((3,))],
        cost(ATTEND),
        vmem=ATTEND_MIB,
    )(text_len, *rest)
    others = [out_blocks[k] for k in masks[1:]]
    if small:
        lines, others = gather_heads(own_heads, give, others)
    else:
        lines = [line_gather(block, "col") for block in (own_heads, swap(give, "row", 1))]
    own_rows = jnp.concatenate([out_packed, *others], axis=0)
    other_rows = swap(own_rows, "row", 1)
    early, late, far = far_routes(col_count)
    sems = pltpu.SemaphoreType.DMA((2, len(routes)))
    bundle = call(
        functools.partial(early_kernel, [route for _, route in early], far, masks),
        (
            jax.ShapeDtypeStruct((width, img), F32),
            jax.ShapeDtypeStruct((width, part_cols), BF16),
            jax.ShapeDtypeStruct((3 * patch, width), BF16),
            jax.ShapeDtypeStruct((8, img), F32),
        ),
        [VMEM] + [HBM] * (2 * len(early) + 2),
        [
            pltpu.VMEM((col_count, part_cols, img), BF16),
            pltpu.VMEM((row_count,) + out_packed.shape, BF16),
            sems,
            pltpu.SemaphoreType.DMA((2, len(masks))),
        ],
        cost(5),
        (VMEM,) * 4,
        vmem=EARLY,
    )(
        mod_own,
        *[line[k] for line in lines for k, _ in early],
        own_rows,
        other_rows,
    )
    partial_sum = call(
        functools.partial(late_kernel, [route for _, route in late]),
        jax.ShapeDtypeStruct((patch + 8, img), F32),
        [VMEM] * 6 + [HBM] * (2 * len(late)),
        [pltpu.VMEM((part_cols, img), BF16), sems],
        cost(3),
        vmem=24,
    )(mod_own, hidden_img.T, *bundle, *[line[k] for line in lines for k, _ in late])
    mask = 1
    while mask < col_count:
        partial_sum = partial_sum + swap(partial_sum, "col", mask)
        mask *= 2
    average = partial_sum[patch : patch + 1] / full_width
    mean_square = partial_sum[patch + 1 : patch + 2] / full_width
    inverse = lax.rsqrt(mean_square - average * average + EPS_NORM)
    gains = partial_sum[patch + 2, :patch][:, None]
    shifts = partial_sum[patch + 3, :patch][:, None]
    velocity = inverse * (partial_sum[:patch] - average * gains) + shifts
    step_now = lax.dynamic_index_in_dim(step_index, request, 0, keepdims=False)
    sigma_step = sigma_of(step_now + 1) - sigma_of(step_now)
    latent_next = latent.T + sigma_step * velocity
    return (velocity.T, latent_next.T)


def solution(mesh):
    in_specs = (
        P("row", "col"),
        P("row", "col"),
        P(),
        P(),
        P("row", None),
        P(None, "row"),
        P("row", None, "col"),
        P("row", None, "col"),
        P("row", None, "col"),
        P(),
        P(),
        P("row", "col"),
        P("row", None),
    )
    out_specs = (P("row", None), P("row", None))
    return jax.shard_map(
        per_device, mesh=mesh, in_specs=in_specs, out_specs=out_specs, check_vma=False
    )
```

```python
import functools

import jax
import jax.numpy as jnp
from jax import lax
from jax.experimental import pallas as pl
from jax.experimental.pallas import tpu as pltpu
from jax.sharding import PartitionSpec as P

STEPS = 28
EPS_NORM = 1e-06
PROJECT_MIB = 44
PROJECT = 20
EARLY = 48
F32 = jnp.float32
BF16 = jnp.bfloat16
HBM = pl.BlockSpec(memory_space=pltpu.HBM)
VMEM = pl.BlockSpec(memory_space=pltpu.VMEM)
SMEM = pl.BlockSpec(memory_space=pltpu.SMEM)


def swap(block, axis, mask):
    count = lax.axis_size(axis)
    return lax.ppermute(block, axis, [(i, i ^ mask) for i in range(count)])


def shift(block, axis, step):
    count = lax.axis_size(axis)
    route = [(i, i + step) for i in range(count) if 0 <= i + step < count]
    return lax.ppermute(block, axis, route)


def tie(*arrays):
    return lax.optimization_barrier(arrays)


def line_gather(block, axis):
    held = {0: block}
    for step in range(1, lax.axis_size(axis)):
        held[-step] = shift(held[1 - step], axis, 1)
        held[step] = shift(held[step - 1], axis, -1)
    return [held[k] for k in sorted(held)]


def line_routes(count):
    if count == 4:
        near = lambda p: jnp.where(p < 2, 2, 1)
        far = lambda p: jnp.where(p < 2, 3, 0)
        inner = lambda p: (p == 1) | (p == 2)
        outer = lambda p: (p == 0) | (p == 3)
        always = lambda p: p >= 0
        return [
            (lambda p: p, always),
            (lambda p: jnp.bitwise_xor(p, 1), always),
            (near, inner),
            (near, outer),
            (far, inner),
            (far, outer),
        ]
    result = []
    for offset in range(1 - count, count):
        inside = lambda p, offset=offset: (p + offset >= 0) & (p + offset < count)
        result.append((lambda p, offset=offset: p + offset, inside))
    return result


def far_routes(count):
    routes = list(enumerate(line_routes(count)))
    if count == 4:
        return routes[:4], routes[4:], routes[4][1][0]
    far = lambda p: count - 1 - p
    early, late = [], []
    for n, (owner, held) in routes:
        is_far = lambda p, owner=owner: owner(p) == far(p)
        early.append((n, (owner, lambda p, held=held, is_far=is_far: held(p) & ~is_far(p))))
        late.append((n, (owner, lambda p, held=held, is_far=is_far: held(p) & is_far(p))))
    return early, late, far


MIDDLE = [(1, 2), (2, 1)]
OUTWARD = [(1, 0), (2, 3)]


def gather_heads(keep, take, others):
    send = lambda held, route: lax.ppermute(held, "col", route)
    join = lambda *held: jnp.concatenate(held, axis=0)
    keep_pair, keep_near = swap(keep, "col", 1), send(keep, MIDDLE)
    take_pair, take_near = swap(take, "col", 1), send(take, MIDDLE)
    keep_pair, keep_near, take_pair, take_near, others = tie(
        keep_pair, keep_near, take_pair, take_near, others
    )
    pair, near = join(keep_pair, take_pair), join(keep_near, take_near)
    near_end, far = send(near, OUTWARD), send(pair, MIDDLE)
    near_end, far = tie(near_end, far)
    return [join(keep, take), pair, near, near_end, far, send(far, OUTWARD)], others


def gather_both(tokens, weights):
    send = lambda held, route: lax.ppermute(held, "col", route)
    first, second = weights
    pair, near = swap(tokens, "col", 1), send(tokens, MIDDLE)
    first_y, second_x = swap(first, "row", 4), swap(second, "row", 2)
    other = lambda held: swap(held, "row", 1)
    peer = other(tokens)
    pair, near, first_y, second_x, first, second = tie(
        pair, near, first_y, second_x, first, second
    )
    near_end, far = send(near, OUTWARD), send(pair, MIDDLE)
    first_x, second_y = swap(first, "row", 2), swap(second, "row", 4)
    near_end, far, first_x, second_y, first_y, second_x, pair, near, peer = tie(
        near_end, far, first_x, second_y, first_y, second_x, pair, near, peer
    )
    far_end = send(far, OUTWARD)
    first_d, second_d = swap(first_y, "row", 2), swap(second_x, "row", 4)
    far_end, first_d, second_d = tie(far_end, first_d, second_d)
    peers = [peer, other(pair), other(near), other(near_end), other(far), other(far_end)]
    held = [
        {0: first, 4: first_y, 2: first_x, 6: first_d},
        {0: second, 2: second_x, 4: second_y, 6: second_d},
    ]
    return [tokens, pair, near, near_end, far, far_end], peers, held


def direct_gather(block, axis, masks):
    return {mask: swap(block, axis, mask) if mask else block for mask in masks}


def doubling_gather(block, axis, masks):
    held = {0: block}
    for mask in masks:
        for known in list(held):
            held[known | mask] = swap(held[known], axis, mask)
    return held


def in_order(pieces, axis):
    masks, place = sorted(pieces[0]), lax.axis_index(axis)
    core = place % 2
    joined = jnp.stack([jnp.stack([piece[k] for k in masks]) for piece in pieces], axis=1)
    joined = joined[jnp.bitwise_xor(jnp.arange(len(masks)), place // 2)]
    joined = jnp.where(core == 0, joined, joined[:, ::-1])
    return joined.reshape(joined.shape[0], -1, joined.shape[-1])


def cost(us):
    return pl.CostEstimate(flops=int(us * 1.15e9), bytes_accessed=0, transcendentals=0)


def call(kernel, outs, in_specs, scratch, estimate, out_specs=None, vmem=16):
    if out_specs is None:
        out_specs = jax.tree.map(lambda _: VMEM, outs)
    return pl.pallas_call(
        kernel,
        out_shape=outs,
        in_specs=in_specs,
        out_specs=out_specs,
        scratch_shapes=scratch,
        cost_estimate=estimate,
        compiler_params=pltpu.CompilerParams(vmem_limit_bytes=vmem * 1024 * 1024),
    )


def line_copies(refs, routes, place, target, sems, act):
    for n, (ref, (owner, held)) in enumerate(zip(refs, routes)):

        @pl.when(held(place))
        def _():
            copy = pltpu.make_async_copy(ref, target(owner(place)), sems.at[n])
            getattr(copy, act)()


def mod_kernel(cond_ref, w_ref, out_ref):
    requests, groups, width = cond_ref.shape[0], w_ref.shape[0], w_ref.shape[2]
    request = lax.axis_index("row") // 2
    values = jnp.concatenate(
        [cond_ref[pl.ds(jnp.bitwise_xor(request, k), 1), :] for k in range(requests)], axis=0
    )
    activated = (values * (1.0 / (1.0 + jnp.exp(-values)))).astype(BF16)
    out_ref[...] = jnp.zeros(out_ref.shape, F32)
    for group in range(groups):
        out_ref[:, group, :width] = jnp.dot(
            activated, w_ref[group], preferred_element_type=F32
        )


def pack_kernel(qkv_ref, kv_ref, keep_ref, give_ref):
    half = keep_ref.shape[1] // 5
    first = lax.axis_index("row") % 2 == 0
    for k in range(5):
        rows = qkv_ref[k] if k < 3 else kv_ref[:, k - 3]
        low, high = rows[:, :half], rows[:, half:]
        here = slice(k * half, (k + 1) * half)
        keep_ref[:, here] = jnp.where(first, low, high)
        give_ref[:, here] = jnp.where(first, high, low)


def stats_kernel(img_ref, txt_ref, out_ref):
    img = img_ref.shape[1]
    txt = txt_ref.shape[0]
    out_ref[...] = jnp.zeros(out_ref.shape, F32)
    for values, low, high in (
        (img_ref[...].astype(F32), 0, img),
        (txt_ref[...].astype(F32).T, img, img + txt),
    ):
        out_ref[0:1, low:high] = jnp.sum(values, axis=0, keepdims=True)
        out_ref[1:2, low:high] = jnp.sum(values * values, axis=0, keepdims=True)


def norm_kernel(total, img_ref, txt_ref, stats_ref, mod_ref, out_ref):
    width, img = img_ref.shape
    txt = txt_ref.shape[0]
    stats = stats_ref[...] / total
    row = lax.broadcasted_iota(jnp.int32, stats.shape, 0)
    average = stats[0:1]
    inverse = lax.rsqrt(stats[1:2] - average * average + EPS_NORM)
    columns = jnp.where(row == 0, average, inverse).T
    chunk = 128
    if out_ref.shape[1] > width:
        out_ref[:, width:] = jnp.zeros((img + txt, out_ref.shape[1] - width), BF16)
    for low in range(0, img + txt, chunk):
        for start in range(0, width, chunk):
            stop = min(start + chunk, width)
            if low < img:
                high = min(low + chunk, img)
                values, group = img_ref[start:stop, low:high].T, 0
            else:
                high = min(low + chunk, img + txt)
                values, group = txt_ref[low - img : high - img, start:stop], 3
            normed = (values.astype(F32) - columns[low:high, 0:1]) * columns[low:high, 1:2]
            stretch = 1.0 + mod_ref[group + 1 : group + 2, start:stop]
            normed = normed * stretch + mod_ref[group : group + 1, start:stop]
            out_ref[low:high, start:stop] = normed.astype(BF16)


def attend(img, txt, head, length_ref, queries, keys, values, out_refs):
    width = queries.shape[1]
    place = lax.axis_index("row")
    side = lax.rem(place, 2)
    slot = lax.broadcasted_iota(jnp.int32, (2 * txt, 1), 0)
    other = (slot >= txt).astype(jnp.int32)
    owner = jnp.where(other == 1, 1 - side, side)
    allowed = owner * txt + slot - other * txt < length_ref[place // 2]
    turned = values.T
    ones = jnp.ones((16, keys.shape[0]), BF16)
    rows = [
        jnp.concatenate([turned[k * head : (k + 1) * head], ones], axis=0)
        for k in range(width // head)
    ]
    lane = lax.broadcasted_iota(jnp.int32, (1, width), 1) // head
    step = 256 if img % 256 == 0 else img

    def scores_of(k, low):
        query = jnp.where(lane == k, queries[low : low + step], 0.0).astype(BF16)
        score = lax.dot_general(
            keys, query, (((1,), (1,)), ((), ())), preferred_element_type=F32
        )
        tail = jnp.where(allowed, score[2 * img :], -1e30)
        return jnp.concatenate([score[: 2 * img], tail], axis=0)

    work = [(k, low) for low in range(0, 2 * img, step) for k in range(width // head)]
    ahead = scores_of(*work[0])
    for n, (k, low) in enumerate(work):
        scores = ahead
        if n + 1 < len(work):
            ahead = scores_of(*work[n + 1])
        weights = jnp.exp(scores - jnp.max(scores, axis=0, keepdims=True)).astype(BF16)
        mixed = jnp.dot(rows[k], weights, preferred_element_type=F32)
        out_ref, at = out_refs[low // img], low % img
        out_ref[k * head : (k + 1) * head, at : at + step] = (
            mixed[:head] / mixed[head : head + 1]
        ).astype(BF16)


def project_kernel(routes, masks, img, head, length_ref, q_gain_ref, k_gain_ref, *refs):
    lines = refs[: len(routes)], refs[len(routes) : 2 * len(routes)]
    refs = refs[2 * len(routes) :]
    n_blocks = 2 * len(masks) if masks else 1
    blocks, refs = refs[:n_blocks], refs[n_blocks:]
    outs, refs = refs[:2], refs[2:]
    x_ref, w_ref, img_ref, txt_ref, q_ref, k_ref, v_ref, sems_x, sems_w = refs
    tokens, wide = lines[0][0].shape
    txt = tokens - img
    count = x_ref.shape[1] // wide
    half = img_ref.shape[1] // 3
    place, col = lax.axis_index("row"), lax.axis_index("col")
    chip, core = place // 2, lax.rem(place, 2)

    def copy_line(n, act):
        for k, (low, high, to) in enumerate(
            ((0, img, n * img), (img, tokens, 2 * img + n * txt))
        ):
            parts = [ref.at[pl.ds(low, high - low)] for ref in lines[n]]
            target = lambda owner: x_ref.at[
                pl.ds(to, high - low), pl.ds(pl.multiple_of(owner * wide, 128), wide)
            ]
            line_copies(parts, routes, col, target, sems_x.at[n, k], act)

    copy_line(0, "start")
    stages = [[], []]
    if not masks:
        width = blocks[0].shape[1]
        for k in range(count):
            target = w_ref.at[pl.ds(k * wide, width)]
            stages[0].append(pltpu.make_async_copy(blocks[0].at[k], target, sems_w.at[0, k]))
    else:
        depth = blocks[0].shape[0]
        width = 2 * depth
        for k in range(count):
            for piece in range(2):
                row = jnp.bitwise_xor(chip, k) * wide + jnp.where(core == piece, 0, depth)
                target = w_ref.at[pl.ds(pl.multiple_of(row, 16), depth)]
                ref = blocks[piece * len(masks) + k]
                copy = pltpu.make_async_copy(ref, target, sems_w.at[piece, k])
                stages[2 * k // count].append(copy)
    for copy in stages[0]:
        copy.start()
    for k in range(count):
        if wide > width:
            w_ref[k * wide + width : (k + 1) * wide] = jnp.zeros((wide - width, 5 * half), BF16)
    row = lax.broadcasted_iota(jnp.int32, (half, half), 0) // head
    column = lax.broadcasted_iota(jnp.int32, (half, half), 1) // head
    mean_of = jnp.where(row == column, 1.0 / head, 0.0).astype(BF16)

    def head_norm(values, gain):
        square = values * values
        mean_square = jnp.zeros_like(square)
        for _ in range(2):
            term = square.astype(BF16)
            mean_square += jnp.dot(term, mean_of, preferred_element_type=F32)
            square = square - term.astype(F32)
        return (values * lax.rsqrt(mean_square + EPS_NORM) * gain).astype(BF16)

    copy_line(0, "wait")
    depth = count // 2 * wide
    for k in range(2):
        for copy in stages[k]:
            copy.wait()
        if k == 0:
            for copy in stages[1]:
                copy.start()
        else:
            copy_line(1, "start")
        if not masks:
            here = pl.ds(k * depth, depth)
        else:
            here = pl.ds(pl.multiple_of(jnp.bitwise_xor(2 * chip // count, k) * depth, 128), depth)
        term = jnp.dot(x_ref[:img, here], w_ref[here, : 3 * half], preferred_element_type=F32)
        img_ref[:img] = term if k == 0 else img_ref[:img] + term
    copy_line(1, "wait")
    img_ref[img:] = jnp.dot(
        x_ref[img : 2 * img], w_ref[:, : 3 * half], preferred_element_type=F32
    )
    txt_ref[...] = jnp.dot(x_ref[2 * img :], w_ref[:, 3 * half :], preferred_element_type=F32)
    scaling = head ** (-0.5)
    wide_gain = lambda gain: jnp.concatenate([gain] * (half // head), axis=1)
    queries = head_norm(img_ref[:, :half], wide_gain(q_gain_ref[...]))
    q_ref[...] = (queries.astype(F32) * scaling).astype(BF16)
    k_ref[: 2 * img] = head_norm(img_ref[:, half : 2 * half], wide_gain(k_gain_ref[0:1]))
    k_ref[2 * img :] = head_norm(txt_ref[:, :half], wide_gain(k_gain_ref[1:2]))
    v_ref[: 2 * img] = img_ref[:, 2 * half :].astype(BF16)
    v_ref[2 * img :] = txt_ref[:, half:].astype(BF16)
    attend(img, txt, head, length_ref, q_ref[...], k_ref[...], v_ref[...], outs)


def place_heads(line, routes, col, target, sems):
    core = lax.rem(lax.axis_index("row"), 2)
    size = line[0].shape[0] // 2
    for act in ("start", "wait"):
        for n in range(2):
            rows = pl.ds(pl.multiple_of(jnp.where(core == n, 0, size), 16), size)
            parts = [ref.at[pl.ds(n * size, size)] for ref in line]
            line_copies(parts, routes, col, lambda owner: target(owner, rows), sems.at[n], act)


def early_kernel(routes, far, masks, mod_ref, *refs):
    n_lines = len(routes)
    line, refs = refs[:n_lines], refs[n_lines:]
    weights, refs = refs[:2], refs[2:]
    sum_ref, far_ref, gain_ref, const_ref, a_ref, w_ref, sems_a, sems_w = refs
    width = sum_ref.shape[0]
    count = a_ref.shape[0]
    depth = w_ref.shape[2]
    place, col = lax.axis_index("row"), lax.axis_index("col")
    copies = []
    for k, ref in enumerate(weights):
        for n, mask in enumerate(masks):
            target = w_ref.at[jnp.bitwise_xor(place, mask + k)]
            source = ref.at[pl.ds(n * w_ref.shape[1], w_ref.shape[1])]
            copies.append(pltpu.make_async_copy(source, target, sems_w.at[k, n]))
    for copy in copies:
        copy.start()
    place_heads(line, routes, col, lambda owner, rows: a_ref.at[owner, rows], sems_a)
    for copy in copies:
        copy.wait()
    per_col = w_ref.shape[0] // count
    farthest = far(col)
    total = None
    for k in range(1, count):
        owner = lax.rem(farthest + k, count)
        for n in range(per_col):
            term = jnp.dot(
                w_ref[owner * per_col + n, :width],
                a_ref[owner, n * depth : (n + 1) * depth],
                preferred_element_type=F32,
            )
            total = term if total is None else total + term
    sum_ref[...] = total
    for n in range(per_col):
        far_ref[:, n * depth : (n + 1) * depth] = w_ref[farthest * per_col + n, :width]

    patch = gain_ref.shape[0] // 3
    slab = width // per_col
    consts = jnp.zeros((8, patch), F32)
    row = lax.broadcasted_iota(jnp.int32, (8, patch), 0)
    for n in range(per_col):
        for k in range((w_ref.shape[1] - width) // patch):
            low, high = k * depth, min((k + 1) * depth, slab)
            if low >= high:
                continue
            piece = w_ref[col * per_col + n, width + k * patch : width + (k + 1) * patch]
            here = slice(n * slab + low, n * slab + high)
            linear = piece[:, : high - low].astype(F32)
            gained = linear * (1.0 + mod_ref[6:7, here])
            both = (jnp.sum(gained, axis=1, keepdims=True), linear * mod_ref[5:6, here])
            both = jnp.concatenate(
                [jnp.broadcast_to(both[0], (patch, 128)), jnp.broadcast_to(
                    jnp.sum(both[1], axis=1, keepdims=True), (patch, 128))], axis=0
            ).T
            consts += jnp.where(
                row == 2, both[:8, :patch], jnp.where(row == 3, both[:8, patch:], 0.0)
            )
            for t in range(3):
                term = gained.astype(BF16)
                gain_ref[t * patch : (t + 1) * patch, here] = term
                gained = gained - term.astype(F32)
    const_ref[...] = jnp.zeros(const_ref.shape, F32)
    const_ref[:, :patch] = consts


def late_kernel(routes, mod_ref, x_ref, sum_ref, far_ref, gain_ref, const_ref, *refs):
    n_lines = len(routes)
    line, (out_ref, a_ref, sems_a) = refs[:n_lines], refs[n_lines:]
    width, tokens = x_ref.shape
    col = lax.axis_index("col")
    place_heads(line, routes, col, lambda owner, rows: a_ref.at[rows], sems_a)
    gate = mod_ref[...].T[:width, 2:3]
    projected = sum_ref[...] + jnp.dot(far_ref[...], a_ref[...], preferred_element_type=F32)
    updated = (x_ref[...].astype(F32) + gate * projected).astype(BF16)
    wide = updated.astype(F32)
    sums = jnp.sum(wide, axis=0, keepdims=True)
    squares = jnp.sum(wide * wide, axis=0, keepdims=True)
    patch = gain_ref.shape[0] // 3
    terms = jnp.dot(gain_ref[...], updated, preferred_element_type=F32)
    out_ref[:patch] = terms[:patch] + terms[patch : 2 * patch] + terms[2 * patch :]
    row = lax.broadcasted_iota(jnp.int32, (8, tokens), 0)
    out_ref[patch:] = jnp.where(row == 0, sums, jnp.where(row == 1, squares, const_ref[...]))


def sigma_of(step_now):
    remain = 1.0 - step_now.astype(F32) / STEPS
    return 3.0 * remain / (1.0 + 2.0 * remain)


def per_device(
    hidden_img,
    hidden_txt,
    text_len,
    step_index,
    latent,
    cond,
    mod_weight,
    qkv_weight,
    kv_text_weight,
    q_gain,
    k_gain,
    out_weight,
    final_weight,
):
    row_count, col_count = lax.axis_size("row"), lax.axis_size("col")
    request = lax.axis_index("row") // 2
    requests = cond.shape[0]
    img, width = hidden_img.shape
    txt = hidden_txt.shape[0]
    head = q_gain.shape[0]
    part_cols = qkv_weight.shape[2]
    half = part_cols // 2
    full_width = width * col_count

    wide = -(-width // 128) * 128
    room = -(-txt // 128) * 128
    tokens = img + room
    mod_part = call(
        mod_kernel,
        jax.ShapeDtypeStruct((requests, 8, wide), F32),
        [VMEM, VMEM],
        [],
        cost(2),
    )(cond, jnp.moveaxis(mod_weight, 1, 0))
    mod_own = mod_part[0]
    for k in range(1, requests):
        mod_own = mod_own + swap(mod_part[k], "row", 2 * k)
    stats = call(
        stats_kernel,
        jax.ShapeDtypeStruct((8, tokens), F32),
        [VMEM, VMEM],
        [],
        cost(1),
    )(hidden_img.T, hidden_txt)
    stats = sum((swap(stats, "col", mask) for mask in range(1, col_count)), stats)

    chip_masks = [1 << bit for bit in range(1, row_count.bit_length() - 1)]
    packed = call(
        pack_kernel,
        (jax.ShapeDtypeStruct((qkv_weight.shape[0], 5 * half), BF16),) * 2,
        [VMEM, VMEM],
        [],
        cost(2),
        (VMEM, VMEM),
    )(jnp.moveaxis(qkv_weight, 1, 0), kv_text_weight)
    packed = packed[0], swap(packed[1], "row", 1)
    *packed, mod_own = tie(*packed, mod_own)
    mod_own = mod_own + swap(mod_own, "row", 1)
    ready = call(
        functools.partial(norm_kernel, full_width),
        jax.ShapeDtypeStruct((img + txt, wide), BF16),
        [VMEM] * 4,
        [],
        cost(1),
    )(hidden_img.T, hidden_txt, stats, mod_own)
    routes = line_routes(col_count)
    small = col_count == 4 and row_count == 8
    if small:
        ready, *packed = tie(ready, *packed)
        line, peer_line, gathered = gather_both(ready, packed)
    else:
        line = line_gather(ready, "col")
        peer_line = [swap(part, "row", 1) for part in line]
        gathered = [doubling_gather(part, "row", chip_masks) for part in packed]

    if gathered[0][0].shape[0] % 16 == 0:
        masks = sorted(gathered[0])
        blocks = [piece[k] for piece in gathered for k in masks]
    else:
        masks, blocks = [], [in_order(gathered, "row")]
    heads_out = jax.ShapeDtypeStruct((half, img), BF16)
    full_wide = col_count * wide
    projected = call(
        functools.partial(project_kernel, routes, masks, img, head),
        (heads_out, heads_out),
        [SMEM, VMEM, VMEM] + [HBM] * (2 * len(routes) + len(blocks)),
        [
            pltpu.VMEM((2 * (img + txt), full_wide), BF16),
            pltpu.VMEM((full_wide, 5 * half), BF16),
            pltpu.VMEM((2 * img, 3 * half), F32),
            pltpu.VMEM((2 * txt, 2 * half), F32),
            pltpu.VMEM((2 * img, half), BF16),
            *[pltpu.VMEM((2 * (img + txt), half), BF16)] * 2,
            pltpu.SemaphoreType.DMA((2, 2, len(routes))),
            pltpu.SemaphoreType.DMA((2, col_count)),
        ],
        cost(PROJECT),
        (VMEM, VMEM),
        vmem=PROJECT_MIB,
    )(text_len, q_gain[None], k_gain, *line, *peer_line, *blocks)
    head_depth, patch = final_weight.shape
    depth = out_weight.shape[0]
    folds = -(-head_depth // depth)
    tail = jnp.pad(final_weight.T, ((0, 0), (0, folds * depth - head_depth)))
    tail = jnp.swapaxes(tail.reshape(patch, folds, depth), 0, 1).reshape(folds * patch, depth)
    out_packed = jnp.concatenate([out_weight.T, tail], axis=0)
    masks = list(range(0, row_count, 2))
    out_blocks = direct_gather(out_packed, "row", masks)

    keep, give, *others = tie(*projected, *[out_blocks[k] for k in masks[1:]])
    own_rows = jnp.concatenate([out_packed, *others], axis=0)
    other_rows = swap(own_rows, "row", 1)
    take = swap(give, "row", 1)
    if small:
        line, other_rows = gather_heads(keep, take, other_rows)
    else:
        line = line_gather(jnp.concatenate([keep, take], axis=0), "col")
    early, late, far = far_routes(col_count)
    sems = pltpu.SemaphoreType.DMA((2, len(routes)))
    bundle = call(
        functools.partial(early_kernel, [route for _, route in early], far, masks),
        (
            jax.ShapeDtypeStruct((width, img), F32),
            jax.ShapeDtypeStruct((width, part_cols), BF16),
            jax.ShapeDtypeStruct((3 * patch, width), BF16),
            jax.ShapeDtypeStruct((8, img), F32),
        ),
        [VMEM] + [HBM] * (len(early) + 2),
        [
            pltpu.VMEM((col_count, part_cols, img), BF16),
            pltpu.VMEM((row_count,) + out_packed.shape, BF16),
            sems,
            pltpu.SemaphoreType.DMA((2, len(masks))),
        ],
        cost(5),
        (VMEM,) * 4,
        vmem=EARLY,
    )(
        mod_own,
        *[line[k] for k, _ in early],
        own_rows,
        other_rows,
    )
    partial_sum = call(
        functools.partial(late_kernel, [route for _, route in late]),
        jax.ShapeDtypeStruct((patch + 8, img), F32),
        [VMEM] * 6 + [HBM] * len(late),
        [pltpu.VMEM((part_cols, img), BF16), sems],
        cost(3),
        vmem=24,
    )(mod_own, hidden_img.T, *bundle, *[line[k] for k, _ in late])
    mask = 1
    while mask < col_count:
        partial_sum = partial_sum + swap(partial_sum, "col", mask)
        mask *= 2
    average = partial_sum[patch : patch + 1] / full_width
    mean_square = partial_sum[patch + 1 : patch + 2] / full_width
    inverse = lax.rsqrt(mean_square - average * average + EPS_NORM)
    gains = partial_sum[patch + 2, :patch][:, None]
    shifts = partial_sum[patch + 3, :patch][:, None]
    velocity = inverse * (partial_sum[:patch] - average * gains) + shifts
    step_now = lax.dynamic_index_in_dim(step_index, request, 0, keepdims=False)
    sigma_step = sigma_of(step_now + 1) - sigma_of(step_now)
    latent_next = latent.T + sigma_step * velocity
    return (velocity.T, latent_next.T)


def solution(mesh):
    in_specs = (
        P("row", "col"),
        P("row", "col"),
        P(),
        P(),
        P("row", None),
        P(None, "row"),
        P("row", None, "col"),
        P("row", None, "col"),
        P("row", None, "col"),
        P(),
        P(),
        P("row", "col"),
        P("row", None),
    )
    out_specs = (P("row", None), P("row", None))
    return jax.shard_map(
        per_device, mesh=mesh, in_specs=in_specs, out_specs=out_specs, check_vma=False
    )
```

```python
import functools

import jax
import jax.numpy as jnp
from jax import lax
from jax.experimental import pallas as pl
from jax.experimental.pallas import tpu as pltpu
from jax.sharding import PartitionSpec as P

STEPS = 28
EPS_NORM = 1e-06
PROJECT_MIB = 44
PROJECT = 20
EARLY = 32
F32 = jnp.float32
BF16 = jnp.bfloat16
HBM = pl.BlockSpec(memory_space=pltpu.HBM)
VMEM = pl.BlockSpec(memory_space=pltpu.VMEM)
SMEM = pl.BlockSpec(memory_space=pltpu.SMEM)


def swap(block, axis, mask):
    count = lax.axis_size(axis)
    return lax.ppermute(block, axis, [(i, i ^ mask) for i in range(count)])


def shift(block, axis, step):
    count = lax.axis_size(axis)
    route = [(i, i + step) for i in range(count) if 0 <= i + step < count]
    return lax.ppermute(block, axis, route)


def tie(*arrays):
    return lax.optimization_barrier(arrays)


def line_gather(block, axis):
    held = {0: block}
    for step in range(1, lax.axis_size(axis)):
        held[-step] = shift(held[1 - step], axis, 1)
        held[step] = shift(held[step - 1], axis, -1)
    return [held[k] for k in sorted(held)]


def line_routes(count):
    if count == 4:
        near = lambda p: jnp.where(p < 2, 2, 1)
        far = lambda p: jnp.where(p < 2, 3, 0)
        inner = lambda p: (p == 1) | (p == 2)
        outer = lambda p: (p == 0) | (p == 3)
        always = lambda p: p >= 0
        return [
            (lambda p: p, always),
            (lambda p: jnp.bitwise_xor(p, 1), always),
            (near, inner),
            (near, outer),
            (far, inner),
            (far, outer),
        ]
    result = []
    for offset in range(1 - count, count):
        inside = lambda p, offset=offset: (p + offset >= 0) & (p + offset < count)
        result.append((lambda p, offset=offset: p + offset, inside))
    return result


def far_routes(count):
    routes = list(enumerate(line_routes(count)))
    if count == 4:
        return routes[:4], routes[4:], routes[4][1][0]
    far = lambda p: count - 1 - p
    early, late = [], []
    for n, (owner, held) in routes:
        is_far = lambda p, owner=owner: owner(p) == far(p)
        early.append((n, (owner, lambda p, held=held, is_far=is_far: held(p) & ~is_far(p))))
        late.append((n, (owner, lambda p, held=held, is_far=is_far: held(p) & is_far(p))))
    return early, late, far


MIDDLE = [(1, 2), (2, 1)]
OUTWARD = [(1, 0), (2, 3)]


def gather_heads(keep, take, others):
    send = lambda held, route: lax.ppermute(held, "col", route)
    join = lambda *held: jnp.concatenate(held, axis=0)
    keep_pair, keep_near = swap(keep, "col", 1), send(keep, MIDDLE)
    take_pair, take_near = swap(take, "col", 1), send(take, MIDDLE)
    keep_pair, keep_near, take_pair, take_near, others = tie(
        keep_pair, keep_near, take_pair, take_near, others
    )
    pair, near = join(keep_pair, take_pair), join(keep_near, take_near)
    near_end, far = send(near, OUTWARD), send(pair, MIDDLE)
    near_end, far = tie(near_end, far)
    return [join(keep, take), pair, near, near_end, far, send(far, OUTWARD)], others


def gather_both(tokens, weights):
    send = lambda held, route: lax.ppermute(held, "col", route)
    first, second = weights
    pair, near = swap(tokens, "col", 1), send(tokens, MIDDLE)
    first_y, second_x = swap(first, "row", 4), swap(second, "row", 2)
    other = lambda held: swap(held, "row", 1)
    peer = other(tokens)
    pair, near, first_y, second_x, first, second = tie(
        pair, near, first_y, second_x, first, second
    )
    near_end, far = send(near, OUTWARD), send(pair, MIDDLE)
    first_x, second_y = swap(first, "row", 2), swap(second, "row", 4)
    near_end, far, first_x, second_y, first_y, second_x, pair, near, peer = tie(
        near_end, far, first_x, second_y, first_y, second_x, pair, near, peer
    )
    far_end = send(far, OUTWARD)
    first_d, second_d = swap(first_y, "row", 2), swap(second_x, "row", 4)
    far_end, first_d, second_d = tie(far_end, first_d, second_d)
    peers = [peer, other(pair), other(near), other(near_end), other(far), other(far_end)]
    held = [
        {0: first, 4: first_y, 2: first_x, 6: first_d},
        {0: second, 2: second_x, 4: second_y, 6: second_d},
    ]
    return [tokens, pair, near, near_end, far, far_end], peers, held


def direct_gather(block, axis, masks):
    return {mask: swap(block, axis, mask) if mask else block for mask in masks}


def doubling_gather(block, axis, masks):
    held = {0: block}
    for mask in masks:
        for known in list(held):
            held[known | mask] = swap(held[known], axis, mask)
    return held


def in_order(pieces, axis):
    masks, place = sorted(pieces[0]), lax.axis_index(axis)
    core = place % 2
    joined = jnp.stack([jnp.stack([piece[k] for k in masks]) for piece in pieces], axis=1)
    joined = joined[jnp.bitwise_xor(jnp.arange(len(masks)), place // 2)]
    joined = jnp.where(core == 0, joined, joined[:, ::-1])
    return joined.reshape(joined.shape[0], -1, joined.shape[-1])


def cost(us):
    return pl.CostEstimate(flops=int(us * 1.15e9), bytes_accessed=0, transcendentals=0)


def call(kernel, outs, in_specs, scratch, estimate, out_specs=None, vmem=16):
    if out_specs is None:
        out_specs = jax.tree.map(lambda _: VMEM, outs)
    return pl.pallas_call(
        kernel,
        out_shape=outs,
        in_specs=in_specs,
        out_specs=out_specs,
        scratch_shapes=scratch,
        cost_estimate=estimate,
        compiler_params=pltpu.CompilerParams(vmem_limit_bytes=vmem * 1024 * 1024),
    )


def line_copies(refs, routes, place, target, sems, act):
    for n, (ref, (owner, held)) in enumerate(zip(refs, routes)):

        @pl.when(held(place))
        def _():
            copy = pltpu.make_async_copy(ref, target(owner(place)), sems.at[n])
            getattr(copy, act)()


def mod_kernel(cond_ref, w_ref, out_ref):
    requests, groups, width = cond_ref.shape[0], w_ref.shape[0], w_ref.shape[2]
    request = lax.axis_index("row") // 2
    values = jnp.concatenate(
        [cond_ref[pl.ds(jnp.bitwise_xor(request, k), 1), :] for k in range(requests)], axis=0
    )
    activated = (values * (1.0 / (1.0 + jnp.exp(-values)))).astype(BF16)
    out_ref[...] = jnp.zeros(out_ref.shape, F32)
    for group in range(groups):
        out_ref[:, group, :width] = jnp.dot(
            activated, w_ref[group], preferred_element_type=F32
        )


def pack_kernel(qkv_ref, kv_ref, keep_ref, give_ref):
    half = keep_ref.shape[1] // 5
    first = lax.axis_index("row") % 2 == 0
    for k in range(5):
        rows = qkv_ref[k] if k < 3 else kv_ref[:, k - 3]
        low, high = rows[:, :half], rows[:, half:]
        here = slice(k * half, (k + 1) * half)
        keep_ref[:, here] = jnp.where(first, low, high)
        give_ref[:, here] = jnp.where(first, high, low)


def stats_kernel(img_ref, txt_ref, out_ref):
    img = img_ref.shape[1]
    txt = txt_ref.shape[0]
    out_ref[...] = jnp.zeros(out_ref.shape, F32)
    for values, low, high in (
        (img_ref[...].astype(F32), 0, img),
        (txt_ref[...].astype(F32).T, img, img + txt),
    ):
        out_ref[0:1, low:high] = jnp.sum(values, axis=0, keepdims=True)
        out_ref[1:2, low:high] = jnp.sum(values * values, axis=0, keepdims=True)


def norm_kernel(total, img_ref, txt_ref, stats_ref, mod_ref, out_ref):
    width, img = img_ref.shape
    txt = txt_ref.shape[0]
    stats = stats_ref[...] / total
    row = lax.broadcasted_iota(jnp.int32, stats.shape, 0)
    average = stats[0:1]
    inverse = lax.rsqrt(stats[1:2] - average * average + EPS_NORM)
    columns = jnp.where(row == 0, average, inverse).T
    chunk = 128
    if out_ref.shape[1] > width:
        out_ref[:, width:] = jnp.zeros((img + txt, out_ref.shape[1] - width), BF16)
    for low in range(0, img + txt, chunk):
        for start in range(0, width, chunk):
            stop = min(start + chunk, width)
            if low < img:
                high = min(low + chunk, img)
                values, group = img_ref[start:stop, low:high].T, 0
            else:
                high = min(low + chunk, img + txt)
                values, group = txt_ref[low - img : high - img, start:stop], 3
            normed = (values.astype(F32) - columns[low:high, 0:1]) * columns[low:high, 1:2]
            stretch = 1.0 + mod_ref[group + 1 : group + 2, start:stop]
            normed = normed * stretch + mod_ref[group : group + 1, start:stop]
            out_ref[low:high, start:stop] = normed.astype(BF16)


def attend(img, txt, head, length_ref, queries, keys, values, out_refs):
    width = queries.shape[1]
    place = lax.axis_index("row")
    side = lax.rem(place, 2)
    slot = lax.broadcasted_iota(jnp.int32, (2 * txt, 1), 0)
    other = (slot >= txt).astype(jnp.int32)
    owner = jnp.where(other == 1, 1 - side, side)
    allowed = owner * txt + slot - other * txt < length_ref[place // 2]
    turned = values.T
    ones = jnp.ones((16, keys.shape[0]), BF16)
    rows = [
        jnp.concatenate([turned[k * head : (k + 1) * head], ones], axis=0)
        for k in range(width // head)
    ]
    lane = lax.broadcasted_iota(jnp.int32, (1, width), 1) // head
    step = 256 if img % 256 == 0 else img

    def scores_of(k, low):
        query = jnp.where(lane == k, queries[low : low + step], 0.0).astype(BF16)
        score = lax.dot_general(
            keys, query, (((1,), (1,)), ((), ())), preferred_element_type=F32
        )
        tail = jnp.where(allowed, score[2 * img :], -1e30)
        return jnp.concatenate([score[: 2 * img], tail], axis=0)

    work = [(k, low) for low in range(0, 2 * img, step) for k in range(width // head)]
    ahead = scores_of(*work[0])
    for n, (k, low) in enumerate(work):
        scores = ahead
        if n + 1 < len(work):
            ahead = scores_of(*work[n + 1])
        weights = jnp.exp(scores - jnp.max(scores, axis=0, keepdims=True)).astype(BF16)
        mixed = jnp.dot(rows[k], weights, preferred_element_type=F32)
        out_ref, at = out_refs[low // img], low % img
        out_ref[k * head : (k + 1) * head, at : at + step] = (
            mixed[:head] / mixed[head : head + 1]
        ).astype(BF16)


def project_kernel(routes, masks, img, head, length_ref, q_gain_ref, k_gain_ref, *refs):
    lines = refs[: len(routes)], refs[len(routes) : 2 * len(routes)]
    refs = refs[2 * len(routes) :]
    n_blocks = 2 * len(masks) if masks else 1
    blocks, refs = refs[:n_blocks], refs[n_blocks:]
    outs, refs = refs[:2], refs[2:]
    x_ref, w_ref, img_ref, txt_ref, q_ref, k_ref, v_ref, sems_x, sems_w = refs
    tokens, wide = lines[0][0].shape
    txt = tokens - img
    count = x_ref.shape[1] // wide
    half = img_ref.shape[1] // 3
    place, col = lax.axis_index("row"), lax.axis_index("col")
    chip, core = place // 2, lax.rem(place, 2)

    def copy_line(n, act):
        for k, (low, high, to) in enumerate(
            ((0, img, n * img), (img, tokens, 2 * img + n * txt))
        ):
            parts = [ref.at[pl.ds(low, high - low)] for ref in lines[n]]
            target = lambda owner: x_ref.at[
                pl.ds(to, high - low), pl.ds(pl.multiple_of(owner * wide, 128), wide)
            ]
            line_copies(parts, routes, col, target, sems_x.at[n, k], act)

    copy_line(0, "start")
    stages = [[], []]
    if not masks:
        width = blocks[0].shape[1]
        for k in range(count):
            target = w_ref.at[pl.ds(k * wide, width)]
            stages[0].append(pltpu.make_async_copy(blocks[0].at[k], target, sems_w.at[0, k]))
    else:
        depth = blocks[0].shape[0]
        width = 2 * depth
        for k in range(count):
            for piece in range(2):
                row = jnp.bitwise_xor(chip, k) * wide + jnp.where(core == piece, 0, depth)
                target = w_ref.at[pl.ds(pl.multiple_of(row, 16), depth)]
                ref = blocks[piece * len(masks) + k]
                copy = pltpu.make_async_copy(ref, target, sems_w.at[piece, k])
                stages[2 * k // count].append(copy)
    for copy in stages[0] + stages[1]:
        copy.start()
    copy_line(1, "start")
    for k in range(count):
        if wide > width:
            w_ref[k * wide + width : (k + 1) * wide] = jnp.zeros((wide - width, 5 * half), BF16)
    row = lax.broadcasted_iota(jnp.int32, (half, half), 0) // head
    column = lax.broadcasted_iota(jnp.int32, (half, half), 1) // head
    mean_of = jnp.where(row == column, 1.0 / head, 0.0).astype(BF16)

    def head_norm(values, gain):
        square = values * values
        mean_square = jnp.zeros_like(square)
        for _ in range(2):
            term = square.astype(BF16)
            mean_square += jnp.dot(term, mean_of, preferred_element_type=F32)
            square = square - term.astype(F32)
        return (values * lax.rsqrt(mean_square + EPS_NORM) * gain).astype(BF16)

    copy_line(0, "wait")
    depth = count // 2 * wide
    for k in range(2):
        for copy in stages[k]:
            copy.wait()
        if not masks:
            here = pl.ds(k * depth, depth)
        else:
            here = pl.ds(pl.multiple_of(jnp.bitwise_xor(2 * chip // count, k) * depth, 128), depth)
        term = jnp.dot(x_ref[:img, here], w_ref[here, : 3 * half], preferred_element_type=F32)
        img_ref[:img] = term if k == 0 else img_ref[:img] + term
    copy_line(1, "wait")
    img_ref[img:] = jnp.dot(
        x_ref[img : 2 * img], w_ref[:, : 3 * half], preferred_element_type=F32
    )
    txt_ref[...] = jnp.dot(x_ref[2 * img :], w_ref[:, 3 * half :], preferred_element_type=F32)
    scaling = head ** (-0.5)
    wide_gain = lambda gain: jnp.concatenate([gain] * (half // head), axis=1)
    queries = head_norm(img_ref[:, :half], wide_gain(q_gain_ref[...]))
    q_ref[...] = (queries.astype(F32) * scaling).astype(BF16)
    k_ref[: 2 * img] = head_norm(img_ref[:, half : 2 * half], wide_gain(k_gain_ref[0:1]))
    k_ref[2 * img :] = head_norm(txt_ref[:, :half], wide_gain(k_gain_ref[1:2]))
    v_ref[: 2 * img] = img_ref[:, 2 * half :].astype(BF16)
    v_ref[2 * img :] = txt_ref[:, half:].astype(BF16)
    attend(img, txt, head, length_ref, q_ref[...], k_ref[...], v_ref[...], outs)


def place_heads(line, routes, col, target, sems):
    core = lax.rem(lax.axis_index("row"), 2)
    size = line[0].shape[0] // 2
    for act in ("start", "wait"):
        for n in range(2):
            rows = pl.ds(pl.multiple_of(jnp.where(core == n, 0, size), 16), size)
            parts = [ref.at[pl.ds(n * size, size)] for ref in line]
            line_copies(parts, routes, col, lambda owner: target(owner, rows), sems.at[n], act)


def early_kernel(routes, far, masks, mod_ref, *refs):
    n_lines = len(routes)
    line, refs = refs[:n_lines], refs[n_lines:]
    weights, refs = refs[:2], refs[2:]
    sum_ref, far_ref, gain_ref, const_ref, a_ref, w_ref, sems_a, sems_w = refs
    width = sum_ref.shape[0]
    count = a_ref.shape[0]
    depth = w_ref.shape[2]
    place, col = lax.axis_index("row"), lax.axis_index("col")
    copies = []
    for k, ref in enumerate(weights):
        for n, mask in enumerate(masks):
            target = w_ref.at[jnp.bitwise_xor(place, mask + k)]
            source = ref.at[pl.ds(n * w_ref.shape[1], w_ref.shape[1])]
            copies.append(pltpu.make_async_copy(source, target, sems_w.at[k, n]))
    for copy in copies:
        copy.start()
    place_heads(line, routes, col, lambda owner, rows: a_ref.at[owner, rows], sems_a)
    for copy in copies:
        copy.wait()
    per_col = w_ref.shape[0] // count
    farthest = far(col)
    total = None
    for k in range(1, count):
        owner = lax.rem(farthest + k, count)
        for n in range(per_col):
            term = jnp.dot(
                w_ref[owner * per_col + n, :width],
                a_ref[owner, n * depth : (n + 1) * depth],
                preferred_element_type=F32,
            )
            total = term if total is None else total + term
    sum_ref[...] = total
    for n in range(per_col):
        far_ref[:, n * depth : (n + 1) * depth] = w_ref[farthest * per_col + n, :width]

    patch = gain_ref.shape[0] // 3
    slab = width // per_col
    consts = jnp.zeros((8, patch), F32)
    row = lax.broadcasted_iota(jnp.int32, (8, patch), 0)
    for n in range(per_col):
        for k in range((w_ref.shape[1] - width) // patch):
            low, high = k * depth, min((k + 1) * depth, slab)
            if low >= high:
                continue
            piece = w_ref[col * per_col + n, width + k * patch : width + (k + 1) * patch]
            here = slice(n * slab + low, n * slab + high)
            linear = piece[:, : high - low].astype(F32)
            gained = linear * (1.0 + mod_ref[6:7, here])
            both = (jnp.sum(gained, axis=1, keepdims=True), linear * mod_ref[5:6, here])
            both = jnp.concatenate(
                [jnp.broadcast_to(both[0], (patch, 128)), jnp.broadcast_to(
                    jnp.sum(both[1], axis=1, keepdims=True), (patch, 128))], axis=0
            ).T
            consts += jnp.where(
                row == 2, both[:8, :patch], jnp.where(row == 3, both[:8, patch:], 0.0)
            )
            for t in range(3):
                term = gained.astype(BF16)
                gain_ref[t * patch : (t + 1) * patch, here] = term
                gained = gained - term.astype(F32)
    const_ref[...] = jnp.zeros(const_ref.shape, F32)
    const_ref[:, :patch] = consts


def late_kernel(routes, mod_ref, x_ref, sum_ref, far_ref, gain_ref, const_ref, *refs):
    n_lines = len(routes)
    line, (out_ref, a_ref, sems_a) = refs[:n_lines], refs[n_lines:]
    width, tokens = x_ref.shape
    col = lax.axis_index("col")
    place_heads(line, routes, col, lambda owner, rows: a_ref.at[rows], sems_a)
    gate = mod_ref[...].T[:width, 2:3]
    projected = sum_ref[...] + jnp.dot(far_ref[...], a_ref[...], preferred_element_type=F32)
    updated = (x_ref[...].astype(F32) + gate * projected).astype(BF16)
    wide = updated.astype(F32)
    sums = jnp.sum(wide, axis=0, keepdims=True)
    squares = jnp.sum(wide * wide, axis=0, keepdims=True)
    patch = gain_ref.shape[0] // 3
    terms = jnp.dot(gain_ref[...], updated, preferred_element_type=F32)
    out_ref[:patch] = terms[:patch] + terms[patch : 2 * patch] + terms[2 * patch :]
    row = lax.broadcasted_iota(jnp.int32, (8, tokens), 0)
    out_ref[patch:] = jnp.where(row == 0, sums, jnp.where(row == 1, squares, const_ref[...]))


def sigma_of(step_now):
    remain = 1.0 - step_now.astype(F32) / STEPS
    return 3.0 * remain / (1.0 + 2.0 * remain)


def per_device(
    hidden_img,
    hidden_txt,
    text_len,
    step_index,
    latent,
    cond,
    mod_weight,
    qkv_weight,
    kv_text_weight,
    q_gain,
    k_gain,
    out_weight,
    final_weight,
):
    row_count, col_count = lax.axis_size("row"), lax.axis_size("col")
    request = lax.axis_index("row") // 2
    requests = cond.shape[0]
    img, width = hidden_img.shape
    txt = hidden_txt.shape[0]
    head = q_gain.shape[0]
    part_cols = qkv_weight.shape[2]
    half = part_cols // 2
    full_width = width * col_count

    wide = -(-width // 128) * 128
    room = -(-txt // 128) * 128
    tokens = img + room
    mod_part = call(
        mod_kernel,
        jax.ShapeDtypeStruct((requests, 8, wide), F32),
        [VMEM, VMEM],
        [],
        cost(2),
    )(cond, jnp.moveaxis(mod_weight, 1, 0))
    mod_own = mod_part[0]
    for k in range(1, requests):
        mod_own = mod_own + swap(mod_part[k], "row", 2 * k)
    stats = call(
        stats_kernel,
        jax.ShapeDtypeStruct((8, tokens), F32),
        [VMEM, VMEM],
        [],
        cost(1),
    )(hidden_img.T, hidden_txt)
    stats = sum((swap(stats, "col", mask) for mask in range(1, col_count)), stats)

    chip_masks = [1 << bit for bit in range(1, row_count.bit_length() - 1)]
    packed = call(
        pack_kernel,
        (jax.ShapeDtypeStruct((qkv_weight.shape[0], 5 * half), BF16),) * 2,
        [VMEM, VMEM],
        [],
        cost(2),
        (VMEM, VMEM),
    )(jnp.moveaxis(qkv_weight, 1, 0), kv_text_weight)
    packed = packed[0], swap(packed[1], "row", 1)
    *packed, mod_own = tie(*packed, mod_own)
    mod_own = mod_own + swap(mod_own, "row", 1)
    ready = call(
        functools.partial(norm_kernel, full_width),
        jax.ShapeDtypeStruct((img + txt, wide), BF16),
        [VMEM] * 4,
        [],
        cost(1),
    )(hidden_img.T, hidden_txt, stats, mod_own)
    routes = line_routes(col_count)
    small = col_count == 4 and row_count == 8
    if small:
        ready, *packed = tie(ready, *packed)
        line, peer_line, gathered = gather_both(ready, packed)
    else:
        line = line_gather(ready, "col")
        peer_line = [swap(part, "row", 1) for part in line]
        gathered = [doubling_gather(part, "row", chip_masks) for part in packed]

    if gathered[0][0].shape[0] % 16 == 0:
        masks = sorted(gathered[0])
        blocks = [piece[k] for piece in gathered for k in masks]
    else:
        masks, blocks = [], [in_order(gathered, "row")]
    heads_out = jax.ShapeDtypeStruct((half, img), BF16)
    full_wide = col_count * wide
    projected = call(
        functools.partial(project_kernel, routes, masks, img, head),
        (heads_out, heads_out),
        [SMEM, VMEM, VMEM] + [HBM] * (2 * len(routes) + len(blocks)),
        [
            pltpu.VMEM((2 * (img + txt), full_wide), BF16),
            pltpu.VMEM((full_wide, 5 * half), BF16),
            pltpu.VMEM((2 * img, 3 * half), F32),
            pltpu.VMEM((2 * txt, 2 * half), F32),
            pltpu.VMEM((2 * img, half), BF16),
            *[pltpu.VMEM((2 * (img + txt), half), BF16)] * 2,
            pltpu.SemaphoreType.DMA((2, 2, len(routes))),
            pltpu.SemaphoreType.DMA((2, col_count)),
        ],
        cost(PROJECT),
        (VMEM, VMEM),
        vmem=PROJECT_MIB,
    )(text_len, q_gain[None], k_gain, *line, *peer_line, *blocks)
    head_depth, patch = final_weight.shape
    depth = out_weight.shape[0]
    folds = -(-head_depth // depth)
    tail = jnp.pad(final_weight.T, ((0, 0), (0, folds * depth - head_depth)))
    tail = jnp.swapaxes(tail.reshape(patch, folds, depth), 0, 1).reshape(folds * patch, depth)
    out_packed = jnp.concatenate([out_weight.T, tail], axis=0)
    masks = list(range(0, row_count, 2))
    out_blocks = direct_gather(out_packed, "row", masks)

    keep, give, *others = tie(*projected, *[out_blocks[k] for k in masks[1:]])
    own_rows = jnp.concatenate([out_packed, *others], axis=0)
    other_rows = swap(own_rows, "row", 1)
    take = swap(give, "row", 1)
    if small:
        line, other_rows = gather_heads(keep, take, other_rows)
    else:
        line = line_gather(jnp.concatenate([keep, take], axis=0), "col")
    early, late, far = far_routes(col_count)
    sems = pltpu.SemaphoreType.DMA((2, len(routes)))
    bundle = call(
        functools.partial(early_kernel, [route for _, route in early], far, masks),
        (
            jax.ShapeDtypeStruct((width, img), F32),
            jax.ShapeDtypeStruct((width, part_cols), BF16),
            jax.ShapeDtypeStruct((3 * patch, width), BF16),
            jax.ShapeDtypeStruct((8, img), F32),
        ),
        [VMEM] + [HBM] * (len(early) + 2),
        [
            pltpu.VMEM((col_count, part_cols, img), BF16),
            pltpu.VMEM((row_count,) + out_packed.shape, BF16),
            sems,
            pltpu.SemaphoreType.DMA((2, len(masks))),
        ],
        cost(5),
        (VMEM,) * 4,
        vmem=EARLY,
    )(
        mod_own,
        *[line[k] for k, _ in early],
        own_rows,
        other_rows,
    )
    partial_sum = call(
        functools.partial(late_kernel, [route for _, route in late]),
        jax.ShapeDtypeStruct((patch + 8, img), F32),
        [VMEM] * 6 + [HBM] * len(late),
        [pltpu.VMEM((part_cols, img), BF16), sems],
        cost(3),
        vmem=24,
    )(mod_own, hidden_img.T, *bundle, *[line[k] for k, _ in late])
    mask = 1
    while mask < col_count:
        partial_sum = partial_sum + swap(partial_sum, "col", mask)
        mask *= 2
    average = partial_sum[patch : patch + 1] / full_width
    mean_square = partial_sum[patch + 1 : patch + 2] / full_width
    inverse = lax.rsqrt(mean_square - average * average + EPS_NORM)
    gains = partial_sum[patch + 2, :patch][:, None]
    shifts = partial_sum[patch + 3, :patch][:, None]
    velocity = inverse * (partial_sum[:patch] - average * gains) + shifts
    step_now = lax.dynamic_index_in_dim(step_index, request, 0, keepdims=False)
    sigma_step = sigma_of(step_now + 1) - sigma_of(step_now)
    latent_next = latent.T + sigma_step * velocity
    return (velocity.T, latent_next.T)


def solution(mesh):
    in_specs = (
        P("row", "col"),
        P("row", "col"),
        P(),
        P(),
        P("row", None),
        P(None, "row"),
        P("row", None, "col"),
        P("row", None, "col"),
        P("row", None, "col"),
        P(),
        P(),
        P("row", "col"),
        P("row", None),
    )
    out_specs = (P("row", None), P("row", None))
    return jax.shard_map(
        per_device, mesh=mesh, in_specs=in_specs, out_specs=out_specs, check_vma=False
    )
```

```python
import functools

import jax
import jax.numpy as jnp
from jax import lax
from jax.experimental import pallas as pl
from jax.experimental.pallas import tpu as pltpu
from jax.sharding import PartitionSpec as P

STEPS = 28
EPS_NORM = 1e-06
PROJECT_MIB = 44
PROJECT = 20
EARLY = 32
F32 = jnp.float32
BF16 = jnp.bfloat16
HBM = pl.BlockSpec(memory_space=pltpu.HBM)
VMEM = pl.BlockSpec(memory_space=pltpu.VMEM)
SMEM = pl.BlockSpec(memory_space=pltpu.SMEM)


def swap(block, axis, mask):
    count = lax.axis_size(axis)
    return lax.ppermute(block, axis, [(i, i ^ mask) for i in range(count)])


def shift(block, axis, step):
    count = lax.axis_size(axis)
    route = [(i, i + step) for i in range(count) if 0 <= i + step < count]
    return lax.ppermute(block, axis, route)


def tie(*arrays):
    return lax.optimization_barrier(arrays)


def line_gather(block, axis):
    held = {0: block}
    for step in range(1, lax.axis_size(axis)):
        held[-step] = shift(held[1 - step], axis, 1)
        held[step] = shift(held[step - 1], axis, -1)
    return [held[k] for k in sorted(held)]


def line_routes(count):
    if count == 4:
        near = lambda p: jnp.where(p < 2, 2, 1)
        far = lambda p: jnp.where(p < 2, 3, 0)
        inner = lambda p: (p == 1) | (p == 2)
        outer = lambda p: (p == 0) | (p == 3)
        always = lambda p: p >= 0
        return [
            (lambda p: p, always),
            (lambda p: jnp.bitwise_xor(p, 1), always),
            (near, inner),
            (near, outer),
            (far, inner),
            (far, outer),
        ]
    result = []
    for offset in range(1 - count, count):
        inside = lambda p, offset=offset: (p + offset >= 0) & (p + offset < count)
        result.append((lambda p, offset=offset: p + offset, inside))
    return result


def far_routes(count):
    routes = list(enumerate(line_routes(count)))
    if count == 4:
        return routes[:4], routes[4:], routes[4][1][0]
    far = lambda p: count - 1 - p
    early, late = [], []
    for n, (owner, held) in routes:
        is_far = lambda p, owner=owner: owner(p) == far(p)
        early.append((n, (owner, lambda p, held=held, is_far=is_far: held(p) & ~is_far(p))))
        late.append((n, (owner, lambda p, held=held, is_far=is_far: held(p) & is_far(p))))
    return early, late, far


MIDDLE = [(1, 2), (2, 1)]
OUTWARD = [(1, 0), (2, 3)]


def gather_heads(keep, take, others):
    send = lambda held, route: lax.ppermute(held, "col", route)
    join = lambda *held: jnp.concatenate(held, axis=0)
    keep_pair, keep_near = swap(keep, "col", 1), send(keep, MIDDLE)
    take_pair, take_near = swap(take, "col", 1), send(take, MIDDLE)
    keep_pair, keep_near, take_pair, take_near, others = tie(
        keep_pair, keep_near, take_pair, take_near, others
    )
    pair, near = join(keep_pair, take_pair), join(keep_near, take_near)
    near_end, far = send(near, OUTWARD), send(pair, MIDDLE)
    near_end, far = tie(near_end, far)
    return [join(keep, take), pair, near, near_end, far, send(far, OUTWARD)], others


def gather_both(tokens, weights):
    send = lambda held, route: lax.ppermute(held, "col", route)
    first, second = weights
    pair, near = swap(tokens, "col", 1), send(tokens, MIDDLE)
    first_y, second_x = swap(first, "row", 4), swap(second, "row", 2)
    other = lambda held: swap(held, "row", 1)
    peer = other(tokens)
    pair, near, first_y, second_x, first, second = tie(
        pair, near, first_y, second_x, first, second
    )
    near_end, far = send(near, OUTWARD), send(pair, MIDDLE)
    first_x, second_y = swap(first, "row", 2), swap(second, "row", 4)
    near_end, far, first_x, second_y, first_y, second_x, pair, near, peer = tie(
        near_end, far, first_x, second_y, first_y, second_x, pair, near, peer
    )
    far_end = send(far, OUTWARD)
    first_d, second_d = swap(first_y, "row", 2), swap(second_x, "row", 4)
    far_end, first_d, second_d = tie(far_end, first_d, second_d)
    peers = [peer, other(pair), other(near), other(near_end), other(far), other(far_end)]
    held = [
        {0: first, 4: first_y, 2: first_x, 6: first_d},
        {0: second, 2: second_x, 4: second_y, 6: second_d},
    ]
    return [tokens, pair, near, near_end, far, far_end], peers, held


def direct_gather(block, axis, masks):
    return {mask: swap(block, axis, mask) if mask else block for mask in masks}


def doubling_gather(block, axis, masks):
    held = {0: block}
    for mask in masks:
        for known in list(held):
            held[known | mask] = swap(held[known], axis, mask)
    return held


def in_order(pieces, axis):
    masks, place = sorted(pieces[0]), lax.axis_index(axis)
    core = place % 2
    joined = jnp.stack([jnp.stack([piece[k] for k in masks]) for piece in pieces], axis=1)
    joined = joined[jnp.bitwise_xor(jnp.arange(len(masks)), place // 2)]
    joined = jnp.where(core == 0, joined, joined[:, ::-1])
    return joined.reshape(joined.shape[0], -1, joined.shape[-1])


def cost(us):
    return pl.CostEstimate(flops=int(us * 1.15e9), bytes_accessed=0, transcendentals=0)


def call(kernel, outs, in_specs, scratch, estimate, out_specs=None, vmem=16):
    if out_specs is None:
        out_specs = jax.tree.map(lambda _: VMEM, outs)
    return pl.pallas_call(
        kernel,
        out_shape=outs,
        in_specs=in_specs,
        out_specs=out_specs,
        scratch_shapes=scratch,
        cost_estimate=estimate,
        compiler_params=pltpu.CompilerParams(vmem_limit_bytes=vmem * 1024 * 1024),
    )


def line_copies(refs, routes, place, target, sems, act):
    for n, (ref, (owner, held)) in enumerate(zip(refs, routes)):

        @pl.when(held(place))
        def _():
            copy = pltpu.make_async_copy(ref, target(owner(place)), sems.at[n])
            getattr(copy, act)()


def mod_kernel(cond_ref, w_ref, out_ref):
    requests, groups, width = cond_ref.shape[0], w_ref.shape[0], w_ref.shape[2]
    request = lax.axis_index("row") // 2
    values = jnp.concatenate(
        [cond_ref[pl.ds(jnp.bitwise_xor(request, k), 1), :] for k in range(requests)], axis=0
    )
    activated = (values * (1.0 / (1.0 + jnp.exp(-values)))).astype(BF16)
    out_ref[...] = jnp.zeros(out_ref.shape, F32)
    for group in range(groups):
        out_ref[:, group, :width] = jnp.dot(
            activated, w_ref[group], preferred_element_type=F32
        )


def pack_kernel(qkv_ref, kv_ref, keep_ref, give_ref):
    half = keep_ref.shape[1] // 5
    first = lax.axis_index("row") % 2 == 0
    for k in range(5):
        rows = qkv_ref[k] if k < 3 else kv_ref[:, k - 3]
        low, high = rows[:, :half], rows[:, half:]
        here = slice(k * half, (k + 1) * half)
        keep_ref[:, here] = jnp.where(first, low, high)
        give_ref[:, here] = jnp.where(first, high, low)


def stats_kernel(img_ref, txt_ref, out_ref):
    img = img_ref.shape[1]
    txt = txt_ref.shape[0]
    out_ref[...] = jnp.zeros(out_ref.shape, F32)
    for values, low, high in (
        (img_ref[...].astype(F32), 0, img),
        (txt_ref[...].astype(F32).T, img, img + txt),
    ):
        out_ref[0:1, low:high] = jnp.sum(values, axis=0, keepdims=True)
        out_ref[1:2, low:high] = jnp.sum(values * values, axis=0, keepdims=True)


def norm_kernel(total, img_ref, txt_ref, stats_ref, mod_ref, out_ref):
    width, img = img_ref.shape
    txt = txt_ref.shape[0]
    stats = stats_ref[...] / total
    row = lax.broadcasted_iota(jnp.int32, stats.shape, 0)
    average = stats[0:1]
    inverse = lax.rsqrt(stats[1:2] - average * average + EPS_NORM)
    columns = jnp.where(row == 0, average, inverse).T
    chunk = 128
    if out_ref.shape[1] > width:
        out_ref[:, width:] = jnp.zeros((img + txt, out_ref.shape[1] - width), BF16)
    for low in range(0, img + txt, chunk):
        for start in range(0, width, chunk):
            stop = min(start + chunk, width)
            if low < img:
                high = min(low + chunk, img)
                values, group = img_ref[start:stop, low:high].T, 0
            else:
                high = min(low + chunk, img + txt)
                values, group = txt_ref[low - img : high - img, start:stop], 3
            normed = (values.astype(F32) - columns[low:high, 0:1]) * columns[low:high, 1:2]
            stretch = 1.0 + mod_ref[group + 1 : group + 2, start:stop]
            normed = normed * stretch + mod_ref[group : group + 1, start:stop]
            out_ref[low:high, start:stop] = normed.astype(BF16)


def attend(img, txt, head, length_ref, queries, keys, values, out_refs):
    width = queries.shape[1]
    place = lax.axis_index("row")
    side = lax.rem(place, 2)
    slot = lax.broadcasted_iota(jnp.int32, (2 * txt, 1), 0)
    other = (slot >= txt).astype(jnp.int32)
    owner = jnp.where(other == 1, 1 - side, side)
    allowed = owner * txt + slot - other * txt < length_ref[place // 2]
    turned = values.T
    ones = jnp.ones((16, keys.shape[0]), BF16)
    rows = [
        jnp.concatenate([turned[k * head : (k + 1) * head], ones], axis=0)
        for k in range(width // head)
    ]
    lane = lax.broadcasted_iota(jnp.int32, (1, width), 1) // head
    step = 256 if img % 256 == 0 else img

    def scores_of(k, low):
        query = jnp.where(lane == k, queries[low : low + step], 0.0).astype(BF16)
        score = lax.dot_general(
            keys, query, (((1,), (1,)), ((), ())), preferred_element_type=F32
        )
        tail = jnp.where(allowed, score[2 * img :], -1e30)
        return jnp.concatenate([score[: 2 * img], tail], axis=0)

    work = [(k, low) for low in range(0, 2 * img, step) for k in range(width // head)]
    ahead = scores_of(*work[0])
    for n, (k, low) in enumerate(work):
        scores = ahead
        if n + 1 < len(work):
            ahead = scores_of(*work[n + 1])
        weights = jnp.exp(scores - jnp.max(scores, axis=0, keepdims=True)).astype(BF16)
        mixed = jnp.dot(rows[k], weights, preferred_element_type=F32)
        out_ref, at = out_refs[low // img], low % img
        out_ref[k * head : (k + 1) * head, at : at + step] = (
            mixed[:head] / mixed[head : head + 1]
        ).astype(BF16)


def project_kernel(routes, masks, img, head, length_ref, q_gain_ref, k_gain_ref, *refs):
    lines = refs[: len(routes)], refs[len(routes) : 2 * len(routes)]
    refs = refs[2 * len(routes) :]
    n_blocks = 2 * len(masks) if masks else 1
    blocks, refs = refs[:n_blocks], refs[n_blocks:]
    outs, refs = refs[:2], refs[2:]
    x_ref, w_ref, img_ref, txt_ref, q_ref, k_ref, v_ref, sems_x, sems_w = refs
    tokens, wide = lines[0][0].shape
    txt = tokens - img
    count = x_ref.shape[1] // wide
    half = img_ref.shape[1] // 3
    place, col = lax.axis_index("row"), lax.axis_index("col")
    chip, core = place // 2, lax.rem(place, 2)

    def copy_line(n, act):
        for k, (low, high, to) in enumerate(
            ((0, img, n * img), (img, tokens, 2 * img + n * txt))
        ):
            parts = [ref.at[pl.ds(low, high - low)] for ref in lines[n]]
            target = lambda owner: x_ref.at[
                pl.ds(to, high - low), pl.ds(pl.multiple_of(owner * wide, 128), wide)
            ]
            line_copies(parts, routes, col, target, sems_x.at[n, k], act)

    copy_line(0, "start")
    stages = [[], []]
    if not masks:
        width = blocks[0].shape[1]
        for k in range(count):
            target = w_ref.at[pl.ds(k * wide, width)]
            stages[0].append(pltpu.make_async_copy(blocks[0].at[k], target, sems_w.at[0, k]))
    else:
        depth = blocks[0].shape[0]
        width = 2 * depth
        for k in range(count):
            for piece in range(2):
                row = jnp.bitwise_xor(chip, k) * wide + jnp.where(core == piece, 0, depth)
                target = w_ref.at[pl.ds(pl.multiple_of(row, 16), depth)]
                ref = blocks[piece * len(masks) + k]
                copy = pltpu.make_async_copy(ref, target, sems_w.at[piece, k])
                stages[2 * k // count].append(copy)
    for copy in stages[0] + stages[1]:
        copy.start()
    copy_line(1, "start")
    for k in range(count):
        if wide > width:
            w_ref[k * wide + width : (k + 1) * wide] = jnp.zeros((wide - width, 5 * half), BF16)
    row = lax.broadcasted_iota(jnp.int32, (half, half), 0) // head
    column = lax.broadcasted_iota(jnp.int32, (half, half), 1) // head
    mean_of = jnp.where(row == column, 1.0 / head, 0.0).astype(BF16)

    def head_norm(values, gain):
        square = values * values
        mean_square = jnp.zeros_like(square)
        for _ in range(2):
            term = square.astype(BF16)
            mean_square += jnp.dot(term, mean_of, preferred_element_type=F32)
            square = square - term.astype(F32)
        return (values * lax.rsqrt(mean_square + EPS_NORM) * gain).astype(BF16)

    copy_line(0, "wait")
    depth = count // 2 * wide
    for k in range(2):
        for copy in stages[k]:
            copy.wait()
        if not masks:
            here = pl.ds(k * depth, depth)
        else:
            here = pl.ds(pl.multiple_of(jnp.bitwise_xor(2 * chip // count, k) * depth, 128), depth)
        term = jnp.dot(x_ref[:img, here], w_ref[here, : 3 * half], preferred_element_type=F32)
        img_ref[:img] = term if k == 0 else img_ref[:img] + term
    copy_line(1, "wait")
    img_ref[img:] = jnp.dot(
        x_ref[img : 2 * img], w_ref[:, : 3 * half], preferred_element_type=F32
    )
    txt_ref[...] = jnp.dot(x_ref[2 * img :], w_ref[:, 3 * half :], preferred_element_type=F32)
    scaling = head ** (-0.5)
    wide_gain = lambda gain: jnp.concatenate([gain] * (half // head), axis=1)
    queries = head_norm(img_ref[:, :half], wide_gain(q_gain_ref[...]))
    q_ref[...] = (queries.astype(F32) * scaling).astype(BF16)
    k_ref[: 2 * img] = head_norm(img_ref[:, half : 2 * half], wide_gain(k_gain_ref[0:1]))
    k_ref[2 * img :] = head_norm(txt_ref[:, :half], wide_gain(k_gain_ref[1:2]))
    v_ref[: 2 * img] = img_ref[:, 2 * half :].astype(BF16)
    v_ref[2 * img :] = txt_ref[:, half:].astype(BF16)
    attend(img, txt, head, length_ref, q_ref[...], k_ref[...], v_ref[...], outs)


def place_heads(line, routes, col, target, sems):
    core = lax.rem(lax.axis_index("row"), 2)
    size = line[0].shape[0] // 2
    for act in ("start", "wait"):
        for n in range(2):
            rows = pl.ds(pl.multiple_of(jnp.where(core == n, 0, size), 16), size)
            parts = [ref.at[pl.ds(n * size, size)] for ref in line]
            line_copies(parts, routes, col, lambda owner: target(owner, rows), sems.at[n], act)


def early_kernel(routes, far, masks, mod_ref, *refs):
    n_lines = len(routes)
    line, refs = refs[:n_lines], refs[n_lines:]
    weights, refs = refs[:2], refs[2:]
    sum_ref, far_ref, gain_ref, const_ref, a_ref, w_ref, sems_a, sems_w = refs
    width = sum_ref.shape[0]
    count = a_ref.shape[0]
    depth = w_ref.shape[2]
    place, col = lax.axis_index("row"), lax.axis_index("col")
    copies = []
    for k, ref in enumerate(weights):
        for n, mask in enumerate(masks):
            target = w_ref.at[jnp.bitwise_xor(place, mask + k)]
            source = ref.at[pl.ds(n * w_ref.shape[1], w_ref.shape[1])]
            copies.append(pltpu.make_async_copy(source, target, sems_w.at[k, n]))
    for copy in copies:
        copy.start()
    place_heads(line, routes, col, lambda owner, rows: a_ref.at[owner, rows], sems_a)
    for copy in copies:
        copy.wait()
    per_col = w_ref.shape[0] // count
    farthest = far(col)
    total = None
    for k in range(1, count):
        owner = lax.rem(farthest + k, count)
        for n in range(per_col):
            term = jnp.dot(
                w_ref[owner * per_col + n, :width],
                a_ref[owner, n * depth : (n + 1) * depth],
                preferred_element_type=F32,
            )
            total = term if total is None else total + term
    sum_ref[...] = total
    for n in range(per_col):
        far_ref[:, n * depth : (n + 1) * depth] = w_ref[farthest * per_col + n, :width]

    patch = gain_ref.shape[0] // 3
    slab = width // per_col
    consts = jnp.zeros((8, patch), F32)
    row = lax.broadcasted_iota(jnp.int32, (8, patch), 0)
    for n in range(per_col):
        for k in range((w_ref.shape[1] - width) // patch):
            low, high = k * depth, min((k + 1) * depth, slab)
            if low >= high:
                continue
            piece = w_ref[col * per_col + n, width + k * patch : width + (k + 1) * patch]
            here = slice(n * slab + low, n * slab + high)
            linear = piece[:, : high - low].astype(F32)
            gained = linear * (1.0 + mod_ref[6:7, here])
            both = (jnp.sum(gained, axis=1, keepdims=True), linear * mod_ref[5:6, here])
            both = jnp.concatenate(
                [jnp.broadcast_to(both[0], (patch, 128)), jnp.broadcast_to(
                    jnp.sum(both[1], axis=1, keepdims=True), (patch, 128))], axis=0
            ).T
            consts += jnp.where(
                row == 2, both[:8, :patch], jnp.where(row == 3, both[:8, patch:], 0.0)
            )
            for t in range(3):
                term = gained.astype(BF16)
                gain_ref[t * patch : (t + 1) * patch, here] = term
                gained = gained - term.astype(F32)
    const_ref[...] = jnp.zeros(const_ref.shape, F32)
    const_ref[:, :patch] = consts


def late_kernel(routes, mod_ref, x_ref, sum_ref, far_ref, gain_ref, const_ref, *refs):
    n_lines = len(routes)
    line, (out_ref, a_ref, sems_a) = refs[:n_lines], refs[n_lines:]
    width, tokens = x_ref.shape
    col = lax.axis_index("col")
    place_heads(line, routes, col, lambda owner, rows: a_ref.at[rows], sems_a)
    gate = mod_ref[...].T[:width, 2:3]
    projected = sum_ref[...] + jnp.dot(far_ref[...], a_ref[...], preferred_element_type=F32)
    updated = (x_ref[...].astype(F32) + gate * projected).astype(BF16)
    wide = updated.astype(F32)
    sums = jnp.sum(wide, axis=0, keepdims=True)
    squares = jnp.sum(wide * wide, axis=0, keepdims=True)
    patch = gain_ref.shape[0] // 3
    terms = jnp.dot(gain_ref[...], updated, preferred_element_type=F32)
    out_ref[:patch] = terms[:patch] + terms[patch : 2 * patch] + terms[2 * patch :]
    row = lax.broadcasted_iota(jnp.int32, (8, tokens), 0)
    out_ref[patch:] = jnp.where(row == 0, sums, jnp.where(row == 1, squares, const_ref[...]))


def sigma_of(step_now):
    remain = 1.0 - step_now.astype(F32) / STEPS
    return 3.0 * remain / (1.0 + 2.0 * remain)


def per_device(
    hidden_img,
    hidden_txt,
    text_len,
    step_index,
    latent,
    cond,
    mod_weight,
    qkv_weight,
    kv_text_weight,
    q_gain,
    k_gain,
    out_weight,
    final_weight,
):
    row_count, col_count = lax.axis_size("row"), lax.axis_size("col")
    request = lax.axis_index("row") // 2
    requests = cond.shape[0]
    img, width = hidden_img.shape
    txt = hidden_txt.shape[0]
    head = q_gain.shape[0]
    part_cols = qkv_weight.shape[2]
    half = part_cols // 2
    full_width = width * col_count

    wide = -(-width // 128) * 128
    room = -(-txt // 128) * 128
    tokens = img + room
    mod_part = call(
        mod_kernel,
        jax.ShapeDtypeStruct((requests, 8, wide), F32),
        [VMEM, VMEM],
        [],
        cost(2),
    )(cond, jnp.moveaxis(mod_weight, 1, 0))
    mod_own = mod_part[0]
    for k in range(1, requests):
        mod_own = mod_own + swap(mod_part[k], "row", 2 * k)
    stats = call(
        stats_kernel,
        jax.ShapeDtypeStruct((8, tokens), F32),
        [VMEM, VMEM],
        [],
        cost(1),
    )(hidden_img.T, hidden_txt)
    stats = sum((swap(stats, "col", mask) for mask in range(1, col_count)), stats)

    chip_masks = [1 << bit for bit in range(1, row_count.bit_length() - 1)]
    packed = call(
        pack_kernel,
        (jax.ShapeDtypeStruct((qkv_weight.shape[0], 5 * half), BF16),) * 2,
        [VMEM, VMEM],
        [],
        cost(2),
        (VMEM, VMEM),
    )(jnp.moveaxis(qkv_weight, 1, 0), kv_text_weight)
    packed = packed[0], swap(packed[1], "row", 1)
    *packed, mod_own = tie(*packed, mod_own)
    mod_own = mod_own + swap(mod_own, "row", 1)
    ready = call(
        functools.partial(norm_kernel, full_width),
        jax.ShapeDtypeStruct((img + txt, wide), BF16),
        [VMEM] * 4,
        [],
        cost(1),
    )(hidden_img.T, hidden_txt, stats, mod_own)
    routes = line_routes(col_count)
    small = col_count == 4 and row_count == 8
    if small:
        line, peer_line, gathered = gather_both(ready, packed)
    else:
        line = line_gather(ready, "col")
        peer_line = [swap(part, "row", 1) for part in line]
        gathered = [doubling_gather(part, "row", chip_masks) for part in packed]

    if gathered[0][0].shape[0] % 16 == 0:
        masks = sorted(gathered[0])
        blocks = [piece[k] for piece in gathered for k in masks]
    else:
        masks, blocks = [], [in_order(gathered, "row")]
    heads_out = jax.ShapeDtypeStruct((half, img), BF16)
    full_wide = col_count * wide
    projected = call(
        functools.partial(project_kernel, routes, masks, img, head),
        (heads_out, heads_out),
        [SMEM, VMEM, VMEM] + [HBM] * (2 * len(routes) + len(blocks)),
        [
            pltpu.VMEM((2 * (img + txt), full_wide), BF16),
            pltpu.VMEM((full_wide, 5 * half), BF16),
            pltpu.VMEM((2 * img, 3 * half), F32),
            pltpu.VMEM((2 * txt, 2 * half), F32),
            pltpu.VMEM((2 * img, half), BF16),
            *[pltpu.VMEM((2 * (img + txt), half), BF16)] * 2,
            pltpu.SemaphoreType.DMA((2, 2, len(routes))),
            pltpu.SemaphoreType.DMA((2, col_count)),
        ],
        cost(PROJECT),
        (VMEM, VMEM),
        vmem=PROJECT_MIB,
    )(text_len, q_gain[None], k_gain, *line, *peer_line, *blocks)
    head_depth, patch = final_weight.shape
    depth = out_weight.shape[0]
    folds = -(-head_depth // depth)
    tail = jnp.pad(final_weight.T, ((0, 0), (0, folds * depth - head_depth)))
    tail = jnp.swapaxes(tail.reshape(patch, folds, depth), 0, 1).reshape(folds * patch, depth)
    out_packed = jnp.concatenate([out_weight.T, tail], axis=0)
    masks = list(range(0, row_count, 2))
    out_blocks = direct_gather(out_packed, "row", masks)

    keep, give, *others = tie(*projected, *[out_blocks[k] for k in masks[1:]])
    own_rows = jnp.concatenate([out_packed, *others], axis=0)
    other_rows = swap(own_rows, "row", 1)
    take = swap(give, "row", 1)
    if small:
        line, other_rows = gather_heads(keep, take, other_rows)
    else:
        line = line_gather(jnp.concatenate([keep, take], axis=0), "col")
    early, late, far = far_routes(col_count)
    sems = pltpu.SemaphoreType.DMA((2, len(routes)))
    bundle = call(
        functools.partial(early_kernel, [route for _, route in early], far, masks),
        (
            jax.ShapeDtypeStruct((width, img), F32),
            jax.ShapeDtypeStruct((width, part_cols), BF16),
            jax.ShapeDtypeStruct((3 * patch, width), BF16),
            jax.ShapeDtypeStruct((8, img), F32),
        ),
        [VMEM] + [HBM] * (len(early) + 2),
        [
            pltpu.VMEM((col_count, part_cols, img), BF16),
            pltpu.VMEM((row_count,) + out_packed.shape, BF16),
            sems,
            pltpu.SemaphoreType.DMA((2, len(masks))),
        ],
        cost(5),
        (VMEM,) * 4,
        vmem=EARLY,
    )(
        mod_own,
        *[line[k] for k, _ in early],
        own_rows,
        other_rows,
    )
    partial_sum = call(
        functools.partial(late_kernel, [route for _, route in late]),
        jax.ShapeDtypeStruct((patch + 8, img), F32),
        [VMEM] * 6 + [HBM] * len(late),
        [pltpu.VMEM((part_cols, img), BF16), sems],
        cost(3),
        vmem=24,
    )(mod_own, hidden_img.T, *bundle, *[line[k] for k, _ in late])
    mask = 1
    while mask < col_count:
        partial_sum = partial_sum + swap(partial_sum, "col", mask)
        mask *= 2
    average = partial_sum[patch : patch + 1] / full_width
    mean_square = partial_sum[patch + 1 : patch + 2] / full_width
    inverse = lax.rsqrt(mean_square - average * average + EPS_NORM)
    gains = partial_sum[patch + 2, :patch][:, None]
    shifts = partial_sum[patch + 3, :patch][:, None]
    velocity = inverse * (partial_sum[:patch] - average * gains) + shifts
    step_now = lax.dynamic_index_in_dim(step_index, request, 0, keepdims=False)
    sigma_step = sigma_of(step_now + 1) - sigma_of(step_now)
    latent_next = latent.T + sigma_step * velocity
    return (velocity.T, latent_next.T)


def solution(mesh):
    in_specs = (
        P("row", "col"),
        P("row", "col"),
        P(),
        P(),
        P("row", None),
        P(None, "row"),
        P("row", None, "col"),
        P("row", None, "col"),
        P("row", None, "col"),
        P(),
        P(),
        P("row", "col"),
        P("row", None),
    )
    out_specs = (P("row", None), P("row", None))
    return jax.shard_map(
        per_device, mesh=mesh, in_specs=in_specs, out_specs=out_specs, check_vma=False
    )
```

```python
import functools

import jax
import jax.numpy as jnp
from jax import lax
from jax.experimental import pallas as pl
from jax.experimental.pallas import tpu as pltpu
from jax.sharding import PartitionSpec as P

STEPS = 28
EPS_NORM = 1e-06
PROJECT_MIB = 44
PROJECT = 20
EARLY = 32
F32 = jnp.float32
BF16 = jnp.bfloat16
HBM = pl.BlockSpec(memory_space=pltpu.HBM)
VMEM = pl.BlockSpec(memory_space=pltpu.VMEM)
SMEM = pl.BlockSpec(memory_space=pltpu.SMEM)


def swap(block, axis, mask):
    count = lax.axis_size(axis)
    return lax.ppermute(block, axis, [(i, i ^ mask) for i in range(count)])


def shift(block, axis, step):
    count = lax.axis_size(axis)
    route = [(i, i + step) for i in range(count) if 0 <= i + step < count]
    return lax.ppermute(block, axis, route)


def tie(*arrays):
    return lax.optimization_barrier(arrays)


def line_gather(block, axis):
    held = {0: block}
    for step in range(1, lax.axis_size(axis)):
        held[-step] = shift(held[1 - step], axis, 1)
        held[step] = shift(held[step - 1], axis, -1)
    return [held[k] for k in sorted(held)]


def line_routes(count):
    if count == 4:
        near = lambda p: jnp.where(p < 2, 2, 1)
        far = lambda p: jnp.where(p < 2, 3, 0)
        inner = lambda p: (p == 1) | (p == 2)
        outer = lambda p: (p == 0) | (p == 3)
        always = lambda p: p >= 0
        return [
            (lambda p: p, always),
            (lambda p: jnp.bitwise_xor(p, 1), always),
            (near, inner),
            (near, outer),
            (far, inner),
            (far, outer),
        ]
    result = []
    for offset in range(1 - count, count):
        inside = lambda p, offset=offset: (p + offset >= 0) & (p + offset < count)
        result.append((lambda p, offset=offset: p + offset, inside))
    return result


def far_routes(count):
    routes = list(enumerate(line_routes(count)))
    if count == 4:
        return routes[:4], routes[4:], routes[4][1][0]
    far = lambda p: count - 1 - p
    early, late = [], []
    for n, (owner, held) in routes:
        is_far = lambda p, owner=owner: owner(p) == far(p)
        early.append((n, (owner, lambda p, held=held, is_far=is_far: held(p) & ~is_far(p))))
        late.append((n, (owner, lambda p, held=held, is_far=is_far: held(p) & is_far(p))))
    return early, late, far


MIDDLE = [(1, 2), (2, 1)]
OUTWARD = [(1, 0), (2, 3)]


def gather_heads(keep, take, others):
    send = lambda held, route: lax.ppermute(held, "col", route)
    join = lambda *held: jnp.concatenate(held, axis=0)
    keep_pair, keep_near = swap(keep, "col", 1), send(keep, MIDDLE)
    take_pair, take_near = swap(take, "col", 1), send(take, MIDDLE)
    keep_pair, keep_near, take_pair, take_near, others = tie(
        keep_pair, keep_near, take_pair, take_near, others
    )
    pair, near = join(keep_pair, take_pair), join(keep_near, take_near)
    near_end, far = send(near, OUTWARD), send(pair, MIDDLE)
    near_end, far = tie(near_end, far)
    return [join(keep, take), pair, near, near_end, far, send(far, OUTWARD)], others


def gather_both(tokens, weights):
    send = lambda held, route: lax.ppermute(held, "col", route)
    first, second = weights
    pair, near = swap(tokens, "col", 1), send(tokens, MIDDLE)
    first_y, second_x = swap(first, "row", 4), swap(second, "row", 2)
    other = lambda held: swap(held, "row", 1)
    peer = other(tokens)
    pair, near, first_y, second_x, first, second = tie(
        pair, near, first_y, second_x, first, second
    )
    near_end, far = send(near, OUTWARD), send(pair, MIDDLE)
    first_x, second_y = swap(first, "row", 2), swap(second, "row", 4)
    near_end, far, first_x, second_y, first_y, second_x, pair, near, peer = tie(
        near_end, far, first_x, second_y, first_y, second_x, pair, near, peer
    )
    far_end = send(far, OUTWARD)
    first_d, second_d = swap(first_y, "row", 2), swap(second_x, "row", 4)
    far_end, first_d, second_d = tie(far_end, first_d, second_d)
    peers = [peer, other(pair), other(near), other(near_end), other(far), other(far_end)]
    held = [
        {0: first, 4: first_y, 2: first_x, 6: first_d},
        {0: second, 2: second_x, 4: second_y, 6: second_d},
    ]
    return [tokens, pair, near, near_end, far, far_end], peers, held


def direct_gather(block, axis, masks):
    return {mask: swap(block, axis, mask) if mask else block for mask in masks}


def doubling_gather(block, axis, masks):
    held = {0: block}
    for mask in masks:
        for known in list(held):
            held[known | mask] = swap(held[known], axis, mask)
    return held


def in_order(pieces, axis):
    masks, place = sorted(pieces[0]), lax.axis_index(axis)
    core = place % 2
    joined = jnp.stack([jnp.stack([piece[k] for k in masks]) for piece in pieces], axis=1)
    joined = joined[jnp.bitwise_xor(jnp.arange(len(masks)), place // 2)]
    joined = jnp.where(core == 0, joined, joined[:, ::-1])
    return joined.reshape(joined.shape[0], -1, joined.shape[-1])


def cost(us):
    return pl.CostEstimate(flops=int(us * 1.15e9), bytes_accessed=0, transcendentals=0)


def call(kernel, outs, in_specs, scratch, estimate, out_specs=None, vmem=16):
    if out_specs is None:
        out_specs = jax.tree.map(lambda _: VMEM, outs)
    return pl.pallas_call(
        kernel,
        out_shape=outs,
        in_specs=in_specs,
        out_specs=out_specs,
        scratch_shapes=scratch,
        cost_estimate=estimate,
        compiler_params=pltpu.CompilerParams(vmem_limit_bytes=vmem * 1024 * 1024),
    )


def line_copies(refs, routes, place, target, sems, act):
    for n, (ref, (owner, held)) in enumerate(zip(refs, routes)):

        @pl.when(held(place))
        def _():
            copy = pltpu.make_async_copy(ref, target(owner(place)), sems.at[n])
            getattr(copy, act)()


def mod_kernel(cond_ref, w_ref, out_ref):
    requests, groups, width = cond_ref.shape[0], w_ref.shape[0], w_ref.shape[2]
    request = lax.axis_index("row") // 2
    values = jnp.concatenate(
        [cond_ref[pl.ds(jnp.bitwise_xor(request, k), 1), :] for k in range(requests)], axis=0
    )
    activated = (values * (1.0 / (1.0 + jnp.exp(-values)))).astype(BF16)
    out_ref[...] = jnp.zeros(out_ref.shape, F32)
    for group in range(groups):
        out_ref[:, group, :width] = jnp.dot(
            activated, w_ref[group], preferred_element_type=F32
        )


def pack_kernel(qkv_ref, kv_ref, keep_ref, give_ref):
    half = keep_ref.shape[1] // 5
    first = lax.axis_index("row") % 2 == 0
    for k in range(5):
        rows = qkv_ref[k] if k < 3 else kv_ref[:, k - 3]
        low, high = rows[:, :half], rows[:, half:]
        here = slice(k * half, (k + 1) * half)
        keep_ref[:, here] = jnp.where(first, low, high)
        give_ref[:, here] = jnp.where(first, high, low)


def stats_kernel(img_ref, txt_ref, out_ref):
    img = img_ref.shape[1]
    txt = txt_ref.shape[0]
    out_ref[...] = jnp.zeros(out_ref.shape, F32)
    for values, low, high in (
        (img_ref[...].astype(F32), 0, img),
        (txt_ref[...].astype(F32).T, img, img + txt),
    ):
        out_ref[0:1, low:high] = jnp.sum(values, axis=0, keepdims=True)
        out_ref[1:2, low:high] = jnp.sum(values * values, axis=0, keepdims=True)


def norm_kernel(total, img_ref, txt_ref, stats_ref, mod_ref, out_ref):
    width, img = img_ref.shape
    txt = txt_ref.shape[0]
    stats = stats_ref[...] / total
    row = lax.broadcasted_iota(jnp.int32, stats.shape, 0)
    average = stats[0:1]
    inverse = lax.rsqrt(stats[1:2] - average * average + EPS_NORM)
    columns = jnp.where(row == 0, average, inverse).T
    chunk = 128
    if out_ref.shape[1] > width:
        out_ref[:, width:] = jnp.zeros((img + txt, out_ref.shape[1] - width), BF16)
    for low in range(0, img + txt, chunk):
        for start in range(0, width, chunk):
            stop = min(start + chunk, width)
            if low < img:
                high = min(low + chunk, img)
                values, group = img_ref[start:stop, low:high].T, 0
            else:
                high = min(low + chunk, img + txt)
                values, group = txt_ref[low - img : high - img, start:stop], 3
            normed = (values.astype(F32) - columns[low:high, 0:1]) * columns[low:high, 1:2]
            stretch = 1.0 + mod_ref[group + 1 : group + 2, start:stop]
            normed = normed * stretch + mod_ref[group : group + 1, start:stop]
            out_ref[low:high, start:stop] = normed.astype(BF16)


def attend(img, txt, head, length_ref, queries, keys, values, out_refs):
    width = queries.shape[1]
    place = lax.axis_index("row")
    side = lax.rem(place, 2)
    slot = lax.broadcasted_iota(jnp.int32, (2 * txt, 1), 0)
    other = (slot >= txt).astype(jnp.int32)
    owner = jnp.where(other == 1, 1 - side, side)
    allowed = owner * txt + slot - other * txt < length_ref[place // 2]
    turned = values.T
    ones = jnp.ones((16, keys.shape[0]), BF16)
    rows = [
        jnp.concatenate([turned[k * head : (k + 1) * head], ones], axis=0)
        for k in range(width // head)
    ]
    lane = lax.broadcasted_iota(jnp.int32, (1, width), 1) // head
    step = 512 if img % 512 == 0 else img

    def scores_of(k, low):
        query = jnp.where(lane == k, queries[low : low + step], 0.0).astype(BF16)
        score = lax.dot_general(
            keys, query, (((1,), (1,)), ((), ())), preferred_element_type=F32
        )
        tail = jnp.where(allowed, score[2 * img :], -1e30)
        return jnp.concatenate([score[: 2 * img], tail], axis=0)

    work = [(k, low) for low in range(0, 2 * img, step) for k in range(width // head)]
    ahead = scores_of(*work[0])
    for n, (k, low) in enumerate(work):
        scores = ahead
        if n + 1 < len(work):
            ahead = scores_of(*work[n + 1])
        weights = jnp.exp(scores - jnp.max(scores, axis=0, keepdims=True)).astype(BF16)
        mixed = jnp.dot(rows[k], weights, preferred_element_type=F32)
        out_ref, at = out_refs[low // img], low % img
        out_ref[k * head : (k + 1) * head, at : at + step] = (
            mixed[:head] / mixed[head : head + 1]
        ).astype(BF16)


def project_kernel(routes, masks, img, head, length_ref, q_gain_ref, k_gain_ref, *refs):
    lines = refs[: len(routes)], refs[len(routes) : 2 * len(routes)]
    refs = refs[2 * len(routes) :]
    n_blocks = 2 * len(masks) if masks else 1
    blocks, refs = refs[:n_blocks], refs[n_blocks:]
    outs, refs = refs[:2], refs[2:]
    x_ref, w_ref, img_ref, txt_ref, q_ref, k_ref, v_ref, sems_x, sems_w = refs
    tokens, wide = lines[0][0].shape
    txt = tokens - img
    count = x_ref.shape[1] // wide
    half = img_ref.shape[1] // 3
    place, col = lax.axis_index("row"), lax.axis_index("col")
    chip, core = place // 2, lax.rem(place, 2)

    def copy_line(n, act):
        for k, (low, high, to) in enumerate(
            ((0, img, n * img), (img, tokens, 2 * img + n * txt))
        ):
            parts = [ref.at[pl.ds(low, high - low)] for ref in lines[n]]
            target = lambda owner: x_ref.at[
                pl.ds(to, high - low), pl.ds(pl.multiple_of(owner * wide, 128), wide)
            ]
            line_copies(parts, routes, col, target, sems_x.at[n, k], act)

    copy_line(0, "start")
    stages = [[], []]
    if not masks:
        width = blocks[0].shape[1]
        for k in range(count):
            target = w_ref.at[pl.ds(k * wide, width)]
            stages[0].append(pltpu.make_async_copy(blocks[0].at[k], target, sems_w.at[0, k]))
    else:
        depth = blocks[0].shape[0]
        width = 2 * depth
        for k in range(count):
            for piece in range(2):
                row = jnp.bitwise_xor(chip, k) * wide + jnp.where(core == piece, 0, depth)
                target = w_ref.at[pl.ds(pl.multiple_of(row, 16), depth)]
                ref = blocks[piece * len(masks) + k]
                copy = pltpu.make_async_copy(ref, target, sems_w.at[piece, k])
                stages[2 * k // count].append(copy)
    for copy in stages[0] + stages[1]:
        copy.start()
    copy_line(1, "start")
    for k in range(count):
        if wide > width:
            w_ref[k * wide + width : (k + 1) * wide] = jnp.zeros((wide - width, 5 * half), BF16)
    row = lax.broadcasted_iota(jnp.int32, (half, half), 0) // head
    column = lax.broadcasted_iota(jnp.int32, (half, half), 1) // head
    mean_of = jnp.where(row == column, 1.0 / head, 0.0).astype(BF16)

    def head_norm(values, gain):
        square = values * values
        mean_square = jnp.zeros_like(square)
        for _ in range(2):
            term = square.astype(BF16)
            mean_square += jnp.dot(term, mean_of, preferred_element_type=F32)
            square = square - term.astype(F32)
        return (values * lax.rsqrt(mean_square + EPS_NORM) * gain).astype(BF16)

    copy_line(0, "wait")
    depth = count // 2 * wide
    for k in range(2):
        for copy in stages[k]:
            copy.wait()
        if not masks:
            here = pl.ds(k * depth, depth)
        else:
            here = pl.ds(pl.multiple_of(jnp.bitwise_xor(2 * chip // count, k) * depth, 128), depth)
        term = jnp.dot(x_ref[:img, here], w_ref[here, : 3 * half], preferred_element_type=F32)
        img_ref[:img] = term if k == 0 else img_ref[:img] + term
    copy_line(1, "wait")
    img_ref[img:] = jnp.dot(
        x_ref[img : 2 * img], w_ref[:, : 3 * half], preferred_element_type=F32
    )
    txt_ref[...] = jnp.dot(x_ref[2 * img :], w_ref[:, 3 * half :], preferred_element_type=F32)
    scaling = head ** (-0.5)
    wide_gain = lambda gain: jnp.concatenate([gain] * (half // head), axis=1)
    queries = head_norm(img_ref[:, :half], wide_gain(q_gain_ref[...]))
    q_ref[...] = (queries.astype(F32) * scaling).astype(BF16)
    k_ref[: 2 * img] = head_norm(img_ref[:, half : 2 * half], wide_gain(k_gain_ref[0:1]))
    k_ref[2 * img :] = head_norm(txt_ref[:, :half], wide_gain(k_gain_ref[1:2]))
    v_ref[: 2 * img] = img_ref[:, 2 * half :].astype(BF16)
    v_ref[2 * img :] = txt_ref[:, half:].astype(BF16)
    attend(img, txt, head, length_ref, q_ref[...], k_ref[...], v_ref[...], outs)


def place_heads(line, routes, col, target, sems):
    core = lax.rem(lax.axis_index("row"), 2)
    size = line[0].shape[0] // 2
    for act in ("start", "wait"):
        for n in range(2):
            rows = pl.ds(pl.multiple_of(jnp.where(core == n, 0, size), 16), size)
            parts = [ref.at[pl.ds(n * size, size)] for ref in line]
            line_copies(parts, routes, col, lambda owner: target(owner, rows), sems.at[n], act)


def early_kernel(routes, far, masks, mod_ref, *refs):
    n_lines = len(routes)
    line, refs = refs[:n_lines], refs[n_lines:]
    weights, refs = refs[:2], refs[2:]
    sum_ref, far_ref, gain_ref, const_ref, a_ref, w_ref, sems_a, sems_w = refs
    width = sum_ref.shape[0]
    count = a_ref.shape[0]
    depth = w_ref.shape[2]
    place, col = lax.axis_index("row"), lax.axis_index("col")
    copies = []
    for k, ref in enumerate(weights):
        for n, mask in enumerate(masks):
            target = w_ref.at[jnp.bitwise_xor(place, mask + k)]
            source = ref.at[pl.ds(n * w_ref.shape[1], w_ref.shape[1])]
            copies.append(pltpu.make_async_copy(source, target, sems_w.at[k, n]))
    for copy in copies:
        copy.start()
    place_heads(line, routes, col, lambda owner, rows: a_ref.at[owner, rows], sems_a)
    for copy in copies:
        copy.wait()
    per_col = w_ref.shape[0] // count
    farthest = far(col)
    total = None
    for k in range(1, count):
        owner = lax.rem(farthest + k, count)
        for n in range(per_col):
            term = jnp.dot(
                w_ref[owner * per_col + n, :width],
                a_ref[owner, n * depth : (n + 1) * depth],
                preferred_element_type=F32,
            )
            total = term if total is None else total + term
    sum_ref[...] = total
    for n in range(per_col):
        far_ref[:, n * depth : (n + 1) * depth] = w_ref[farthest * per_col + n, :width]

    patch = gain_ref.shape[0] // 3
    slab = width // per_col
    consts = jnp.zeros((8, patch), F32)
    row = lax.broadcasted_iota(jnp.int32, (8, patch), 0)
    for n in range(per_col):
        for k in range((w_ref.shape[1] - width) // patch):
            low, high = k * depth, min((k + 1) * depth, slab)
            if low >= high:
                continue
            piece = w_ref[col * per_col + n, width + k * patch : width + (k + 1) * patch]
            here = slice(n * slab + low, n * slab + high)
            linear = piece[:, : high - low].astype(F32)
            gained = linear * (1.0 + mod_ref[6:7, here])
            both = (jnp.sum(gained, axis=1, keepdims=True), linear * mod_ref[5:6, here])
            both = jnp.concatenate(
                [jnp.broadcast_to(both[0], (patch, 128)), jnp.broadcast_to(
                    jnp.sum(both[1], axis=1, keepdims=True), (patch, 128))], axis=0
            ).T
            consts += jnp.where(
                row == 2, both[:8, :patch], jnp.where(row == 3, both[:8, patch:], 0.0)
            )
            for t in range(3):
                term = gained.astype(BF16)
                gain_ref[t * patch : (t + 1) * patch, here] = term
                gained = gained - term.astype(F32)
    const_ref[...] = jnp.zeros(const_ref.shape, F32)
    const_ref[:, :patch] = consts


def late_kernel(routes, mod_ref, x_ref, sum_ref, far_ref, gain_ref, const_ref, *refs):
    n_lines = len(routes)
    line, (out_ref, a_ref, sems_a) = refs[:n_lines], refs[n_lines:]
    width, tokens = x_ref.shape
    col = lax.axis_index("col")
    place_heads(line, routes, col, lambda owner, rows: a_ref.at[rows], sems_a)
    gate = mod_ref[...].T[:width, 2:3]
    projected = sum_ref[...] + jnp.dot(far_ref[...], a_ref[...], preferred_element_type=F32)
    updated = (x_ref[...].astype(F32) + gate * projected).astype(BF16)
    wide = updated.astype(F32)
    sums = jnp.sum(wide, axis=0, keepdims=True)
    squares = jnp.sum(wide * wide, axis=0, keepdims=True)
    patch = gain_ref.shape[0] // 3
    terms = jnp.dot(gain_ref[...], updated, preferred_element_type=F32)
    out_ref[:patch] = terms[:patch] + terms[patch : 2 * patch] + terms[2 * patch :]
    row = lax.broadcasted_iota(jnp.int32, (8, tokens), 0)
    out_ref[patch:] = jnp.where(row == 0, sums, jnp.where(row == 1, squares, const_ref[...]))


def sigma_of(step_now):
    remain = 1.0 - step_now.astype(F32) / STEPS
    return 3.0 * remain / (1.0 + 2.0 * remain)


def per_device(
    hidden_img,
    hidden_txt,
    text_len,
    step_index,
    latent,
    cond,
    mod_weight,
    qkv_weight,
    kv_text_weight,
    q_gain,
    k_gain,
    out_weight,
    final_weight,
):
    row_count, col_count = lax.axis_size("row"), lax.axis_size("col")
    request = lax.axis_index("row") // 2
    requests = cond.shape[0]
    img, width = hidden_img.shape
    txt = hidden_txt.shape[0]
    head = q_gain.shape[0]
    part_cols = qkv_weight.shape[2]
    half = part_cols // 2
    full_width = width * col_count

    wide = -(-width // 128) * 128
    room = -(-txt // 128) * 128
    tokens = img + room
    mod_part = call(
        mod_kernel,
        jax.ShapeDtypeStruct((requests, 8, wide), F32),
        [VMEM, VMEM],
        [],
        cost(2),
    )(cond, jnp.moveaxis(mod_weight, 1, 0))
    mod_own = mod_part[0]
    for k in range(1, requests):
        mod_own = mod_own + swap(mod_part[k], "row", 2 * k)
    stats = call(
        stats_kernel,
        jax.ShapeDtypeStruct((8, tokens), F32),
        [VMEM, VMEM],
        [],
        cost(1),
    )(hidden_img.T, hidden_txt)
    stats = sum((swap(stats, "col", mask) for mask in range(1, col_count)), stats)

    chip_masks = [1 << bit for bit in range(1, row_count.bit_length() - 1)]
    packed = call(
        pack_kernel,
        (jax.ShapeDtypeStruct((qkv_weight.shape[0], 5 * half), BF16),) * 2,
        [VMEM, VMEM],
        [],
        cost(2),
        (VMEM, VMEM),
    )(jnp.moveaxis(qkv_weight, 1, 0), kv_text_weight)
    packed = packed[0], swap(packed[1], "row", 1)
    *packed, mod_own = tie(*packed, mod_own)
    mod_own = mod_own + swap(mod_own, "row", 1)
    ready = call(
        functools.partial(norm_kernel, full_width),
        jax.ShapeDtypeStruct((img + txt, wide), BF16),
        [VMEM] * 4,
        [],
        cost(1),
    )(hidden_img.T, hidden_txt, stats, mod_own)
    routes = line_routes(col_count)
    small = col_count == 4 and row_count == 8
    if small:
        line, peer_line, gathered = gather_both(ready, packed)
    else:
        line = line_gather(ready, "col")
        peer_line = [swap(part, "row", 1) for part in line]
        gathered = [doubling_gather(part, "row", chip_masks) for part in packed]

    if gathered[0][0].shape[0] % 16 == 0:
        masks = sorted(gathered[0])
        blocks = [piece[k] for piece in gathered for k in masks]
    else:
        masks, blocks = [], [in_order(gathered, "row")]
    heads_out = jax.ShapeDtypeStruct((half, img), BF16)
    full_wide = col_count * wide
    projected = call(
        functools.partial(project_kernel, routes, masks, img, head),
        (heads_out, heads_out),
        [SMEM, VMEM, VMEM] + [HBM] * (2 * len(routes) + len(blocks)),
        [
            pltpu.VMEM((2 * (img + txt), full_wide), BF16),
            pltpu.VMEM((full_wide, 5 * half), BF16),
            pltpu.VMEM((2 * img, 3 * half), F32),
            pltpu.VMEM((2 * txt, 2 * half), F32),
            pltpu.VMEM((2 * img, half), BF16),
            *[pltpu.VMEM((2 * (img + txt), half), BF16)] * 2,
            pltpu.SemaphoreType.DMA((2, 2, len(routes))),
            pltpu.SemaphoreType.DMA((2, col_count)),
        ],
        cost(PROJECT),
        (VMEM, VMEM),
        vmem=PROJECT_MIB,
    )(text_len, q_gain[None], k_gain, *line, *peer_line, *blocks)
    head_depth, patch = final_weight.shape
    depth = out_weight.shape[0]
    folds = -(-head_depth // depth)
    tail = jnp.pad(final_weight.T, ((0, 0), (0, folds * depth - head_depth)))
    tail = jnp.swapaxes(tail.reshape(patch, folds, depth), 0, 1).reshape(folds * patch, depth)
    out_packed = jnp.concatenate([out_weight.T, tail], axis=0)
    masks = list(range(0, row_count, 2))
    out_blocks = direct_gather(out_packed, "row", masks)

    keep, give, *others = tie(*projected, *[out_blocks[k] for k in masks[1:]])
    own_rows = jnp.concatenate([out_packed, *others], axis=0)
    other_rows = swap(own_rows, "row", 1)
    take = swap(give, "row", 1)
    if small:
        line, other_rows = gather_heads(keep, take, other_rows)
    else:
        line = line_gather(jnp.concatenate([keep, take], axis=0), "col")
    early, late, far = far_routes(col_count)
    sems = pltpu.SemaphoreType.DMA((2, len(routes)))
    bundle = call(
        functools.partial(early_kernel, [route for _, route in early], far, masks),
        (
            jax.ShapeDtypeStruct((width, img), F32),
            jax.ShapeDtypeStruct((width, part_cols), BF16),
            jax.ShapeDtypeStruct((3 * patch, width), BF16),
            jax.ShapeDtypeStruct((8, img), F32),
        ),
        [VMEM] + [HBM] * (len(early) + 2),
        [
            pltpu.VMEM((col_count, part_cols, img), BF16),
            pltpu.VMEM((row_count,) + out_packed.shape, BF16),
            sems,
            pltpu.SemaphoreType.DMA((2, len(masks))),
        ],
        cost(5),
        (VMEM,) * 4,
        vmem=EARLY,
    )(
        mod_own,
        *[line[k] for k, _ in early],
        own_rows,
        other_rows,
    )
    partial_sum = call(
        functools.partial(late_kernel, [route for _, route in late]),
        jax.ShapeDtypeStruct((patch + 8, img), F32),
        [VMEM] * 6 + [HBM] * len(late),
        [pltpu.VMEM((part_cols, img), BF16), sems],
        cost(3),
        vmem=24,
    )(mod_own, hidden_img.T, *bundle, *[line[k] for k, _ in late])
    mask = 1
    while mask < col_count:
        partial_sum = partial_sum + swap(partial_sum, "col", mask)
        mask *= 2
    average = partial_sum[patch : patch + 1] / full_width
    mean_square = partial_sum[patch + 1 : patch + 2] / full_width
    inverse = lax.rsqrt(mean_square - average * average + EPS_NORM)
    gains = partial_sum[patch + 2, :patch][:, None]
    shifts = partial_sum[patch + 3, :patch][:, None]
    velocity = inverse * (partial_sum[:patch] - average * gains) + shifts
    step_now = lax.dynamic_index_in_dim(step_index, request, 0, keepdims=False)
    sigma_step = sigma_of(step_now + 1) - sigma_of(step_now)
    latent_next = latent.T + sigma_step * velocity
    return (velocity.T, latent_next.T)


def solution(mesh):
    in_specs = (
        P("row", "col"),
        P("row", "col"),
        P(),
        P(),
        P("row", None),
        P(None, "row"),
        P("row", None, "col"),
        P("row", None, "col"),
        P("row", None, "col"),
        P(),
        P(),
        P("row", "col"),
        P("row", None),
    )
    out_specs = (P("row", None), P("row", None))
    return jax.shard_map(
        per_device, mesh=mesh, in_specs=in_specs, out_specs=out_specs, check_vma=False
    )
```
